32 devices in a mesh: dp: 8 (over z, y), row: 2 (over x), col: 2 (over core).
Axes of the slice: x: 2, y: 2, z: 4, core: 2. Of those that a mesh axis runs over, the one named last changes fastest.
Arguments:
- inputs: bfloat16 [12288, 1536], P(('dp', 'col'), 'row'), may hold values from -6 to 6
- segments: int32 [12288], P(('dp', 'row')), may hold values from 0 to 3, as said below
- positions: int32 [12288], P(('dp', 'row')), may hold values from 0 to 2558, as said below
- w_query: bfloat16 [1536, 1536], P('row', 'col'), may hold values from -0.15625 to 0.15625
- w_key: bfloat16 [1536, 256], P('row', 'col'), may hold values from -0.15625 to 0.15625
- w_value: bfloat16 [1536, 256], P('row', 'col'), may hold values from -0.15625 to 0.15625
- b_query: bfloat16 [1536], P('col'), may hold values from -3 to 3
- b_key: bfloat16 [256], P('col'), may hold values from -3 to 3
- b_value: bfloat16 [256], P('col'), may hold values from -3 to 3
- w_out: bfloat16 [1536, 1536], P('col', 'row'), may hold values from -0.625 to 0.625
- gain_one: bfloat16 [1536], P('row'), may hold values from 0.099609375 to 1.8984375
- gain_two: bfloat16 [1536], P('row'), may hold values from 0.099609375 to 1.8984375
- w_gate: bfloat16 [1536, 8960], P('row', 'col'), may hold values from -0.15625 to 0.15625
- w_up: bfloat16 [1536, 8960], P('row', 'col'), may hold values from -0.15625 to 0.15625
- w_down: bfloat16 [8960, 1536], P('col', 'row'), may hold values from -0.0625 to 0.0625
- cotangent: bfloat16 [12288, 1536], P(('dp', 'col'), 'row'), may hold values from -6 to 6
Outputs:
- output: bfloat16 [12288, 1536], P(('dp', 'col'), 'row')
- input_grad: float32 [12288, 1536], P(('dp', 'col'), 'row')
- query_grad: float32 [1536, 1536], P(('row', 'dp'), 'col')
- key_grad: float32 [1536, 256], P(('row', 'dp'), 'col')
- value_grad: float32 [1536, 256], P(('row', 'dp'), 'col')
- query_bias_grad: float32 [1536], P('col')
- key_bias_grad: float32 [256], P('col')
- value_bias_grad: float32 [256], P('col')
- out_grad: float32 [1536, 1536], P('col', ('row', 'dp'))
- gain_one_grad: float32 [1536], P('row')
- gain_two_grad: float32 [1536], P('row')
- gate_grad: float32 [1536, 8960], P(('row', 'dp'), 'col')
- up_grad: float32 [1536, 8960], P(('row', 'dp'), 'col')
- down_grad: float32 [8960, 1536], P('col', ('row', 'dp'))
The draws below stay inside these ranges and needn't reach their ends.
Inputs may be any that keep to these rules, and one draw needn't show every extreme that they name: `segments`: within each aligned block of 768 tokens (the tokens of one device), document numbers start at 0 and never fall; every document lies inside one block and has at most 512 tokens, and each block holds one of exactly 512. Within a document, positions rise by one from token to token; a document's first position is 0 to 2047.
All inputs are finite; a program needn't handle non-finite values.
Results may differ from the reference program's by a relative error of at most 0.023.
Values may be sent and summed in bfloat16 or wider, within the bound.
No kernel may reach another device: no remote copies, remote signals or barrier semaphores. Data moves between devices by JAX's collectives and lax.ppermute only.
A program may use at most 384 MiB of HBM per device.

```python
import jax
import jax.numpy as jnp
from jax import lax

D = 1536
HQ = 12
KVH = 2
HD = 128
FF = 8960
ROWS = 768
DOC = 512
QW = 1536
KW = 256
TOKENS = 12288


def document_layout(key):
    blocks = TOKENS // ROWS
    piece = DOC // 4
    first_key, third_key = jax.random.split(key, 2)
    long_start = jax.random.randint(first_key, (blocks, 1), 0, ROWS - DOC + 1)
    long_start = long_start.at[0, 0].set(min(1, ROWS - DOC))
    indices = jnp.arange(ROWS, dtype=jnp.int32)[None, :]
    before = indices < long_start
    after = indices >= long_start + DOC
    begins = before & (indices % piece == 0) | after & ((indices - long_start - DOC) % piece == 0) | (indices == long_start)
    segment_ids = jnp.cumsum(begins.astype(jnp.int32), axis=1) - 1
    starts = lax.cummax(jnp.where(begins, indices, 0), axis=1)
    offsets = jax.random.randint(third_key, (blocks, ROWS), 0, 2048)
    offsets = offsets.at[0].set(2047)
    offsets = offsets.at[1].set(0)
    placed = indices - starts + jnp.take_along_axis(offsets, starts, axis=1)
    return (segment_ids.reshape(TOKENS).astype(jnp.int32), placed.reshape(TOKENS).astype(jnp.int32))


def draw_segments(key, part):
    return document_layout(key)[0]


def draw_positions(key, part):
    return document_layout(key)[1]


def levels(rng, dims, shards, low, high):
    loudness, own = 1.0, jax.random.fold_in(rng, 6)
    for position, blocks in shards:
        heights = jnp.exp(jax.random.uniform(jax.random.fold_in(own, position), (blocks,), jnp.float32, low / len(shards), high / len(shards)))
        loudness = loudness * jnp.repeat(heights, dims[position] // blocks).reshape([-1 if axis == position else 1 for axis in range(len(dims))])
    return loudness


def centred(own_key, dims, width, bound, pieces=(), kind=jnp.bfloat16):
    values = jax.random.normal(own_key, dims, jnp.float32) * width
    if len(pieces) > 0:
        values = levels(own_key, dims, pieces, -0.22, 0.18) * values
    return jnp.clip(values, min=-bound, max=bound).astype(kind)


def setup_inputs(seed: int = 0) -> dict:
    arg_keys = jax.random.split(jax.random.key(seed), 17)
    return {
        "inputs": centred(arg_keys[0], (TOKENS, D), 1.0, 6.0, ((0, 16), (1, 2))),
        "segments": draw_segments(jax.random.fold_in(arg_keys[16], 71), 0),
        "positions": draw_positions(jax.random.fold_in(arg_keys[16], 71), 0),
        "w_query": centred(arg_keys[3], (D, QW), D ** -0.5, 0.15625, ((0, 2), (1, 2))),
        "w_key": centred(arg_keys[4], (D, KW), D ** -0.5, 0.15625, ((0, 2), (1, 2))),
        "w_value": centred(arg_keys[5], (D, KW), D ** -0.5, 0.15625, ((0, 2), (1, 2))),
        "b_query": centred(arg_keys[6], (QW,), 0.5, 3.0, ((0, 2),)),
        "b_key": centred(arg_keys[7], (KW,), 0.5, 3.0, ((0, 2),)),
        "b_value": centred(arg_keys[8], (KW,), 0.5, 3.0, ((0, 2),)),
        "w_out": centred(arg_keys[9], (QW, D), (QW // 16) ** -0.5, 0.625, ((0, 2), (1, 2))),
        "gain_one": jnp.clip(1.0 + 0.18 * jax.random.normal(arg_keys[10], (D,), jnp.float32), 0.099609375, 1.8984375).astype(jnp.bfloat16),
        "gain_two": jnp.clip(1.0 + 0.18 * jax.random.normal(arg_keys[11], (D,), jnp.float32), 0.099609375, 1.8984375).astype(jnp.bfloat16),
        "w_gate": centred(arg_keys[12], (D, FF), D ** -0.5, 0.15625, ((0, 2), (1, 2))),
        "w_up": centred(arg_keys[13], (D, FF), D ** -0.5, 0.15625, ((0, 2), (1, 2))),
        "w_down": centred(arg_keys[14], (FF, D), FF ** -0.5, 0.0625, ((0, 2), (1, 2))),
        "cotangent": centred(arg_keys[15], (TOKENS, D), 1.0, 6.0, ((0, 16), (1, 2))),
    }


EPS = 1e-06
THETA = 1000000.0
HIGH = lax.Precision.HIGHEST

@jax.custom_vjp
def low(v):
    return lax.optimization_barrier(v.astype(jnp.bfloat16)).astype(jnp.float32)

@jax.custom_vjp
def low_back(v):
    return v

def low_keep(v):
    return (low(v), None)

def low_pass(kept, grad):
    return (grad,)

def back_keep(v):
    return (v, None)

def back_low(kept, grad):
    return (low(grad),)
low.defvjp(low_keep, low_pass)
low_back.defvjp(back_keep, back_low)

def matmul(left, right):
    return jnp.dot(left, right, preferred_element_type=jnp.float32, precision=HIGH)

def normalize(values, gain):
    return values * lax.rsqrt(lax.optimization_barrier(jnp.mean(values * values, axis=-1, keepdims=True)) + EPS) * gain

def angles(positions):
    indices = jnp.arange(HD // 2, dtype=jnp.float32)
    inverse = jnp.exp(indices * (-2.0 / HD) * jnp.log(jnp.float32(THETA)))
    turned = positions.astype(jnp.float32)[:, None] * inverse[None, :]
    return (jnp.cos(turned)[:, None, :], jnp.sin(turned)[:, None, :])

def rotate(values, cosine, sine):
    halfway = HD // 2
    front_half = values[..., :halfway]
    back_half = values[..., halfway:]
    return jnp.concatenate([front_half * cosine - back_half * sine, back_half * cosine + front_half * sine], axis=-1)

def attend_block(item):
    queries, keys_block, values_block, segment_block = item
    length = queries.shape[0]
    grouped = queries.reshape(length, KVH, HQ // KVH, HD)
    scores = jnp.einsum('qkgd,pkd->kgqp', grouped, keys_block, precision=HIGH) * HD ** (-0.5)
    scores = low_back(scores)
    places = jnp.arange(length)
    allowed = (segment_block[:, None] == segment_block[None, :]) & (places[None, :] <= places[:, None])
    scores = jnp.where(allowed, scores, -1e+30)
    weights = low(jax.nn.softmax(scores, axis=-1))
    mixture = jnp.einsum('kgqp,pkd->qkgd', weights, values_block, precision=HIGH)
    return mixture.reshape(length, HQ * HD)

def layer(inputs, w_query, w_key, w_value, b_query, b_key, b_value, w_out, gain_one, gain_two, w_gate, w_up, w_down, cosine, sine, segments):
    normed = low(normalize(inputs, gain_one))
    queries = low_back(matmul(normed, w_query) + b_query).reshape(-1, HQ, HD)
    queries = low(rotate(queries, cosine, sine))
    keys_all = low_back(matmul(normed, w_key) + b_key).reshape(-1, KVH, HD)
    keys_all = low(rotate(keys_all, cosine, sine))
    values_all = low(low_back(matmul(normed, w_value) + b_value)).reshape(-1, KVH, HD)
    blocks = TOKENS // ROWS
    attended = lax.map(jax.checkpoint(attend_block), (queries.reshape(blocks, ROWS, HQ, HD), keys_all.reshape(blocks, ROWS, KVH, HD), values_all.reshape(blocks, ROWS, KVH, HD), segments.reshape(blocks, ROWS)))
    attended = low(low_back(attended.reshape(-1, HQ * HD)))
    branch = low_back(matmul(attended, w_out))
    middle = inputs + branch
    normed_two = low(normalize(middle, gain_two))
    gate = low_back(matmul(normed_two, w_gate))
    upward = low_back(matmul(normed_two, w_up))
    hidden = low(jax.nn.silu(gate) * upward)
    return middle + matmul(hidden, w_down)

def reference(inputs, segments, positions, w_query, w_key, w_value, b_query, b_key, b_value, w_out, gain_one, gain_two, w_gate, w_up, w_down, cotangent):
    cosine, sine = angles(positions)
    floats = [item.astype(jnp.float32) for item in (inputs, w_query, w_key, w_value, b_query, b_key, b_value, w_out, gain_one, gain_two, w_gate, w_up, w_down)]

    def forward(*params):
        return layer(*params, cosine, sine, segments)
    result, pullback = jax.vjp(forward, *floats)
    grads = pullback(cotangent.astype(jnp.float32))
    return (result.astype(jnp.bfloat16), grads[0], grads[1], grads[2], grads[3], grads[4], grads[5], grads[6], grads[7], grads[8], grads[9], grads[10], grads[11], grads[12])
```

```python
import jax
import jax.numpy as jnp
from jax import lax
from jax.sharding import PartitionSpec as P

D = 1536
HQ = 12
KVH = 2
HD = 128
LANES = 128


EPS = 1e-06
THETA = 1000000.0
BF = jnp.bfloat16
F32 = jnp.float32


def swap_row(value):
    return lax.ppermute(value, "row", [(0, 1), (1, 0)])


def swap_col(value):
    return lax.ppermute(value, "col", [(0, 1), (1, 0)])


def swap_pair(value):
    size = lax.axis_size("dp")
    return lax.ppermute(value, "dp", [(i, i ^ 1) for i in range(size)])


def shift_outer(value, step):
    size = lax.axis_size("dp")
    return lax.ppermute(value, "dp", [(i, (i + 2 * step) % size) for i in range(size)])


def turn_square(value):
    return lax.ppermute(value, ("row", "col"), [(0, 0), (1, 2), (2, 1), (3, 3)])


def product(left, right):
    return jnp.dot(left, right, preferred_element_type=F32)


def product_left(left, right):
    return lax.dot_general(
        left, right, (((0,), (0,)), ((), ())), preferred_element_type=F32
    )


def product_right(left, right):
    return lax.dot_general(
        left, right, (((1,), (1,)), ((), ())), preferred_element_type=F32
    )


def angles(positions):
    indices = jnp.arange(HD // 2, dtype=F32)
    inverse = jnp.exp(indices * (-2.0 / HD) * jnp.log(F32(THETA)))
    turned = positions.astype(F32)[:, None] * inverse[None, :]
    return (jnp.cos(turned)[:, None, :], jnp.sin(turned)[:, None, :])


def rotate(values, cosine, sine):
    halfway = HD // 2
    front_half = values[..., :halfway]
    back_half = values[..., halfway:]
    return jnp.concatenate(
        [front_half * cosine - back_half * sine, back_half * cosine + front_half * sine], axis=-1
    )


def masked_scores(grouped, keys_local, segments):
    length = grouped.shape[0]
    scores = jnp.einsum(
        "qkgd,pkd->kgqp", grouped, keys_local, preferred_element_type=F32
    ) * HD ** (-0.5)
    places = jnp.arange(length)
    allowed = (segments[:, None] == segments[None, :]) & (places[None, :] <= places[:, None])
    return jnp.where(allowed, scores, -1e30)


def pick(array, index, axis=0):
    return lax.dynamic_index_in_dim(array, index, axis, keepdims=False)


def fetch_block(block, inner):
    halves = block.reshape((2, block.shape[0] // 2) + block.shape[1:])
    direct = swap_row(pick(halves, inner))
    other = swap_pair(direct)
    low = jnp.where(inner == 0, direct, other)
    high = jnp.where(inner == 0, other, direct)
    return jnp.concatenate([low, high], axis=0)


def sum_groups(block, inner, outer_index):
    parts, rows, columns = block.shape
    outer = lax.axis_size("dp") // 2
    piece = rows // (2 * outer)
    cut = block.reshape(parts, outer, 2, piece, columns)
    half = pick(cut, inner, 2).astype(F32) + swap_pair(pick(cut, 1 - inner, 2)).astype(F32)
    half = half.astype(BF)
    total = pick(half, outer_index, 1).astype(F32)
    for step in range(1, outer):
        sent = pick(half, (outer_index + step) % outer, 1)
        total = total + shift_outer(sent, step).astype(F32)
    return total


def body(
    inputs,
    segments,
    positions,
    w_query,
    w_key,
    w_value,
    b_query,
    b_key,
    b_value,
    w_out,
    gain_one,
    gain_two,
    w_gate,
    w_up,
    w_down,
    cotangent,
):
    length = inputs.shape[0]
    width = inputs.shape[1]
    heads_here = w_query.shape[1] // HD
    pairs_here = w_key.shape[1] // HD
    group_size = HQ // KVH
    query_width = w_query.shape[1]
    key_width = w_key.shape[1]
    row = lax.axis_index("row")
    col = lax.axis_index("col")
    group = lax.axis_index("dp")
    inner = group % 2
    outer_index = group // 2
    same = row == col

    def by_row(mine, other):
        return jnp.where(same, mine, other), jnp.where(same, other, mine)

    mine = turn_square(inputs)
    other = swap_col(mine)
    weights_attention = jnp.concatenate([w_query, w_key, w_value], axis=1)
    fetched_attention = fetch_block(weights_attention, inner)
    gains = jnp.stack([gain_one, gain_two])
    fetched_gains = swap_row(gains)
    gains_mine, _ = by_row(gains, fetched_gains)
    gains_mine = gains_mine.astype(F32)
    gains_all = jnp.concatenate([gains, fetched_gains], axis=1).astype(F32)

    hidden_here = w_gate.shape[1]
    blocks = hidden_here // LANES
    quarter = (blocks + 1) // 2 * LANES
    overlap = 2 * quarter - hidden_here
    start_mine = row * (hidden_here - quarter)
    start_other = (1 - row) * (hidden_here - quarter)
    own_gate = lax.dynamic_slice_in_dim(w_gate, start_mine, quarter, 1)
    own_up = lax.dynamic_slice_in_dim(w_up, start_mine, quarter, 1)
    own_down = lax.dynamic_slice_in_dim(w_down, start_mine, quarter, 0)
    fetched_gate = fetch_block(lax.dynamic_slice_in_dim(w_gate, start_other, quarter, 1), inner)
    fetched_up = fetch_block(lax.dynamic_slice_in_dim(w_up, start_other, quarter, 1), inner)
    fetched_out = fetch_block(w_out, inner)
    fetched_down = fetch_block(lax.dynamic_slice_in_dim(w_down, start_other, quarter, 0), inner)
    full_gate = jnp.concatenate([own_gate, fetched_gate], axis=0)
    full_up = jnp.concatenate([own_up, fetched_up], axis=0)
    full_down = jnp.concatenate([own_down, fetched_down], axis=1)
    counted = (jnp.arange(quarter) >= row * overlap)[None, :]

    cot_own = by_row(cotangent, swap_col(cotangent))
    cot_far = swap_row(cotangent)
    cot_far = by_row(cot_far, swap_col(cot_far))
    full_cot = jnp.concatenate(
        [jnp.concatenate([cot_own[0], cot_far[0]], axis=1),
         jnp.concatenate([cot_own[1], cot_far[1]], axis=1)], axis=0
    )
    cot_mine = jnp.where(same, cot_own[0], cot_far[0]).astype(F32)

    cosine, sine = angles(positions)
    residual = mine.astype(F32)
    both = jnp.concatenate(by_row(mine, other), axis=1).astype(F32)
    rstd_one = lax.rsqrt(jnp.mean(both * both, axis=1, keepdims=True) + EPS)
    full_one = (both * rstd_one * gains_all[0]).astype(BF)
    normed_one = residual * rstd_one
    full_attention = jnp.concatenate([weights_attention, fetched_attention], axis=0)
    projected = product(full_one, full_attention)
    bias = jnp.concatenate([b_query, b_key, b_value]).astype(F32)
    projected = projected + bias
    queries = rotate(
        projected[:, :query_width].reshape(length, heads_here, HD), cosine, sine
    ).astype(BF)
    keys_local = rotate(
        projected[:, query_width : query_width + key_width].reshape(length, pairs_here, HD),
        cosine,
        sine,
    ).astype(BF)
    values_local = (
        projected[:, query_width + key_width :].astype(BF).reshape(length, pairs_here, HD)
    )
    grouped = queries.reshape(length, pairs_here, group_size, HD)
    scores = masked_scores(grouped, keys_local, segments)
    row_max = jnp.max(scores, axis=-1, keepdims=True)
    row_sum = jnp.sum(jnp.exp(scores - row_max), axis=-1, keepdims=True)
    log_total = row_max + jnp.log(row_sum)
    weights = jnp.exp(scores - log_total).astype(BF)
    attended = jnp.einsum("kgqp,pkd->qkgd", weights, values_local, preferred_element_type=F32)
    attended = attended.reshape(length, query_width).astype(BF)
    out_keep, out_send = by_row(w_out, fetched_out)
    branch = product(attended, out_keep) + swap_col(
        product(attended, out_send).astype(BF)
    ).astype(F32)
    middle = residual + branch
    squares = jnp.sum(middle * middle, axis=1)
    rstd_two = lax.rsqrt((squares + swap_col(squares)) / D + EPS)[:, None]
    normed_two = middle * rstd_two
    low_two = (normed_two * gains_mine[1]).astype(BF)
    near = jnp.concatenate(by_row(low_two, swap_col(low_two)), axis=1)
    far_two = swap_row(low_two)
    far = jnp.concatenate(by_row(far_two, swap_col(far_two)), axis=1)
    full_two = jnp.concatenate([near, far], axis=0)

    gate = product(full_two, full_gate)
    upward = product(full_two, full_up)
    sigma = jax.nn.sigmoid(gate)
    hidden = jnp.where(counted, gate * sigma * upward, 0.0).astype(BF)
    hidden_grad = jnp.where(counted, product_right(full_cot, full_down), 0.0)
    gate_low = (hidden_grad * upward * sigma * (1.0 + gate * (1.0 - sigma))).astype(BF)
    up_low = (hidden_grad * gate * sigma).astype(BF)

    def gather_sum(partial):
        keep, send = by_row(partial[:, :width].astype(BF), partial[:, width:].astype(BF))
        half = keep.astype(F32) + swap_col(send).astype(F32)
        return half[:length] + swap_row(half[length:].astype(BF)).astype(F32)

    grad_down = product_left(full_cot, hidden).astype(BF).reshape(2, width, quarter)
    sum_down = sum_groups(grad_down, inner, outer_index)
    grad_gate = product_left(full_two, gate_low).astype(BF).reshape(2, width, quarter)
    sum_gate = sum_groups(grad_gate, inner, outer_index)
    grad_up = product_left(full_two, up_low).astype(BF).reshape(2, width, quarter)
    sum_up = sum_groups(grad_up, inner, outer_index)

    normed_grad_two = gather_sum(
        product_right(gate_low, full_gate) + product_right(up_low, full_up)
    )
    output = turn_square(
        (middle + gather_sum(product(hidden, full_down))).astype(BF)
    )
    scaled_two = normed_grad_two * gains_mine[1]
    gain_two_part = jnp.sum(normed_grad_two * normed_two, axis=0)
    dots = jnp.sum(scaled_two * normed_two, axis=1)
    mean_two = (dots + swap_col(dots)) / D
    middle_grad = cot_mine + rstd_two * (scaled_two - normed_two * mean_two[:, None])
    low_mid = middle_grad.astype(BF)
    full_mid = jnp.concatenate(by_row(low_mid, swap_col(low_mid)), axis=1)
    full_out = jnp.concatenate([w_out, fetched_out], axis=1)
    att_grad = product_right(full_mid, full_out).astype(BF)
    grad_out = product_left(full_mid, attended)

    att_grouped = att_grad.reshape(length, pairs_here, group_size, HD)
    scores = masked_scores(grouped, keys_local, segments)
    probs = jnp.exp(scores - log_total)
    weights = probs.astype(BF)
    prob_grad = jnp.einsum(
        "qkgd,pkd->kgqp", att_grouped, values_local, preferred_element_type=F32
    )
    delta = jnp.sum(probs * prob_grad, axis=-1, keepdims=True)
    score_grad = (probs * (prob_grad - delta)).astype(BF)
    query_turned = jnp.einsum(
        "kgqp,pkd->qkgd", score_grad, keys_local, preferred_element_type=F32
    ) * HD ** (-0.5)
    key_turned = jnp.einsum(
        "kgqp,qkgd->pkd", score_grad, grouped, preferred_element_type=F32
    ) * HD ** (-0.5)
    value_back = jnp.einsum(
        "kgqp,qkgd->pkd", weights, att_grouped, preferred_element_type=F32
    )
    query_low = (
        rotate(query_turned.reshape(length, heads_here, HD), cosine, -sine)
        .reshape(length, query_width)
        .astype(BF)
    )
    key_low = rotate(key_turned, cosine, -sine).reshape(length, key_width).astype(BF)
    value_low = value_back.reshape(length, key_width).astype(BF)
    back_low = jnp.concatenate([query_low, key_low, value_low], axis=1)
    bias_part = jnp.sum(back_low.astype(F32), axis=0)

    input_part = product_right(back_low, full_attention)
    keep, send = by_row(input_part[:, :width], input_part[:, width:])
    normed_grad_one = keep + swap_col(send.astype(BF)).astype(F32)
    scaled_one = normed_grad_one * gains_mine[0]
    gain_one_part = jnp.sum(normed_grad_one * normed_one, axis=0)
    dots = jnp.sum(scaled_one * normed_one, axis=1)
    mean_one = (dots + swap_col(dots)) / D
    input_grad = middle_grad + rstd_one * (scaled_one - normed_one * mean_one[:, None])
    input_grad = turn_square(input_grad.astype(BF)).astype(F32)

    grad_attention = product_left(full_one, back_low)
    grads = jnp.concatenate([grad_attention, grad_out], axis=1)
    grads = grads[:width] + swap_row(grads[width:].astype(BF)).astype(F32)
    sum_attention = sum_groups(grads.astype(BF)[None], inner, outer_index)[0]

    small = lax.psum(
        jnp.concatenate([bias_part, gain_one_part, gain_two_part]), ("dp", "row")
    )
    total_width = query_width + 2 * key_width
    gain_sums = small[total_width:].reshape(2, width)
    gain_sums, _ = by_row(gain_sums, swap_col(gain_sums))

    def joined(total):
        near = total[0]
        far = swap_row(total[1].astype(BF)).astype(F32)
        low = jnp.where(row == 0, near, far)
        high = jnp.where(row == 0, far, near)
        return jnp.concatenate([low, high[:, overlap:]], axis=1)

    return (
        output,
        input_grad,
        sum_attention[:, :query_width],
        sum_attention[:, query_width : query_width + key_width],
        sum_attention[:, query_width + key_width : total_width],
        small[:query_width],
        small[query_width : query_width + key_width],
        small[query_width + key_width : total_width],
        sum_attention[:, total_width:].T,
        gain_sums[0],
        gain_sums[1],
        joined(sum_gate),
        joined(sum_up),
        joined(sum_down).T,
    )


def solution(mesh):
    return jax.shard_map(
        body,
        mesh=mesh,
        in_specs=(
            P(("dp", "col"), "row"),
            P(("dp", "row")),
            P(("dp", "row")),
            P("row", "col"),
            P("row", "col"),
            P("row", "col"),
            P("col"),
            P("col"),
            P("col"),
            P("col", "row"),
            P("row"),
            P("row"),
            P("row", "col"),
            P("row", "col"),
            P("col", "row"),
            P(("dp", "col"), "row"),
        ),
        out_specs=(
            P(("dp", "col"), "row"),
            P(("dp", "col"), "row"),
            P(("row", "dp"), "col"),
            P(("row", "dp"), "col"),
            P(("row", "dp"), "col"),
            P("col"),
            P("col"),
            P("col"),
            P("col", ("row", "dp")),
            P("row"),
            P("row"),
            P(("row", "dp"), "col"),
            P(("row", "dp"), "col"),
            P("col", ("row", "dp")),
        ),
        check_vma=False,
    )
```

```python
import functools

import jax
import jax.numpy as jnp
from jax import lax
from jax.experimental import pallas as pl
from jax.experimental.pallas import tpu as pltpu
from jax.sharding import PartitionSpec as P

D = 1536
HQ = 12
KVH = 2
HD = 128
LANES = 128
PARTS = 4
TILE = 256
WIDE_TILE = 384
MIB = 1024 * 1024
SCALE = 10.0

EPS = 1e-06
THETA = 1000000.0
BF = jnp.bfloat16
F32 = jnp.float32

SAME, INNER, START, START_FAR, SKIP, OWN, PAIR, NEAR, ACROSS, ROW = range(10)


def swap_row(value):
    return lax.ppermute(value, "row", [(0, 1), (1, 0)])


def swap_col(value):
    return lax.ppermute(value, "col", [(0, 1), (1, 0)])


def swap_bit(value, bit):
    size = lax.axis_size("dp")
    return lax.ppermute(value, "dp", [(i, i ^ (1 << bit)) for i in range(size)])


def trade_col(value):
    return lax.all_to_all(value, "col", 0, 0)


def turn_square(value):
    return lax.ppermute(value, ("row", "col"), [(0, 0), (1, 2), (2, 1), (3, 3)])


def pick(array, index, axis=0):
    return lax.dynamic_index_in_dim(array, index, axis, keepdims=False)


ANY = pl.BlockSpec(memory_space=pl.ANY)
SCALARS = pl.BlockSpec(memory_space=pltpu.SMEM)
WHOLE = pl.BlockSpec(memory_space=pltpu.VMEM)


def shape(dims, dtype):
    return jax.ShapeDtypeStruct(dims, dtype)


def cost(flops, moved=0, exps=0):
    return pl.CostEstimate(
        flops=int(flops * SCALE), bytes_accessed=int(moved * SCALE), transcendentals=int(exps * SCALE)
    )


def run(kernel, ins, outs, after=(), grid=None, out_specs=None, scratch=(), limit=56, aliases=None,
        estimate=None, name=None):
    given = len(ins)
    count = len(outs)

    def body(*refs):
        kernel(*refs[:given], *refs[given + len(after):])

    return pl.pallas_call(
        body,
        grid=grid if grid is not None else (),
        in_specs=[spec for _, spec in ins] + [ANY] * len(after),
        out_specs=out_specs if out_specs is not None else [WHOLE] * count,
        out_shape=outs,
        scratch_shapes=list(scratch),
        input_output_aliases=aliases or {},
        cost_estimate=estimate,
        name=name,
        compiler_params=pltpu.CompilerParams(vmem_limit_bytes=limit * MIB),
    )(*[array for array, _ in ins], *after)


def dot(left, right):
    return jnp.dot(left, right, preferred_element_type=F32)


def dot_right(left, right):
    return lax.dot_general(left, right, (((1,), (1,)), ((), ())), preferred_element_type=F32)


def dot_left(left, right):
    return lax.dot_general(left, right, (((0,), (0,)), ((), ())), preferred_element_type=F32)


def copies(pairs, sems):
    started = [pltpu.make_async_copy(src, dst, sems.at[i]) for i, (src, dst) in enumerate(pairs)]
    for one in started:
        one.start()
    for one in started:
        one.wait()


def rows_at(start, size):
    return pl.ds(pl.multiple_of(start, 16), size)


def lanes_at(start, size):
    return pl.ds(pl.multiple_of(start, LANES), size)


def pack_weights(scalars, arrays, part, dims, place, after=(), down=False, scale=1, chunk=0):
    def kernel(s, *refs):
        srcs, out, sems = refs[: len(arrays)], refs[len(arrays)], refs[len(arrays) + 1]
        start = (s[place] * scale + chunk) * dims[0]
        pairs = []
        at = 0
        for src in srcs:
            if down:
                pairs.append((src.at[rows_at(s[START_FAR] + start, dims[0]), :], out))
            elif part is not None:
                pairs.append((src.at[rows_at(start, dims[0]), lanes_at(s[START_FAR], part)],
                              out.at[:, at:at + part]))
                at += part
            else:
                wide = src.shape[1]
                pairs.append((src.at[rows_at(start, dims[0]), :], out.at[:, at:at + wide]))
                at += wide
        copies(pairs, sems)

    return run(kernel, [(scalars, SCALARS)] + [(a, ANY) for a in arrays], [shape(dims, BF)],
               after=after, scratch=[pltpu.SemaphoreType.DMA((len(arrays),))], limit=48,
               estimate=cost(0, 4 * dims[0] * dims[1]), name="pack")[0]


QUARTERS = 5
HALVES = 2
CHUNKED = 4


def placed(s, fetched, at, total):
    if len(fetched) in (HALVES, CHUNKED):
        chunks = len(fetched) // 2
        size = total // 2
        step = size // chunks
        rows = [rows_at(at + half * size + i * step, step)
                for i in range(chunks) for half in (s[INNER], 1 - s[INNER])]
    else:
        size = total // 4
        rows = [rows_at(at + s[place] * size, size) for place in (OWN, PAIR, NEAR)]
        rows += [rows_at(at + s[ACROSS] * size + i * (size // 2), size // 2) for i in range(2)]
    return list(zip(fetched, rows))


def project(scalars, mine, other, gain, gain_far, w_query, w_key, w_value, fetched, bias, cosine,
            sine, after=()):
    length, width = mine.shape
    qw, kw = w_query.shape[1], w_key.shape[1]
    total = qw + 2 * kw

    def kernel(s, mine, other, gain, gain_far, wq, wk, wv, *refs):
        fetched, (bias, cosine, sine, q, k, v, a, r, w) = refs[:QUARTERS], refs[QUARTERS:]
        x = mine[...].astype(F32)
        y = other[...].astype(F32)
        squares = jnp.sum(x * x, axis=1, keepdims=True) + jnp.sum(y * y, axis=1, keepdims=True)
        rstd = lax.rsqrt(squares / D + EPS)
        r[...] = rstd

        @pl.when(s[SAME] == 1)
        def _():
            a[:, :width] = (x * rstd * gain[...]).astype(BF)
            a[:, width:] = (y * rstd * gain_far[...]).astype(BF)

        @pl.when(s[SAME] == 0)
        def _():
            a[:, :width] = (y * rstd * gain[...]).astype(BF)
            a[:, width:] = (x * rstd * gain_far[...]).astype(BF)

        w[:width, :qw] = wq[...]
        w[:width, qw:qw + kw] = wk[...]
        w[:width, qw + kw:] = wv[...]
        for piece, rows in placed(s, fetched, width, width):
            w[rows, :] = piece[...]
        out = dot(a[...], w[...]) + bias[...]
        c, t = cosine[...], sine[...]
        for head in range(qw // HD):
            u = out[:, head * HD:(head + 1) * HD]
            q[:, head * HD:(head + 1) * HD] = (u * c + pltpu.roll(u, HD // 2, 1) * t).astype(BF)
        for head in range(kw // HD):
            u = out[:, qw + head * HD:qw + (head + 1) * HD]
            k[:, head * HD:(head + 1) * HD] = (u * c + pltpu.roll(u, HD // 2, 1) * t).astype(BF)
        v[...] = out[:, qw + kw:].astype(BF)

    arrays = [mine, other, gain, gain_far, w_query, w_key, w_value, *fetched, bias, cosine, sine]
    return run(kernel, [(scalars, SCALARS)] + [(a, WHOLE) for a in arrays],
               [shape((length, qw), BF), shape((length, kw), BF), shape((length, kw), BF),
                shape((length, 2 * width), BF), shape((length, 1), F32)], after=after,
               scratch=[pltpu.VMEM((2 * width, total), BF)],
               estimate=cost(2 * length * 2 * width * total, 12 * MIB), name="qkv")


def allowed_keys(seg_col, seg_row, start, size, keys):
    rows = lax.broadcasted_iota(jnp.int32, (size, keys), 0) + start
    cols = lax.broadcasted_iota(jnp.int32, (size, keys), 1)
    return (seg_col[start:start + size, :] == seg_row[:, :keys]) & (cols <= rows)


def attend(scalars, q, k, v, seg_col, seg_row, w_out, fetched, after=()):
    length, qw = q.shape
    heads, pairs = qw // HD, k.shape[1] // HD
    width = w_out.shape[1]

    def kernel(s, q, k, v, seg_col, seg_row, w_out, *refs):
        fetched, (o, lse, part, w) = refs[:QUARTERS], refs[QUARTERS:]
        for start in range(0, length, TILE):
            keys = start + TILE
            allowed = allowed_keys(seg_col, seg_row, start, TILE, keys)
            rows = slice(start, start + TILE)
            for head in range(heads):
                pair = head // (heads // pairs)
                place = slice(head * HD, (head + 1) * HD)
                mine = slice(pair * HD, (pair + 1) * HD)
                scores = dot_right(q[rows, place], k[:keys, mine]) * HD ** (-0.5)
                scores = jnp.where(allowed, scores, -1e30)
                top = jnp.max(scores, axis=1, keepdims=True)
                raised = jnp.exp(scores - top)
                total = jnp.sum(raised, axis=1, keepdims=True)
                weights = (raised * (1.0 / total)).astype(BF)
                o[rows, place] = dot(weights, v[:keys, mine]).astype(BF)
                lse[rows, head:head + 1] = top + jnp.log(total)
        w[:, :width] = w_out[...]
        for piece, rows in placed(s, fetched, 0, qw):
            w[rows, width:] = piece[...]
        value = dot(o[...], w[...]).astype(BF)
        part[0] = value
        part[1] = value

    arrays = [q, k, v, seg_col, seg_row, w_out, *fetched]
    return run(kernel, [(scalars, SCALARS)] + [(a, WHOLE) for a in arrays],
               [shape((length, qw), BF), shape((length, LANES), F32), shape((2, length, 2 * width), BF)],
               after=after,
               scratch=[pltpu.VMEM((qw, 2 * width), BF)],
               estimate=cost(4 * length * length * qw + 2 * length * qw * 2 * width, 12 * MIB,
                             heads * length * length), name="attention")


def tiled(array, tile):
    return array, pl.BlockSpec((tile, array.shape[1]), lambda i: (i, 0))


def both_tiled(array, tile):
    return array, pl.BlockSpec((2, tile, array.shape[2]), lambda i: (0, i, 0))


def fixed(array):
    return array, pl.BlockSpec(array.shape, lambda i: (0, 0))


def norm_two(scalars, mine, other, parts, gain, gain_far, after=()):
    length, width = mine.shape

    def kernel(s, mine, other, parts, gain, gain_far, h, near, far, r):
        added = parts[0].astype(F32) + parts[1].astype(F32)

        def fill(first, second):
            h[:, :width] = first[...].astype(F32) + added[:, :width]
            h[:, width:] = second[...].astype(F32) + added[:, width:]

        pl.when(s[SAME] == 1)(lambda: fill(mine, other))
        pl.when(s[SAME] == 0)(lambda: fill(other, mine))
        rstd = lax.rsqrt(jnp.sum(h[...] * h[...], axis=1, keepdims=True) / D + EPS)
        r[...] = rstd
        first = (h[:, :width] * rstd * gain[...]).astype(BF)
        second = (h[:, width:] * rstd * gain_far[...]).astype(BF)

        @pl.when(s[SAME] == 1)
        def _():
            near[...] = first
            far[...] = second

        @pl.when(s[SAME] == 0)
        def _():
            near[...] = second
            far[...] = first

    tile = TILE // 2
    outs = [shape((length, 2 * width), F32), shape((length, width), BF), shape((length, width), BF),
            shape((length, 1), F32)]
    return run(kernel, [(scalars, SCALARS)] + [tiled(mine, tile), tiled(other, tile), both_tiled(parts, tile)]
               + [fixed(gain), fixed(gain_far)], outs, after=after, grid=(length // tile,),
               out_specs=[tiled(o, tile)[1] for o in outs],
               estimate=cost(length * width * 20, 16 * MIB), name="norm_two")


def gate_up(scalars, pieces, w_gate, w_up, fetched, first, total, part, kept=None, after=()):
    width = pieces[0][0].shape[1]
    counts = [near.shape[0] // WIDE_TILE for near, _ in pieces]
    steps = sum(counts)
    offset = first // WIDE_TILE
    starts = [sum(counts[:i]) for i in range(len(counts))]

    def kernel(s, *refs):
        halves = refs[:2 * len(pieces)]
        wg, wu, *fetched = refs[2 * len(pieces):2 * len(pieces) + 2 + CHUNKED]
        b, z, up_slope, gate_slope, w, sems = refs[-6:]
        step = pl.program_id(0)

        @pl.when(step == 0)
        def _():
            load_gate_up(s, wg, wu, fetched, w, sems, part, width)

        def fill(near, far):
            @pl.when(s[SAME] == 1)
            def _():
                b[:, :width] = near[...]
                b[:, width:] = far[...]

            @pl.when(s[SAME] == 0)
            def _():
                b[:, :width] = far[...]
                b[:, width:] = near[...]

        for i in range(len(pieces)):
            pl.when((step >= starts[i]) & (step < starts[i] + counts[i]))(
                functools.partial(fill, halves[2 * i], halves[2 * i + 1])
            )

        both = dot(b[...], w[...])
        gate, upward = both[:, :part], both[:, part:]
        counted = lax.broadcasted_iota(jnp.int32, gate.shape, 1) >= s[SKIP]
        sigma = 1.0 / (1.0 + jnp.exp(-gate))
        sigma = jnp.where(counted, sigma, 0.0)
        silu = gate * sigma
        z[...] = (silu * upward).astype(BF)
        up_slope[...] = silu.astype(BF)
        gate_slope[...] = (upward * sigma * (1.0 + gate * (1.0 - sigma))).astype(BF)

    def block(start, count):
        return pl.BlockSpec((WIDE_TILE, width), lambda i: (jnp.clip(i - start, 0, count - 1), 0))

    ins = [(scalars, SCALARS)]
    for pair, start, count in zip(pieces, starts, counts):
        ins += [(array, block(start, count)) for array in pair]
    ins += [(array, ANY) for array in (w_gate, w_up, *fetched)]
    aliases = {}
    if kept is not None:
        aliases = {len(ins) + i: i for i in range(4)}
        ins += [(array, ANY) for array in kept]
    at = lambda i: (i + offset, 0)
    length = steps * WIDE_TILE
    return run(kernel, ins,
               [shape((total, 2 * width), BF)] + [shape((total, part), BF)] * 3,
               after=after, grid=(steps,),
               out_specs=[pl.BlockSpec((WIDE_TILE, 2 * width), at)]
               + [pl.BlockSpec((WIDE_TILE, part), at)] * 3,
               scratch=[pltpu.VMEM((2 * width, 2 * part), BF), pltpu.SemaphoreType.DMA((2 + CHUNKED,))],
               aliases=aliases,
               estimate=cost(8 * length * width * part, 12 * MIB + length * 12000, length * part),
               name="gate_up")


def load_gate_up(s, wg, wu, fetched, w, sems, part, width):
    lanes = lanes_at(s[START], part)
    copies([(wg.at[:, lanes], w.at[:width, :part]), (wu.at[:, lanes], w.at[:width, part:])]
           + [(piece, w.at[rows, :]) for piece, rows in placed(s, fetched, width, width)], sems)


def place_rows(scalars, pieces, after=()):
    length, width = pieces[0][0][0].shape
    flat = [array for group in pieces for pair in group for array in pair]

    def kernel(s, *refs):
        srcs, out, sems = refs[:len(flat)], refs[len(flat)], refs[len(flat) + 1]
        pairs = []
        for i, src in enumerate(srcs):
            group, side, token = i // 4, (i // 2) % 2, i % 2
            place = jnp.where(s[SAME] == 1, token, 1 - token) * length
            pairs.append((src, out.at[rows_at(2 * group * length + place, length),
                                      side * width:(side + 1) * width]))
        copies(pairs, sems)

    return run(kernel, [(scalars, SCALARS)] + [(a, ANY) for a in flat],
               [shape((2 * len(pieces) * length, 2 * width), BF)], after=after,
               scratch=[pltpu.SemaphoreType.DMA((len(flat),))], limit=48,
               estimate=cost(0, 16 * len(flat) * length * width // 4), name="place_rows")[0]


def copy_of(array, after):
    def kernel(src, out, sem):
        copies([(src, out)], sem)

    return run(kernel, [(array, ANY)], [shape(array.shape, array.dtype)], after=after,
               scratch=[pltpu.SemaphoreType.DMA((1,))], limit=48,
               estimate=cost(0, 4 * array.size), name="copy_of")[0]


def hold(array, *after):
    if not after:
        return array

    def kernel(src, out):
        pass

    return run(kernel, [(array, ANY)], [shape(array.shape, array.dtype)], after=after, out_specs=[ANY],
               aliases={0: 0}, limit=48, estimate=cost(0, 0), name="hold")[0]


def load_down(s, w_down, fetched, w, sems, part, width):
    copies([(w_down.at[rows_at(s[START], part), :], w.at[:, :width])]
           + [(piece, w.at[rows, width:]) for piece, rows in placed(s, fetched, 0, part)], sems)


def hidden_back(scalars, cot, up_slope, gate_slope, w_down, fetched, after=()):
    total, width = cot.shape[0], cot.shape[1] // 2
    part = up_slope.shape[1]

    def kernel(s, g, up_slope, gate_slope, w_down, *refs):
        fetched, (out, w, sems) = refs[:HALVES], refs[HALVES:]

        @pl.when(pl.program_id(0) == 0)
        def _():
            load_down(s, w_down, fetched, w, sems, part, width)

        back = dot_right(g[...], w[...])
        out[:, :part] = (back * gate_slope[...].astype(F32)).astype(BF)
        out[:, part:] = (back * up_slope[...].astype(F32)).astype(BF)

    at = lambda i: (i, 0)
    tile = 2 * TILE
    return run(kernel,
               [(scalars, SCALARS), (cot, pl.BlockSpec((tile, 2 * width), at)),
                (up_slope, pl.BlockSpec((tile, part), at)), (gate_slope, pl.BlockSpec((tile, part), at)),
                (w_down, ANY)] + [(piece, ANY) for piece in fetched],
               [shape((total, 2 * part), BF)], after=after, grid=(total // tile,),
               out_specs=[pl.BlockSpec((tile, 2 * part), at)],
               scratch=[pltpu.VMEM((part, 2 * width), BF), pltpu.SemaphoreType.DMA((1 + HALVES,))],
               estimate=cost(4 * total * width * part, total * 14000), name="hidden_back")[0]


def split_store(s, value, keep, send, width):
    first, second = value[:, :width].astype(BF), value[:, width:].astype(BF)

    @pl.when(s[SAME] == 1)
    def _():
        keep[...] = first
        send[...] = second

    @pl.when(s[SAME] == 0)
    def _():
        keep[...] = second
        send[...] = first


def norm_back(scalars, low, w_gate, w_up, fetched, first, length, after=(), stacked=False):
    width = w_gate.shape[0]
    part = low.shape[1] // 2
    offset = first // WIDE_TILE

    def kernel(s, low, wg, wu, *refs):
        fetched, (*outs, w, sems) = refs[:CHUNKED], refs[CHUNKED:]

        @pl.when(pl.program_id(0) == 0)
        def _():
            load_gate_up(s, wg, wu, fetched, w, sems, part, width)

        value = dot_right(low[...], w[...])
        if stacked:
            outs[0][s[ROW]] = value[:, :width].astype(BF)
            outs[0][1 - s[ROW]] = value[:, width:].astype(BF)
        else:
            split_store(s, value, *outs, width)

    tiles = [pl.BlockSpec((WIDE_TILE, width), lambda i: (i, 0))] * 2
    outs = [shape((length, width), BF)] * 2
    if stacked:
        outs = [shape((2, length, width), BF)]
        tiles = [pl.BlockSpec((2, WIDE_TILE, width), lambda i: (0, i, 0))]
    return run(kernel,
               [(scalars, SCALARS), (low, pl.BlockSpec((WIDE_TILE, 2 * part), lambda i: (i + offset, 0))),
                (w_gate, ANY), (w_up, ANY)] + [(piece, ANY) for piece in fetched],
               outs, after=after, grid=(length // WIDE_TILE,), out_specs=tiles,
               scratch=[pltpu.VMEM((2 * width, 2 * part), BF), pltpu.SemaphoreType.DMA((2 + CHUNKED,))],
               estimate=cost(8 * length * width * part, 8 * MIB + length * 8000), name="norm_back")


def down_project(scalars, hidden, w_down, fetched, after=()):
    total, part = hidden.shape
    width = w_down.shape[1]

    def kernel(s, z, w_down, *refs):
        fetched, (keep, send, w, sems) = refs[:HALVES], refs[HALVES:]

        @pl.when(pl.program_id(0) == 0)
        def _():
            load_down(s, w_down, fetched, w, sems, part, width)

        split_store(s, dot(z[...], w[...]), keep, send, width)

    at = lambda i: (i, 0)
    tile = 2 * TILE
    return run(kernel,
               [(scalars, SCALARS), (hidden, pl.BlockSpec((tile, part), at)), (w_down, ANY)]
               + [(piece, ANY) for piece in fetched],
               [shape((total, width), BF)] * 2, after=after, grid=(total // tile,),
               out_specs=[pl.BlockSpec((tile, width), at)] * 2,
               scratch=[pltpu.VMEM((part, 2 * width), BF), pltpu.SemaphoreType.DMA((1 + HALVES,))],
               estimate=cost(4 * total * width * part, total * 8000), name="down_project")


def weight_grad(scalars, left, right, piece, columns, place=0, after=()):
    tokens, width = left.shape[0], left.shape[1] // 2
    groups = width // (2 * piece)

    def kernel(s, left, right, keep, send):
        value = dot_left(left[...], right[...]).astype(BF).reshape(groups, 2, piece, columns)

        @pl.when(s[INNER] == 0)
        def _():
            keep[0] = value[:, 0]
            send[0] = value[:, 1]

        @pl.when(s[INNER] == 1)
        def _():
            keep[0] = value[:, 1]
            send[0] = value[:, 0]

    block = pl.BlockSpec((1, groups, piece, columns), lambda i: (i, 0, 0, 0))
    return run(kernel,
               [(scalars, SCALARS), (left, pl.BlockSpec((tokens, width), lambda i: (0, i))),
                (right, pl.BlockSpec((tokens, columns), lambda i: (0, place)))],
               [shape((2, groups, piece, columns), BF)] * 2, after=after, grid=(2,),
               out_specs=[block, block],
               estimate=cost(4 * tokens * width * columns, tokens * (4 * width + 4 * columns)),
               name="weight_grad")


def small_grad(left, right, after=()):
    tokens, width = left.shape[0], left.shape[1] // 2
    columns = right.shape[1]

    def kernel(left, right, keep, send):
        send[...] = dot_left(left[:, width:], right[...]).astype(BF)
        keep[...] = dot_left(left[:, :width], right[...]).astype(BF)

    return run(kernel, [(left, WHOLE), (right, WHOLE)], [shape((width, columns), BF)] * 2, after=after,
               estimate=cost(4 * tokens * width * columns, 8 * MIB), name="small_grad")


def middle_back(scalars, both, h, r, gain, gain_far, cot, after=()):
    _, length, width = both.shape

    def kernel(s, both, h, r, gain, gain_far, g, dh, low, gain_part, db):
        def fill(first, second):
            db[:, :width] = first.astype(F32)
            db[:, width:] = second.astype(F32)

        pl.when(s[ROW] == 0)(lambda: fill(both[0], both[1]))
        pl.when(s[ROW] == 1)(lambda: fill(both[1], both[0]))
        rstd = r[...]
        normed = h[...] * rstd
        gains = jnp.concatenate([gain[...], gain_far[...]], axis=1)

        @pl.when(pl.program_id(0) == 0)
        def _():
            gain_part[...] = jnp.zeros_like(gain_part)

        gain_part[...] += jnp.sum(db[...] * normed, axis=0, keepdims=True)
        scaled = db[...] * gains
        mean = jnp.sum(scaled * normed, axis=1, keepdims=True) / D
        value = g[...].astype(F32) + rstd * (scaled - normed * mean)
        dh[...] = value
        low[...] = value.astype(BF)

    tile = TILE // 2
    outs = [shape((length, 2 * width), F32), shape((length, 2 * width), BF), shape((1, 2 * width), F32)]
    return run(kernel, [(scalars, SCALARS)] + [both_tiled(both, tile), tiled(h, tile), tiled(r, tile)]
               + [fixed(gain), fixed(gain_far), tiled(cot, tile)], outs, after=after,
               grid=(length // tile,),
               out_specs=[tiled(o, tile)[1] for o in outs[:2]] + [fixed(outs[2])[1]],
               scratch=[pltpu.VMEM((tile, 2 * width), F32)],
               estimate=cost(length * width * 30, 20 * MIB), name="middle_back")


def attend_back(scalars, low, q, k, v, lse, seg_col, seg_row, w_out, out_fetched, w_query, w_key, w_value,
                qkv_fetched, cosine, sine, after=()):
    length, qw = q.shape
    kw = k.shape[1]
    heads, pairs = qw // HD, kw // HD
    width = w_out.shape[1]
    total = qw + 2 * kw

    def kernel(s, low, q, k, v, lse, seg_col, seg_row, w_out, *refs):
        out_fetched, (wq, wk, wv), refs = refs[:QUARTERS], refs[QUARTERS:QUARTERS + 3], refs[QUARTERS + 3:]
        fetched, (cosine, sine, back, part, bias, wo, w, do, dk, dv) = refs[:QUARTERS], refs[QUARTERS:]
        wo[:, :width] = w_out[...]
        for piece, rows in placed(s, out_fetched, 0, qw):
            wo[rows, width:] = piece[...]
        do[...] = dot_right(low[...], wo[...]).astype(BF)
        dk[...] = jnp.zeros_like(dk)
        dv[...] = jnp.zeros_like(dv)
        for start in range(0, length, TILE):
            keys = start + TILE
            allowed = allowed_keys(seg_col, seg_row, start, TILE, keys)
            rows = slice(start, start + TILE)
            c, t = cosine[rows, :], sine[rows, :]
            for head in range(heads):
                pair = head // (heads // pairs)
                place = slice(head * HD, (head + 1) * HD)
                mine = slice(pair * HD, (pair + 1) * HD)
                scores = dot_right(q[rows, place], k[:keys, mine]) * HD ** (-0.5)
                probs = jnp.where(allowed, jnp.exp(scores - lse[rows, head:head + 1]), 0.0)
                grads = dot_right(do[rows, place], v[:keys, mine])
                delta = jnp.sum(probs * grads, axis=1, keepdims=True)
                score_grad = (probs * (grads - delta)).astype(BF)
                dv[:keys, mine] += dot_left(probs.astype(BF), do[rows, place])
                dk[:keys, mine] += dot_left(score_grad, q[rows, place])
                u = dot(score_grad, k[:keys, mine]) * HD ** (-0.5)
                back[rows, place] = (u * c - pltpu.roll(u, HD // 2, 1) * t).astype(BF)
        for pair in range(pairs):
            u = dk[:, pair * HD:(pair + 1) * HD] * HD ** (-0.5)
            u = u * cosine[...] - pltpu.roll(u, HD // 2, 1) * sine[...]
            back[:, qw + pair * HD:qw + (pair + 1) * HD] = u.astype(BF)
        back[:, qw + kw:] = dv[...].astype(BF)
        w[:width, :qw] = wq[...]
        w[:width, qw:qw + kw] = wk[...]
        w[:width, qw + kw:] = wv[...]
        for piece, rows in placed(s, fetched, width, width):
            w[rows, :] = piece[...]
        value = dot_right(back[...], w[...]).astype(BF)
        part[0] = value
        part[1] = value
        bias[...] = jnp.sum(back[...].astype(F32), axis=0, keepdims=True)

    arrays = [low, q, k, v, lse, seg_col, seg_row, w_out, *out_fetched, w_query, w_key, w_value,
              *qkv_fetched, cosine, sine]
    return run(kernel, [(scalars, SCALARS)] + [(a, WHOLE) for a in arrays],
               [shape((length, total), BF), shape((2, length, 2 * width), BF), shape((1, total), F32)],
               after=after,
               scratch=[pltpu.VMEM((qw, 2 * width), BF), pltpu.VMEM((2 * width, total), BF),
                        pltpu.VMEM((length, qw), BF), pltpu.VMEM((length, kw), F32),
                        pltpu.VMEM((length, kw), F32)],
               estimate=cost(10 * length * length * qw + 2 * length * 2 * width * (qw + total), 20 * MIB,
                             heads * length * length), name="attention_back")


def input_back(scalars, parts, mine, other, r, gain, gain_far, dh, after=()):
    length, width = mine.shape

    def kernel(s, parts, mine, other, r, dh, gain, gain_far, out, gain_part, n):
        def fill(first, second):
            n[:, :width] = first[...].astype(F32) * r[...]
            n[:, width:] = second[...].astype(F32) * r[...]

        pl.when(s[SAME] == 1)(lambda: fill(mine, other))
        pl.when(s[SAME] == 0)(lambda: fill(other, mine))
        da = parts[0].astype(F32) + parts[1].astype(F32)
        normed = n[...]

        @pl.when(pl.program_id(0) == 0)
        def _():
            gain_part[...] = jnp.zeros_like(gain_part)

        gain_part[...] += jnp.sum(da * normed, axis=0, keepdims=True)
        scaled = da * jnp.concatenate([gain[...], gain_far[...]], axis=1)
        mean = jnp.sum(scaled * normed, axis=1, keepdims=True) / D
        value = (dh[...] + r[...] * (scaled - normed * mean)).astype(BF)

        @pl.when(s[SAME] == 1)
        def _():
            out[...] = value[:, :width]

        @pl.when(s[SAME] == 0)
        def _():
            out[...] = value[:, width:]

    tile = TILE // 2
    outs = [shape((length, width), BF), shape((1, 2 * width), F32)]
    return run(kernel, [(scalars, SCALARS)] + [both_tiled(parts, tile)] + [tiled(a, tile) for a in (mine, other, r, dh)]
               + [fixed(gain), fixed(gain_far)], outs, after=after, grid=(length // tile,),
               out_specs=[tiled(outs[0], tile)[1], fixed(outs[1])[1]],
               scratch=[pltpu.VMEM((tile, 2 * width), F32)],
               estimate=cost(length * width * 30, 16 * MIB), name="input_back")


def body(
    inputs,
    segments,
    positions,
    w_query,
    w_key,
    w_value,
    b_query,
    b_key,
    b_value,
    w_out,
    gain_one,
    gain_two,
    w_gate,
    w_up,
    w_down,
    cotangent,
):
    length, width = inputs.shape
    query_width = w_query.shape[1]
    key_width = w_key.shape[1]
    total_width = query_width + 2 * key_width
    row = lax.axis_index("row")
    col = lax.axis_index("col")
    group = lax.axis_index("dp")
    groups = lax.axis_size("dp")
    inner = group % 2
    near_bit = (group // 2) % 2
    same = row == col

    hidden_here = w_gate.shape[1]
    blocks = hidden_here // LANES
    wide = -(-blocks // PARTS)
    part = wide * LANES
    overlap = PARTS * part - hidden_here

    def start_of(index):
        return jnp.minimum(index * wide, blocks - wide) * LANES

    mine_part = near_bit * 2 + row
    place_of = lambda low, high: 2 * low + high
    scalars = jnp.stack(
        [same.astype(jnp.int32), inner, start_of(mine_part), start_of(near_bit * 2 + 1 - row),
         jnp.where(mine_part == PARTS - 1, overlap, 0), place_of(inner, near_bit),
         place_of(1 - inner, near_bit), place_of(inner, 1 - near_bit), place_of(1 - inner, 1 - near_bit), row]
    ).astype(jnp.int32)

    def by_row(mine, other):
        return jnp.where(same, mine, other), jnp.where(same, other, mine)

    half = width // 2
    gains = jnp.stack([gain_one, gain_two])
    fetched_gains = swap_row(gains)
    mine = turn_square(inputs)
    sent_qkv = pack_weights(scalars, [w_query, w_key, w_value], None, (width // 4, total_width), OWN)
    qkv_direct = swap_row(sent_qkv)
    cot_near = swap_bit(cotangent, 1)
    mine = hold(mine, sent_qkv)
    other = swap_col(mine)
    sent_out = pack_weights(
        scalars, [w_out], None, (query_width // 4, width), OWN, after=[qkv_direct]
    )
    out_direct = swap_row(sent_out)
    sent_gu = []
    for chunk in range(2):
        sent_gu.append(pack_weights(
            scalars, [w_gate, w_up], part, (width // 4, 2 * part), INNER, scale=2, chunk=chunk,
            after=[out_direct, fetched_gains] + sent_gu,
        ))
    gu_direct = [swap_row(sent) for sent in sent_gu]
    fetched_gains = fetched_gains.astype(F32)
    gains = gains.astype(F32)

    def relay_far(direct, pair, near, *after):
        pair, near = hold(pair, *after), hold(near, *after)
        cut = direct.shape[0] // 2
        return direct, pair, near, swap_bit(pair[:cut], 1), swap_bit(near[cut:], 0)

    def relay_near(direct):
        return direct, swap_bit(direct, 0), swap_bit(direct, 1)

    cot_near = hold(cot_near, sent_gu[1])
    qkv_fetched = relay_far(*relay_near(qkv_direct), sent_gu[1])
    out_fetched = relay_far(*relay_near(out_direct), sent_gu[1])

    indices = jnp.arange(HD // 2, dtype=F32)
    inverse = jnp.exp(indices * (-2.0 / HD) * jnp.log(F32(THETA)))
    turned = positions.astype(F32)[:, None] * inverse[None, :]
    cosine, sine = jnp.cos(turned), jnp.sin(turned)
    cosine = jnp.concatenate([cosine, cosine], axis=1)
    sine = jnp.concatenate([-sine, sine], axis=1)
    bias = jnp.concatenate([b_query, b_key, b_value]).astype(F32)[None, :]
    seg_col, seg_row = segments[:, None], segments[None, :]

    q, k, v, low_one, r_one = project(
        scalars, mine, other, gains[:1], fetched_gains[:1], w_query, w_key, w_value, qkv_fetched,
        bias, cosine, sine, after=sent_gu[1:] + [cot_near],
    )

    gu_first = hold(gu_direct[0], k)
    gu_fetched = [gu_first, swap_bit(gu_first, 0)]
    cot = copy_of(cotangent, after=[k])
    cot_row = swap_row(cot)
    attended, lse, out_part = attend(scalars, q, k, v, seg_col, seg_row, w_out, out_fetched, after=[gu_first, cot])
    gu_second = hold(gu_direct[1], lse)
    gu_fetched += [gu_second, swap_bit(gu_second, 0)]
    h, low_near, low_far, r_two = norm_two(
        scalars, mine, other, trade_col(hold(out_part, gu_second)), gains[1:], fetched_gains[1:],
        after=[gu_fetched[1]],
    )

    b_row = swap_row(low_near)
    b_near = swap_bit(low_near, 1)
    cot_row = hold(cot_row, low_near)
    cot_low = swap_bit(cot_row[:half], 1)
    tokens = 4 * length
    ffn = functools.partial(
        gate_up, scalars, w_gate=w_gate, w_up=w_up, fetched=gu_fetched, total=tokens, part=part,
    )
    kept = ffn([(low_near, low_far)], first=0, after=[cot_row])
    b_row, b_near = hold(b_row, kept[1]), hold(b_near, kept[1])
    b_row_other, b_near_other = swap_col(b_row), swap_col(b_near)
    b_low = swap_bit(b_row[:half], 1)
    b_high = swap_row(b_near[half:])
    cot_near = hold(cot_near, b_near_other)
    cot_high = swap_row(cot_near[half:])
    sent_down = pack_weights(
        scalars, [w_down], None, (part // 2, width), INNER, after=[cot_near], down=True
    )
    down_direct = swap_row(sent_down)
    kept = ffn([(b_row, b_row_other), (b_near, b_near_other)], first=length, kept=kept, after=[sent_down])
    b_low, b_high, cot_low, cot_high, down_direct = (
        hold(array, kept[1]) for array in (b_low, b_high, cot_low, cot_high, down_direct)
    )
    down_fetched = down_direct, swap_bit(down_direct, 0)
    cot_far = jnp.concatenate([cot_low, cot_high], axis=0)
    cot_pieces = [[(one, swap_col(one)) for one in pair] for pair in ((cot, cot_row), (cot_near, cot_far))]
    kept = ffn([(b_low, swap_col(b_low)), (b_high, swap_col(b_high))], first=3 * length, kept=kept)
    full_two, hidden, up_slope, gate_slope = kept
    full_cot = place_rows(scalars, cot_pieces, after=[hidden])

    piece = width // groups
    down_keep, down_send = weight_grad(scalars, full_cot, hidden, piece, part)
    low_back = hidden_back(
        scalars, full_cot, up_slope, gate_slope, w_down, down_fetched, after=[down_send]
    )
    back = functools.partial(
        norm_back, scalars, low_back, w_gate, w_up, gu_fetched
    )

    def sum_far(keep, send):
        across = (keep.astype(F32) + send.astype(F32)).astype(BF)
        return across[:half], across[half:]

    def sum_near(keep, send, via_row, via_near):
        to_row = keep[:length].astype(F32) + send[:length].astype(F32)
        to_near = keep[length:].astype(F32) + send[length:].astype(F32)
        to_row = jnp.concatenate([to_row[:half], to_row[half:] + via_near.astype(F32)], axis=0)
        to_near = jnp.concatenate([to_near[:half] + via_row.astype(F32), to_near[half:]], axis=0)
        return to_row.astype(BF), to_near.astype(BF)

    def sum_own(keep, send, via_row, via_near):
        return (keep.astype(F32) + send.astype(F32)) + (via_row.astype(F32) + via_near.astype(F32))

    far_both = trade_col(back(3 * length, length, stacked=True)[0])
    to_row, to_near = sum_far(far_both[0], far_both[1])
    own_keep, own_send = back(0, length, after=[to_row, to_near])
    two_keep, two_send = back(length, 2 * length, after=[own_send])
    via_row, via_near = swap_row(to_row), swap_bit(to_near, 1)
    gate_keep, gate_send = weight_grad(scalars, full_two, low_back, piece, part, 0, after=[two_send])
    two_got = hold(swap_col(two_send), gate_send)
    via_row, via_near = hold(via_row, gate_send), hold(via_near, gate_send)
    to_row, to_near = sum_near(two_keep, two_got, via_row, via_near)
    via_row, via_near = swap_row(to_row), swap_bit(to_near, 1)
    own_got = swap_col(own_send)
    out_keep, out_send = down_project(scalars, hidden, w_down, down_fetched, after=[to_row, to_near])
    up_keep, up_send = weight_grad(scalars, full_two, low_back, piece, part, 1, after=[out_send])
    via_row, via_near = hold(via_row, up_send), hold(via_near, up_send)
    normed_grad = sum_own(own_keep, own_got, via_row, via_near).astype(BF)
    dh, low_mid, gain_two_part = middle_back(
        scalars, trade_col(jnp.stack([normed_grad, normed_grad])), h, r_two, gains[1:], fetched_gains[1:],
        full_cot,
    )
    out_grad_keep, out_grad_send = small_grad(low_mid, attended)
    first = 3 * length
    out_got = hold(swap_col(out_send), out_grad_send)
    to_row, to_near = sum_far(out_keep[first:], out_got[first:])
    back_low, in_part, bias_part = attend_back(
        scalars, low_mid, q, k, v, lse, seg_col, seg_row, w_out, out_fetched, w_query, w_key,
        w_value, qkv_fetched, cosine, sine, after=[out_grad_send, to_row, to_near],
    )
    via_row, via_near = hold(swap_row(to_row), back_low), hold(swap_bit(to_near, 1), back_low)
    qkv_grad_keep, qkv_grad_send = small_grad(low_one, back_low)
    to_row, to_near = sum_near(out_keep[length:first], out_got[length:first], via_row, via_near)
    input_grad, gain_one_part = input_back(
        scalars, trade_col(hold(in_part, qkv_grad_send)), mine, other, r_one, gains[:1], fetched_gains[:1], dh,
        after=[qkv_grad_send, to_row, to_near],
    )
    via_row, via_near = swap_row(to_row), swap_bit(to_near, 1)
    branch = sum_own(out_keep[:length], out_got[:length], via_row, via_near)
    h_mine, _ = by_row(h[:, :width], h[:, width:])
    output = turn_square((h_mine + branch).astype(BF))
    input_grad_low = input_grad
    input_grad = turn_square(input_grad).astype(F32)

    def add_bits(kept, sent, low_bits, after=()):
        value = kept.astype(F32) + sent.astype(F32)
        bits = (groups >> low_bits).bit_length() - 1
        for index in range(bits):
            bit = (group >> (low_bits + index)) % 2
            cut = value.reshape((value.shape[0], value.shape[1] // 2, 2) + value.shape[2:])
            recv = swap_bit(pick(cut, 1 - bit, 2).astype(BF), low_bits + index)
            if after:
                recv = hold(recv, *after)
            value = pick(cut, bit, 2) + recv.astype(F32)
        return value

    def ffn_sum(keep, send, steps):
        steps = [[step] if step is not None else [] for step in steps]
        recv = hold(swap_bit(send, 0), *steps[0])
        parts = (2, keep.shape[1] // 2, 2 * piece, keep.shape[3])
        value = add_bits(keep.reshape(parts), recv.reshape(parts), 2, after=steps[1])[:, 0]
        near, far = value[0], hold(swap_row(value[1].astype(BF)), *steps[2]).astype(F32)
        near, far = near.reshape(2, piece, -1), far.reshape(2, piece, -1)
        pair = jnp.stack([jnp.where(row == 0, near, far), jnp.where(row == 0, far, near)], axis=1)
        own = pick(pair, near_bit)
        across = hold(swap_bit(pick(pair, 1 - near_bit).astype(BF), 1), *steps[3]).astype(F32)
        four = jnp.concatenate(
            [jnp.where(near_bit == 0, own, across), jnp.where(near_bit == 0, across, own)], axis=0
        )
        last = four[PARTS - 1][:, overlap:]
        return jnp.concatenate([four[i] for i in range(PARTS - 1)] + [last], axis=1)

    down_grad = ffn_sum(down_keep, down_send, [two_send, up_send, low_mid, back_low]).T
    gate_grad = ffn_sum(gate_keep, gate_send, [low_mid, back_low, qkv_grad_send, None])
    up_grad = ffn_sum(up_keep, up_send, [back_low, input_grad_low, None, None])

    out_grads = out_grad_keep.astype(F32) + hold(swap_row(out_grad_send), qkv_grad_send).astype(F32)
    qkv_grads = qkv_grad_keep.astype(F32) + swap_row(qkv_grad_send).astype(F32)
    grads = jnp.concatenate([qkv_grads, out_grads], axis=1)
    cut = grads.reshape(groups // 2, 2, piece, -1)
    recv = swap_bit(pick(cut, 1 - inner, 1).astype(BF), 0)
    sum_attention = add_bits(pick(cut, inner, 1)[None], recv[None], 1)[0, 0]

    def canonical(value):
        first, second = value[:, :width], value[:, width:]
        return jnp.where(row == 0, value, jnp.concatenate([second, first], axis=1))[0]

    small = jnp.concatenate([bias_part[0], canonical(gain_one_part), canonical(gain_two_part)])
    small = small + swap_row(small)
    for bit in range(groups.bit_length() - 1):
        small = small + swap_bit(small, bit)
    gain_sums = pick(small[total_width:].reshape(2, 2, width), row, 1)

    return (
        output,
        input_grad,
        sum_attention[:, :query_width],
        sum_attention[:, query_width : query_width + key_width],
        sum_attention[:, query_width + key_width : total_width],
        small[:query_width],
        small[query_width : query_width + key_width],
        small[query_width + key_width : total_width],
        sum_attention[:, total_width:].T,
        gain_sums[0],
        gain_sums[1],
        gate_grad,
        up_grad,
        down_grad,
    )


def solution(mesh):
    return jax.shard_map(
        body,
        mesh=mesh,
        in_specs=(
            P(("dp", "col"), "row"),
            P(("dp", "row")),
            P(("dp", "row")),
            P("row", "col"),
            P("row", "col"),
            P("row", "col"),
            P("col"),
            P("col"),
            P("col"),
            P("col", "row"),
            P("row"),
            P("row"),
            P("row", "col"),
            P("row", "col"),
            P("col", "row"),
            P(("dp", "col"), "row"),
        ),
        out_specs=(
            P(("dp", "col"), "row"),
            P(("dp", "col"), "row"),
            P(("row", "dp"), "col"),
            P(("row", "dp"), "col"),
            P(("row", "dp"), "col"),
            P("col"),
            P("col"),
            P("col"),
            P("col", ("row", "dp")),
            P("row"),
            P("row"),
            P(("row", "dp"), "col"),
            P(("row", "dp"), "col"),
            P("col", ("row", "dp")),
        ),
        check_vma=False,
    )
```

```python
import functools

import jax
import jax.numpy as jnp
from jax import lax
from jax.experimental import pallas as pl
from jax.experimental.pallas import tpu as pltpu
from jax.sharding import PartitionSpec as P

D = 1536
HQ = 12
KVH = 2
HD = 128
LANES = 128
PARTS = 4
TILE = 256
WIDE_TILE = 384
MIB = 1024 * 1024
SCALE = 10.0
GLUE = 1e9

EPS = 1e-06
THETA = 1000000.0
BF = jnp.bfloat16
F32 = jnp.float32

SAME, INNER, START, START_FAR, SKIP, OWN, PAIR, NEAR, ACROSS, ROW, BITS = range(11)


def swap_row(value):
    return lax.ppermute(value, "row", [(0, 1), (1, 0)])


def swap_col(value):
    return lax.ppermute(value, "col", [(0, 1), (1, 0)])


def swap_bit(value, bit):
    size = lax.axis_size("dp")
    return lax.ppermute(value, "dp", [(i, i ^ (1 << bit)) for i in range(size)])


def trade_col(value):
    return lax.all_to_all(value, "col", 0, 0)


def turn_square(value):
    return lax.ppermute(value, ("row", "col"), [(0, 0), (1, 2), (2, 1), (3, 3)])


def pick(array, index, axis=0):
    return lax.dynamic_index_in_dim(array, index, axis, keepdims=False)


ANY = pl.BlockSpec(memory_space=pl.ANY)
SCALARS = pl.BlockSpec(memory_space=pltpu.SMEM)
WHOLE = pl.BlockSpec(memory_space=pltpu.VMEM)


def shape(dims, dtype):
    return jax.ShapeDtypeStruct(dims, dtype)


def cost(flops, moved=0, exps=0):
    return pl.CostEstimate(
        flops=int(flops * SCALE), bytes_accessed=int(moved * SCALE), transcendentals=int(exps * SCALE)
    )


LAST = []


def run(kernel, ins, outs, after=(), grid=None, out_specs=None, scratch=(), limit=56, aliases=None,
        estimate=None, name=None):
    given = len(ins)
    count = len(outs)
    after = [*after, *LAST]

    def body(*refs):
        kernel(*refs[:given], *refs[given + len(after):])

    results = pl.pallas_call(
        body,
        grid=grid if grid is not None else (),
        in_specs=[spec for _, spec in ins] + [ANY] * len(after),
        out_specs=out_specs if out_specs is not None else [WHOLE] * count,
        out_shape=outs,
        scratch_shapes=list(scratch),
        input_output_aliases=aliases or {},
        cost_estimate=estimate,
        name=name,
        compiler_params=pltpu.CompilerParams(vmem_limit_bytes=limit * MIB),
    )(*[array for array, _ in ins], *after)
    LAST[:] = [results[-1]]
    return results


def dot(left, right):
    return jnp.dot(left, right, preferred_element_type=F32)


def dot_right(left, right):
    return lax.dot_general(left, right, (((1,), (1,)), ((), ())), preferred_element_type=F32)


def dot_left(left, right):
    return lax.dot_general(left, right, (((0,), (0,)), ((), ())), preferred_element_type=F32)


def copies(pairs, sems):
    started = [pltpu.make_async_copy(src, dst, sems.at[i]) for i, (src, dst) in enumerate(pairs)]
    for one in started:
        one.start()
    for one in started:
        one.wait()


def rows_at(start, size):
    return pl.ds(pl.multiple_of(start, 16), size)


def lanes_at(start, size):
    return pl.ds(pl.multiple_of(start, LANES), size)


def pack_weights(scalars, arrays, part, dims, place, after=(), down=False, scale=1, chunk=0):
    def kernel(s, *refs):
        srcs, out, sems = refs[: len(arrays)], refs[len(arrays)], refs[len(arrays) + 1]
        start = (s[place] * scale + chunk) * dims[0]
        pairs = []
        at = 0
        for src in srcs:
            if down:
                pairs.append((src.at[rows_at(s[START_FAR] + start, dims[0]), :], out))
            elif part is not None:
                pairs.append((src.at[rows_at(start, dims[0]), lanes_at(s[START_FAR], part)],
                              out.at[:, at:at + part]))
                at += part
            else:
                wide = src.shape[1]
                pairs.append((src.at[rows_at(start, dims[0]), :], out.at[:, at:at + wide]))
                at += wide
        copies(pairs, sems)

    return run(kernel, [(scalars, SCALARS)] + [(a, ANY) for a in arrays], [shape(dims, BF)],
               after=after, scratch=[pltpu.SemaphoreType.DMA((len(arrays),))], limit=48,
               estimate=cost(0, 4 * dims[0] * dims[1]), name="pack")[0]


QUARTERS = 5
HALVES = 2
CHUNKED = 4


def placed(s, fetched, at, total):
    if len(fetched) in (HALVES, CHUNKED):
        chunks = len(fetched) // 2
        size = total // 2
        step = size // chunks
        rows = [rows_at(at + half * size + i * step, step)
                for i in range(chunks) for half in (s[INNER], 1 - s[INNER])]
    else:
        size = total // 4
        rows = [rows_at(at + s[place] * size, size) for place in (OWN, PAIR, NEAR)]
        rows += [rows_at(at + s[ACROSS] * size + i * (size // 2), size // 2) for i in range(2)]
    return list(zip(fetched, rows))


def project(scalars, mine, other, gain, gain_far, w_query, w_key, w_value, fetched, bias, cosine,
            sine, after=()):
    length, width = mine.shape
    qw, kw = w_query.shape[1], w_key.shape[1]
    total = qw + 2 * kw

    def kernel(s, mine, other, gain, gain_far, wq, wk, wv, *refs):
        fetched, (bias, cosine, sine, q, k, v, a, r, w) = refs[:QUARTERS], refs[QUARTERS:]
        x = mine[...].astype(F32)
        y = other[...].astype(F32)
        squares = jnp.sum(x * x, axis=1, keepdims=True) + jnp.sum(y * y, axis=1, keepdims=True)
        rstd = lax.rsqrt(squares / D + EPS)
        r[...] = rstd

        @pl.when(s[SAME] == 1)
        def _():
            a[:, :width] = (x * rstd * gain[...]).astype(BF)
            a[:, width:] = (y * rstd * gain_far[...]).astype(BF)

        @pl.when(s[SAME] == 0)
        def _():
            a[:, :width] = (y * rstd * gain[...]).astype(BF)
            a[:, width:] = (x * rstd * gain_far[...]).astype(BF)

        w[:width, :qw] = wq[...]
        w[:width, qw:qw + kw] = wk[...]
        w[:width, qw + kw:] = wv[...]
        for piece, rows in placed(s, fetched, width, width):
            w[rows, :] = piece[...]
        out = dot(a[...], w[...]) + bias[...]
        c, t = cosine[...], sine[...]
        for head in range(qw // HD):
            u = out[:, head * HD:(head + 1) * HD]
            q[:, head * HD:(head + 1) * HD] = (u * c + pltpu.roll(u, HD // 2, 1) * t).astype(BF)
        for head in range(kw // HD):
            u = out[:, qw + head * HD:qw + (head + 1) * HD]
            k[:, head * HD:(head + 1) * HD] = (u * c + pltpu.roll(u, HD // 2, 1) * t).astype(BF)
        v[...] = out[:, qw + kw:].astype(BF)

    arrays = [mine, other, gain, gain_far, w_query, w_key, w_value, *fetched, bias, cosine, sine]
    return run(kernel, [(scalars, SCALARS)] + [(a, WHOLE) for a in arrays],
               [shape((length, qw), BF), shape((length, kw), BF), shape((length, kw), BF),
                shape((length, 2 * width), BF), shape((length, 1), F32)], after=after,
               scratch=[pltpu.VMEM((2 * width, total), BF)],
               estimate=cost(2 * length * 2 * width * total, 12 * MIB), name="qkv")


def allowed_keys(seg_col, seg_row, start, size, keys):
    rows = lax.broadcasted_iota(jnp.int32, (size, keys), 0) + start
    cols = lax.broadcasted_iota(jnp.int32, (size, keys), 1)
    return (seg_col[start:start + size, :] == seg_row[:, :keys]) & (cols <= rows)


def attend(scalars, q, k, v, seg_col, seg_row, w_out, fetched, after=()):
    length, qw = q.shape
    heads, pairs = qw // HD, k.shape[1] // HD
    width = w_out.shape[1]

    def kernel(s, q, k, v, seg_col, seg_row, w_out, *refs):
        fetched, (o, lse, part, w) = refs[:QUARTERS], refs[QUARTERS:]
        for start in range(0, length, TILE):
            keys = start + TILE
            allowed = allowed_keys(seg_col, seg_row, start, TILE, keys)
            rows = slice(start, start + TILE)
            for head in range(heads):
                pair = head // (heads // pairs)
                place = slice(head * HD, (head + 1) * HD)
                mine = slice(pair * HD, (pair + 1) * HD)
                scores = dot_right(q[rows, place], k[:keys, mine]) * HD ** (-0.5)
                scores = jnp.where(allowed, scores, -1e30)
                top = jnp.max(scores, axis=1, keepdims=True)
                raised = jnp.exp(scores - top)
                total = jnp.sum(raised, axis=1, keepdims=True)
                weights = (raised * (1.0 / total)).astype(BF)
                o[rows, place] = dot(weights, v[:keys, mine]).astype(BF)
                lse[rows, head:head + 1] = top + jnp.log(total)
        w[:, :width] = w_out[...]
        for piece, rows in placed(s, fetched, 0, qw):
            w[rows, width:] = piece[...]
        value = dot(o[...], w[...]).astype(BF)
        part[0] = value
        part[1] = value

    arrays = [q, k, v, seg_col, seg_row, w_out, *fetched]
    return run(kernel, [(scalars, SCALARS)] + [(a, WHOLE) for a in arrays],
               [shape((length, qw), BF), shape((length, LANES), F32), shape((2, length, 2 * width), BF)],
               after=after,
               scratch=[pltpu.VMEM((qw, 2 * width), BF)],
               estimate=cost(4 * length * length * qw + 2 * length * qw * 2 * width, 12 * MIB,
                             heads * length * length), name="attention")


def tiled(array, tile):
    return array, pl.BlockSpec((tile, array.shape[1]), lambda i: (i, 0))


def both_tiled(array, tile):
    return array, pl.BlockSpec((2, tile, array.shape[2]), lambda i: (0, i, 0))


def fixed(array):
    return array, pl.BlockSpec(array.shape, lambda i: (0, 0))


def norm_two(scalars, mine, other, parts, gain, gain_far, after=()):
    length, width = mine.shape

    def kernel(s, mine, other, parts, gain, gain_far, h, near, far, r):
        added = parts[0].astype(F32) + parts[1].astype(F32)

        def fill(first, second):
            h[:, :width] = first[...].astype(F32) + added[:, :width]
            h[:, width:] = second[...].astype(F32) + added[:, width:]

        pl.when(s[SAME] == 1)(lambda: fill(mine, other))
        pl.when(s[SAME] == 0)(lambda: fill(other, mine))
        rstd = lax.rsqrt(jnp.sum(h[...] * h[...], axis=1, keepdims=True) / D + EPS)
        r[...] = rstd
        first = (h[:, :width] * rstd * gain[...]).astype(BF)
        second = (h[:, width:] * rstd * gain_far[...]).astype(BF)

        @pl.when(s[SAME] == 1)
        def _():
            near[...] = first
            far[...] = second

        @pl.when(s[SAME] == 0)
        def _():
            near[...] = second
            far[...] = first

    tile = TILE // 2
    outs = [shape((length, 2 * width), F32), shape((length, width), BF), shape((length, width), BF),
            shape((length, 1), F32)]
    return run(kernel, [(scalars, SCALARS)] + [tiled(mine, tile), tiled(other, tile), both_tiled(parts, tile)]
               + [fixed(gain), fixed(gain_far)], outs, after=after, grid=(length // tile,),
               out_specs=[tiled(o, tile)[1] for o in outs],
               estimate=cost(length * width * 20, 16 * MIB), name="norm_two")


def gate_up(scalars, pieces, w_gate, w_up, fetched, first, total, part, kept=None, after=(), share=1):
    width = pieces[0][0].shape[-1]
    counts = [piece[0].shape[-2] // WIDE_TILE for piece in pieces]
    steps = sum(counts)
    offset = first // WIDE_TILE
    starts = [sum(counts[:i]) for i in range(len(counts))]

    def kernel(s, *refs):
        halves, refs = refs[:given], refs[given:]
        wg, wu, *fetched = refs[:2 + CHUNKED]
        b, z, up_slope, gate_slope, w, sems = refs[-6:]
        step = pl.program_id(0)

        @pl.when(step == 0)
        def _():
            load_gate_up(s, wg, wu, fetched, w, sems, part, width)

        def fill(*piece):
            if len(piece) == 1:
                near, far, straight = piece[0].at[0], piece[0].at[1], s[ROW] == 0
            else:
                near, far, straight = *piece, s[SAME] == 1

            @pl.when(straight)
            def _():
                b[:, :width] = near[...]
                b[:, width:] = far[...]

            @pl.when(jnp.logical_not(straight))
            def _():
                b[:, :width] = far[...]
                b[:, width:] = near[...]

        at = 0
        for piece, start, count in zip(pieces, starts, counts):
            pl.when((step >= start) & (step < start + count))(
                functools.partial(fill, *halves[at:at + len(piece)])
            )
            at += len(piece)

        both = dot(b[...], w[...])
        gate, upward = both[:, :part], both[:, part:]
        counted = lax.broadcasted_iota(jnp.int32, gate.shape, 1) >= s[SKIP]
        sigma = 1.0 / (1.0 + jnp.exp(-gate))
        sigma = jnp.where(counted, sigma, 0.0)
        silu = gate * sigma
        z[...] = (silu * upward).astype(BF)
        up_slope[...] = silu.astype(BF)
        gate_slope[...] = (upward * sigma * (1.0 + gate * (1.0 - sigma))).astype(BF)

    def block(array, start, count):
        if len(array.shape) == 3:
            return pl.BlockSpec((2, WIDE_TILE, width), lambda i: (0, jnp.clip(i - start, 0, count - 1), 0))
        return pl.BlockSpec((WIDE_TILE, width), lambda i: (jnp.clip(i - start, 0, count - 1), 0))

    ins = [(scalars, SCALARS)]
    for piece, start, count in zip(pieces, starts, counts):
        ins += [(array, block(array, start, count)) for array in piece]
    given = len(ins) - 1
    ins += [(array, ANY) for array in (w_gate, w_up, *fetched)]
    aliases = {}
    if kept is not None:
        aliases = {len(ins) + i: i for i in range(4)}
        ins += [(array, ANY) for array in kept]
    at = lambda i: (i + offset, 0)
    length = steps * WIDE_TILE
    return run(kernel, ins,
               [shape((total, 2 * width), BF)] + [shape((total, part), BF)] * 3,
               after=after, grid=(steps,),
               out_specs=[pl.BlockSpec((WIDE_TILE, 2 * width), at)]
               + [pl.BlockSpec((WIDE_TILE, part), at)] * 3,
               scratch=[pltpu.VMEM((2 * width, 2 * part), BF), pltpu.SemaphoreType.DMA((2 + CHUNKED,))],
               aliases=aliases,
               estimate=cost(share * 8 * length * width * part, share * 12 * MIB, share * length * part),
               name="gate_up")


def load_gate_up(s, wg, wu, fetched, w, sems, part, width):
    lanes = lanes_at(s[START], part)
    copies([(wg.at[:, lanes], w.at[:width, :part]), (wu.at[:, lanes], w.at[:width, part:])]
           + [(piece, w.at[rows, :]) for piece, rows in placed(s, fetched, width, width)], sems)


def place_rows(scalars, pieces, after=()):
    length, width = pieces[0][0][0].shape
    flat = [array for group in pieces for pair in group for array in pair]

    def kernel(s, *refs):
        srcs, out, sems = refs[:len(flat)], refs[len(flat)], refs[len(flat) + 1]
        pairs = []
        for i, src in enumerate(srcs):
            group, side, token = i // 4, (i // 2) % 2, i % 2
            place = jnp.where(s[SAME] == 1, token, 1 - token) * length
            if i == len(srcs) - 1:
                place = (1 - s[ROW]) * length
            elif i == len(srcs) - 2:
                place = s[ROW] * length
            pairs.append((src, out.at[rows_at(2 * group * length + place, length),
                                      side * width:(side + 1) * width]))
        copies(pairs, sems)

    return run(kernel, [(scalars, SCALARS)] + [(a, ANY) for a in flat],
               [shape((2 * len(pieces) * length, 2 * width), BF)], after=after,
               scratch=[pltpu.SemaphoreType.DMA((len(flat),))], limit=48,
               estimate=cost(0, 16 * len(flat) * length * width // 4), name="place_rows")[0]


def copy_of(array, after):
    def kernel(src, out, sem):
        copies([(src, out)], sem)

    return run(kernel, [(array, ANY)], [shape(array.shape, array.dtype)], after=after,
               scratch=[pltpu.SemaphoreType.DMA((1,))], limit=48,
               estimate=cost(0, 4 * array.size), name="copy_of")[0]


def hold(array, *after):
    def kernel(src, out):
        pass

    return run(kernel, [(array, ANY)], [shape(array.shape, array.dtype)], after=after, out_specs=[ANY],
               aliases={0: 0}, limit=48, estimate=cost(0, 0), name="hold")[0]


def load_down(s, w_down, fetched, w, sems, part, width):
    copies([(w_down.at[rows_at(s[START], part), :], w.at[:, :width])]
           + [(piece, w.at[rows, width:]) for piece, rows in placed(s, fetched, 0, part)], sems)


def hidden_back(scalars, cot, up_slope, gate_slope, w_down, fetched, after=()):
    total, width = cot.shape[0], cot.shape[1] // 2
    part = up_slope.shape[1]

    def kernel(s, g, up_slope, gate_slope, w_down, *refs):
        fetched, (out, w, sems) = refs[:HALVES], refs[HALVES:]

        @pl.when(pl.program_id(0) == 0)
        def _():
            load_down(s, w_down, fetched, w, sems, part, width)

        back = dot_right(g[...], w[...])
        out[:, :part] = (back * gate_slope[...].astype(F32)).astype(BF)
        out[:, part:] = (back * up_slope[...].astype(F32)).astype(BF)

    at = lambda i: (i, 0)
    tile = 2 * TILE
    return run(kernel,
               [(scalars, SCALARS), (cot, pl.BlockSpec((tile, 2 * width), at)),
                (up_slope, pl.BlockSpec((tile, part), at)), (gate_slope, pl.BlockSpec((tile, part), at)),
                (w_down, ANY)] + [(piece, ANY) for piece in fetched],
               [shape((total, 2 * part), BF)], after=after, grid=(total // tile,),
               out_specs=[pl.BlockSpec((tile, 2 * part), at)],
               scratch=[pltpu.VMEM((part, 2 * width), BF), pltpu.SemaphoreType.DMA((1 + HALVES,))],
               estimate=cost(4 * total * width * part, total * 14000), name="hidden_back")[0]


def split_store(s, value, keep, send, width):
    first, second = value[:, :width].astype(BF), value[:, width:].astype(BF)

    @pl.when(s[SAME] == 1)
    def _():
        keep[...] = first
        send[...] = second

    @pl.when(s[SAME] == 0)
    def _():
        keep[...] = second
        send[...] = first


def norm_back(scalars, low, w_gate, w_up, fetched, first, length, after=(), stacked=False):
    width = w_gate.shape[0]
    part = low.shape[1] // 2
    offset = first // WIDE_TILE

    def kernel(s, low, wg, wu, *refs):
        fetched, (*outs, w, sems) = refs[:CHUNKED], refs[CHUNKED:]

        @pl.when(pl.program_id(0) == 0)
        def _():
            load_gate_up(s, wg, wu, fetched, w, sems, part, width)

        value = dot_right(low[...], w[...])
        if stacked:
            outs[0][s[ROW]] = value[:, :width].astype(BF)
            outs[0][1 - s[ROW]] = value[:, width:].astype(BF)
        else:
            split_store(s, value, *outs, width)

    tiles = [pl.BlockSpec((WIDE_TILE, width), lambda i: (i, 0))] * 2
    outs = [shape((length, width), BF)] * 2
    if stacked:
        outs = [shape((2, length, width), BF)]
        tiles = [pl.BlockSpec((2, WIDE_TILE, width), lambda i: (0, i, 0))]
    return run(kernel,
               [(scalars, SCALARS), (low, pl.BlockSpec((WIDE_TILE, 2 * part), lambda i: (i + offset, 0))),
                (w_gate, ANY), (w_up, ANY)] + [(piece, ANY) for piece in fetched],
               outs, after=after, grid=(length // WIDE_TILE,), out_specs=tiles,
               scratch=[pltpu.VMEM((2 * width, 2 * part), BF), pltpu.SemaphoreType.DMA((2 + CHUNKED,))],
               estimate=cost(8 * length * width * part, 8 * MIB + length * 8000), name="norm_back")


def down_project(scalars, hidden, w_down, fetched, after=()):
    total, part = hidden.shape
    width = w_down.shape[1]

    def kernel(s, z, w_down, *refs):
        fetched, (keep, send, w, sems) = refs[:HALVES], refs[HALVES:]

        @pl.when(pl.program_id(0) == 0)
        def _():
            load_down(s, w_down, fetched, w, sems, part, width)

        split_store(s, dot(z[...], w[...]), keep, send, width)

    at = lambda i: (i, 0)
    tile = 2 * TILE
    return run(kernel,
               [(scalars, SCALARS), (hidden, pl.BlockSpec((tile, part), at)), (w_down, ANY)]
               + [(piece, ANY) for piece in fetched],
               [shape((total, width), BF)] * 2, after=after, grid=(total // tile,),
               out_specs=[pl.BlockSpec((tile, width), at)] * 2,
               scratch=[pltpu.VMEM((part, 2 * width), BF), pltpu.SemaphoreType.DMA((1 + HALVES,))],
               estimate=cost(4 * total * width * part, total * 8000), name="down_project")


def weight_grad(scalars, left, right, piece, columns, place=0, after=()):
    tokens, width = left.shape[0], left.shape[1] // 2
    groups = width // (2 * piece)

    def kernel(s, left, right, keep, send):
        value = dot_left(left[...], right[...]).astype(BF).reshape(groups, 2, piece, columns)

        @pl.when(s[INNER] == 0)
        def _():
            keep[0] = value[:, 0]
            send[0] = value[:, 1]

        @pl.when(s[INNER] == 1)
        def _():
            keep[0] = value[:, 1]
            send[0] = value[:, 0]

    block = pl.BlockSpec((1, groups, piece, columns), lambda i: (i, 0, 0, 0))
    return run(kernel,
               [(scalars, SCALARS), (left, pl.BlockSpec((tokens, width), lambda i: (0, i))),
                (right, pl.BlockSpec((tokens, columns), lambda i: (0, place)))],
               [shape((2, groups, piece, columns), BF)] * 2, after=after, grid=(2,),
               out_specs=[block, block],
               estimate=cost(4 * tokens * width * columns, tokens * (4 * width + 4 * columns)),
               name="weight_grad")


def small_grad(left, right, after=()):
    tokens, width = left.shape[0], left.shape[1] // 2
    columns = right.shape[1]

    def kernel(left, right, keep, send):
        send[...] = dot_left(left[:, width:], right[...]).astype(BF)
        keep[...] = dot_left(left[:, :width], right[...]).astype(BF)

    return run(kernel, [(left, WHOLE), (right, WHOLE)], [shape((width, columns), BF)] * 2, after=after,
               estimate=cost(4 * tokens * width * columns, 8 * MIB), name="small_grad")


def middle_back(scalars, both, h, r, gain, gain_far, cot, after=()):
    _, length, width = both.shape

    def kernel(s, both, h, r, gain, gain_far, g, dh, low, gain_part, db):
        def fill(first, second):
            db[:, :width] = first.astype(F32)
            db[:, width:] = second.astype(F32)

        pl.when(s[ROW] == 0)(lambda: fill(both[0], both[1]))
        pl.when(s[ROW] == 1)(lambda: fill(both[1], both[0]))
        rstd = r[...]
        normed = h[...] * rstd
        gains = jnp.concatenate([gain[...], gain_far[...]], axis=1)

        @pl.when(pl.program_id(0) == 0)
        def _():
            gain_part[...] = jnp.zeros_like(gain_part)

        gain_part[...] += jnp.sum(db[...] * normed, axis=0, keepdims=True)
        scaled = db[...] * gains
        mean = jnp.sum(scaled * normed, axis=1, keepdims=True) / D
        value = g[...].astype(F32) + rstd * (scaled - normed * mean)
        dh[...] = value
        low[...] = value.astype(BF)

    tile = TILE // 2
    outs = [shape((length, 2 * width), F32), shape((length, 2 * width), BF), shape((1, 2 * width), F32)]
    return run(kernel, [(scalars, SCALARS)] + [both_tiled(both, tile), tiled(h, tile), tiled(r, tile)]
               + [fixed(gain), fixed(gain_far), tiled(cot, tile)], outs, after=after,
               grid=(length // tile,),
               out_specs=[tiled(o, tile)[1] for o in outs[:2]] + [fixed(outs[2])[1]],
               scratch=[pltpu.VMEM((tile, 2 * width), F32)],
               estimate=cost(length * width * 30, 20 * MIB), name="middle_back")


def attend_back(scalars, low, q, k, v, lse, seg_col, seg_row, w_out, out_fetched, w_query, w_key, w_value,
                qkv_fetched, cosine, sine, after=()):
    length, qw = q.shape
    kw = k.shape[1]
    heads, pairs = qw // HD, kw // HD
    width = w_out.shape[1]
    total = qw + 2 * kw

    def kernel(s, low, q, k, v, lse, seg_col, seg_row, w_out, *refs):
        out_fetched, (wq, wk, wv), refs = refs[:QUARTERS], refs[QUARTERS:QUARTERS + 3], refs[QUARTERS + 3:]
        fetched, (cosine, sine, back, bias, part, wo, w, do, dk, dv) = refs[:QUARTERS], refs[QUARTERS:]
        wo[:, :width] = w_out[...]
        for piece, rows in placed(s, out_fetched, 0, qw):
            wo[rows, width:] = piece[...]
        do[...] = dot_right(low[...], wo[...]).astype(BF)
        dk[...] = jnp.zeros_like(dk)
        dv[...] = jnp.zeros_like(dv)
        for start in range(0, length, TILE):
            keys = start + TILE
            allowed = allowed_keys(seg_col, seg_row, start, TILE, keys)
            rows = slice(start, start + TILE)
            c, t = cosine[rows, :], sine[rows, :]
            for head in range(heads):
                pair = head // (heads // pairs)
                place = slice(head * HD, (head + 1) * HD)
                mine = slice(pair * HD, (pair + 1) * HD)
                scores = dot_right(q[rows, place], k[:keys, mine]) * HD ** (-0.5)
                probs = jnp.where(allowed, jnp.exp(scores - lse[rows, head:head + 1]), 0.0)
                grads = dot_right(do[rows, place], v[:keys, mine])
                delta = jnp.sum(probs * grads, axis=1, keepdims=True)
                score_grad = (probs * (grads - delta)).astype(BF)
                dv[:keys, mine] += dot_left(probs.astype(BF), do[rows, place])
                dk[:keys, mine] += dot_left(score_grad, q[rows, place])
                u = dot(score_grad, k[:keys, mine]) * HD ** (-0.5)
                back[rows, place] = (u * c - pltpu.roll(u, HD // 2, 1) * t).astype(BF)
        for pair in range(pairs):
            u = dk[:, pair * HD:(pair + 1) * HD] * HD ** (-0.5)
            u = u * cosine[...] - pltpu.roll(u, HD // 2, 1) * sine[...]
            back[:, qw + pair * HD:qw + (pair + 1) * HD] = u.astype(BF)
        back[:, qw + kw:] = dv[...].astype(BF)
        w[:width, :qw] = wq[...]
        w[:width, qw:qw + kw] = wk[...]
        w[:width, qw + kw:] = wv[...]
        for piece, rows in placed(s, fetched, width, width):
            w[rows, :] = piece[...]
        value = dot_right(back[...], w[...]).astype(BF)
        part[0] = value
        part[1] = value
        bias[...] = jnp.sum(back[...].astype(F32), axis=0, keepdims=True)

    arrays = [low, q, k, v, lse, seg_col, seg_row, w_out, *out_fetched, w_query, w_key, w_value,
              *qkv_fetched, cosine, sine]
    return run(kernel, [(scalars, SCALARS)] + [(a, WHOLE) for a in arrays],
               [shape((length, total), BF), shape((1, total), F32), shape((2, length, 2 * width), BF)],
               after=after,
               scratch=[pltpu.VMEM((qw, 2 * width), BF), pltpu.VMEM((2 * width, total), BF),
                        pltpu.VMEM((length, qw), BF), pltpu.VMEM((length, kw), F32),
                        pltpu.VMEM((length, kw), F32)],
               estimate=cost(10 * length * length * qw + 2 * length * 2 * width * (qw + total), 20 * MIB,
                             heads * length * length), name="attention_back")


def input_back(scalars, parts, mine, other, r, gain, gain_far, dh, after=()):
    length, width = mine.shape

    def kernel(s, parts, mine, other, r, dh, gain, gain_far, out, gain_part, n):
        def fill(first, second):
            n[:, :width] = first[...].astype(F32) * r[...]
            n[:, width:] = second[...].astype(F32) * r[...]

        pl.when(s[SAME] == 1)(lambda: fill(mine, other))
        pl.when(s[SAME] == 0)(lambda: fill(other, mine))
        da = parts[0].astype(F32) + parts[1].astype(F32)
        normed = n[...]

        @pl.when(pl.program_id(0) == 0)
        def _():
            gain_part[...] = jnp.zeros_like(gain_part)

        gain_part[...] += jnp.sum(da * normed, axis=0, keepdims=True)
        scaled = da * jnp.concatenate([gain[...], gain_far[...]], axis=1)
        mean = jnp.sum(scaled * normed, axis=1, keepdims=True) / D
        value = (dh[...] + r[...] * (scaled - normed * mean)).astype(BF)

        @pl.when(s[SAME] == 1)
        def _():
            out[...] = value[:, :width]

        @pl.when(s[SAME] == 0)
        def _():
            out[...] = value[:, width:]

    tile = TILE // 2
    outs = [shape((length, width), BF), shape((1, 2 * width), F32)]
    return run(kernel, [(scalars, SCALARS)] + [both_tiled(parts, tile)] + [tiled(a, tile) for a in (mine, other, r, dh)]
               + [fixed(gain), fixed(gain_far)], outs, after=after, grid=(length // tile,),
               out_specs=[tiled(outs[0], tile)[1], fixed(outs[1])[1]],
               scratch=[pltpu.VMEM((tile, 2 * width), F32)],
               estimate=cost(length * width * 30, 16 * MIB), name="input_back")


def halve(scalars, keep, recv, bit, after=()):
    parts, many, _, rows, columns = keep.shape

    def kernel(s, keep, recv, kept, sent):
        total = (keep[0, 0].astype(F32) + recv[0, 0].astype(F32)).astype(BF)

        @pl.when(s[BITS + bit] == 0)
        def _():
            kept[0, 0] = total[0]
            sent[0, 0] = total[1]

        @pl.when(s[BITS + bit] == 1)
        def _():
            kept[0, 0] = total[1]
            sent[0, 0] = total[0]

    wide = pl.BlockSpec((1, 1, 2, rows, columns), lambda i, j: (i, j, 0, 0, 0))
    narrow = pl.BlockSpec((1, 1, rows, columns), lambda i, j: (i, j, 0, 0))
    return run(kernel, [(scalars, SCALARS), (keep, wide), (recv, wide)],
               [shape((parts, many, rows, columns), BF)] * 2, after=after, grid=(parts, many),
               out_specs=[narrow] * 2, estimate=cost(GLUE), name="halve")


def sum_rows(keep, recv, after=()):
    _, pieces, rows, columns = keep.shape

    def kernel(keep, recv, near, sent):
        near[0] = (keep[0, 0].astype(F32) + recv[0, 0].astype(F32)).astype(BF)
        sent[0] = (keep[1, 0].astype(F32) + recv[1, 0].astype(F32)).astype(BF)

    wide = pl.BlockSpec((2, 1, rows, columns), lambda i: (0, i, 0, 0))
    narrow = pl.BlockSpec((1, rows, columns), lambda i: (i, 0, 0))
    return run(kernel, [(keep, wide), (recv, wide)], [shape((pieces, rows, columns), BF)] * 2, after=after,
               grid=(pieces,), out_specs=[narrow] * 2, estimate=cost(GLUE),
               name="sum_rows")


def deal_near(scalars, near, far, after=()):
    def kernel(s, near, far, own, sent):
        for bit, out in ((s[BITS + 1], own), (1 - s[BITS + 1], sent)):
            out[s[ROW]] = near[bit]
            out[1 - s[ROW]] = far[bit]

    return run(kernel, [(scalars, SCALARS), (near, WHOLE), (far, WHOLE)], [shape(near.shape, BF)] * 2,
               after=after, estimate=cost(GLUE), name="deal_near")


def lay_columns(scalars, own, across, overlap, after=()):
    _, rows, part = own.shape
    total = PARTS * part - overlap

    def kernel(s, own, across, out):
        def fill(first, second):
            for i, piece in enumerate((first[0], first[1], second[0])):
                out[:, i * part:(i + 1) * part] = piece.astype(F32)
            out[:, 3 * part:] = second[1][:, overlap:].astype(F32)

        pl.when(s[BITS + 1] == 0)(lambda: fill(own, across))
        pl.when(s[BITS + 1] == 1)(lambda: fill(across, own))

    return run(kernel, [(scalars, SCALARS), (own, WHOLE), (across, WHOLE)], [shape((rows, total), F32)],
               after=after, estimate=cost(GLUE), name="lay_columns")[0]


def sum_plain(keep, recv, after=()):
    def kernel(keep, recv, out):
        out[...] = keep[...].astype(F32) + recv[...].astype(F32)

    return run(kernel, [(keep, WHOLE), (recv, WHOLE)], [shape(keep.shape, F32)], after=after,
               estimate=cost(GLUE), name="sum_plain")[0]


def sum_split(keep, recv, widths, after=()):
    rows = keep.shape[1]

    def kernel(keep, recv, *outs):
        at = 0
        for out, width in zip(outs, widths):
            part = slice(at, at + width)
            out[...] = keep[0, :, part].astype(F32) + recv[0, :, part].astype(F32)
            at += width

    return run(kernel, [(keep, WHOLE), (recv, WHOLE)], [shape((rows, width), F32) for width in widths],
               after=after, estimate=cost(GLUE), name="sum_split")


def sum_far(keep, send, first, after=()):
    width = keep.shape[1]
    half = width // 2
    offset = first // half

    def kernel(keep, send, to_row, to_near):
        value = (keep[...].astype(F32) + send[...].astype(F32)).astype(BF)
        pl.when(pl.program_id(0) == 0)(lambda: to_row.__setitem__(..., value))
        pl.when(pl.program_id(0) == 1)(lambda: to_near.__setitem__(..., value))

    block = pl.BlockSpec((half, width), lambda i: (offset + i, 0))
    return run(kernel, [(keep, block), (send, block)], [shape((half, width), BF)] * 2, after=after, grid=(2,),
               out_specs=[pl.BlockSpec((half, width), lambda i: (0, 0))] * 2,
               estimate=cost(GLUE), name="sum_far")


def sum_near(keep, send, via_row, via_near, first, after=()):
    half, width = via_row.shape
    length = 2 * half
    offset = first // length

    def kernel(keep, send, via_row, via_near, to_row, to_near):
        step = pl.program_id(0)

        def put(out, plain, more, via):
            out[plain, :] = (keep[plain, :].astype(F32) + send[plain, :].astype(F32)).astype(BF)
            out[more, :] = (keep[more, :].astype(F32) + send[more, :].astype(F32)
                            + via[...].astype(F32)).astype(BF)

        low, high = slice(0, half), slice(half, length)
        pl.when(step == 0)(lambda: put(to_row, low, high, via_near))
        pl.when(step == 1)(lambda: put(to_near, high, low, via_row))

    block = pl.BlockSpec((length, width), lambda i: (offset + i, 0))
    whole = pl.BlockSpec((length, width), lambda i: (0, 0))
    return run(kernel, [(keep, block), (send, block), fixed(via_row), fixed(via_near)],
               [shape((length, width), BF)] * 2, after=after, grid=(2,), out_specs=[whole, whole],
               estimate=cost(GLUE), name="sum_near")


def sum_own(keep, send, via_row, via_near, after=()):
    length, width = via_row.shape

    def kernel(keep, send, via_row, via_near, out):
        value = (keep[...].astype(F32) + send[...].astype(F32)) + (
            via_row[...].astype(F32) + via_near[...].astype(F32))
        out[0] = value.astype(BF)
        out[1] = value.astype(BF)

    outs = [shape((2, length, width), BF)]
    return run(kernel, [tiled(a, TILE) for a in (keep, send, via_row, via_near)], outs, after=after,
               grid=(length // TILE,), out_specs=[both_tiled(outs[0], TILE)[1]],
               estimate=cost(GLUE), name="sum_own")[0]


def sum_output(scalars, keep, send, via_row, via_near, h, after=()):
    length, width = via_row.shape

    def kernel(s, keep, send, via_row, via_near, h, out):
        value = (keep[...].astype(F32) + send[...].astype(F32)) + (
            via_row[...].astype(F32) + via_near[...].astype(F32))
        pl.when(s[SAME] == 1)(lambda: out.__setitem__(..., (h[:, :width] + value).astype(BF)))
        pl.when(s[SAME] == 0)(lambda: out.__setitem__(..., (h[:, width:] + value).astype(BF)))

    outs = [shape((length, width), BF)]
    return run(kernel, [(scalars, SCALARS)] + [tiled(a, TILE) for a in (keep, send, via_row, via_near, h)],
               outs, after=after, grid=(length // TILE,), out_specs=[tiled(outs[0], TILE)[1]],
               estimate=cost(GLUE), name="sum_output")[0]


def body(
    inputs,
    segments,
    positions,
    w_query,
    w_key,
    w_value,
    b_query,
    b_key,
    b_value,
    w_out,
    gain_one,
    gain_two,
    w_gate,
    w_up,
    w_down,
    cotangent,
):
    length, width = inputs.shape
    query_width = w_query.shape[1]
    key_width = w_key.shape[1]
    total_width = query_width + 2 * key_width
    row = lax.axis_index("row")
    col = lax.axis_index("col")
    group = lax.axis_index("dp")
    groups = lax.axis_size("dp")
    inner = group % 2
    near_bit = (group // 2) % 2
    same = row == col

    hidden_here = w_gate.shape[1]
    blocks = hidden_here // LANES
    wide = -(-blocks // PARTS)
    part = wide * LANES
    overlap = PARTS * part - hidden_here

    def start_of(index):
        return jnp.minimum(index * wide, blocks - wide) * LANES

    mine_part = near_bit * 2 + row
    place_of = lambda low, high: 2 * low + high
    scalars = jnp.stack(
        [same.astype(jnp.int32), inner, start_of(mine_part), start_of(near_bit * 2 + 1 - row),
         jnp.where(mine_part == PARTS - 1, overlap, 0), place_of(inner, near_bit),
         place_of(1 - inner, near_bit), place_of(inner, 1 - near_bit), place_of(1 - inner, 1 - near_bit), row]
        + [(group >> bit) % 2 for bit in range(groups.bit_length() - 1)]
    ).astype(jnp.int32)

    def by_row(mine, other):
        return jnp.where(same, mine, other), jnp.where(same, other, mine)

    LAST.clear()
    half = width // 2
    gains = jnp.stack([gain_one, gain_two])
    fetched_gains = swap_row(gains)
    mine = turn_square(inputs)
    other = swap_col(mine)
    def pack_gate_up(chunk):
        return swap_row(pack_weights(
            scalars, [w_gate, w_up], part, (width // 4, 2 * part), INNER, scale=2, chunk=chunk
        ))

    def relay(direct):
        pair, near = swap_bit(direct, 0), swap_bit(direct, 1)
        cut = direct.shape[0] // 2
        return direct, pair, near, swap_bit(pair[:cut], 1), swap_bit(near[cut:], 0)

    qkv_fetched = relay(swap_row(
        pack_weights(scalars, [w_query, w_key, w_value], None, (width // 4, total_width), OWN)
    ))
    out_fetched = relay(swap_row(
        pack_weights(scalars, [w_out], None, (query_width // 4, width), OWN)
    ))
    fetched_gains = hold(fetched_gains).astype(F32)
    gains = gains.astype(F32)
    gu_direct = [pack_gate_up(0), pack_gate_up(1)]
    gu_first = hold(gu_direct[0])
    gu_fetched = [gu_first, swap_bit(gu_first, 0)]

    indices = jnp.arange(HD // 2, dtype=F32)
    inverse = jnp.exp(indices * (-2.0 / HD) * jnp.log(F32(THETA)))
    turned = positions.astype(F32)[:, None] * inverse[None, :]
    cosine, sine = jnp.cos(turned), jnp.sin(turned)
    cosine = jnp.concatenate([cosine, cosine], axis=1)
    sine = jnp.concatenate([-sine, sine], axis=1)
    bias = jnp.concatenate([b_query, b_key, b_value]).astype(F32)[None, :]
    seg_col, seg_row = segments[:, None], segments[None, :]

    q, k, v, low_one, r_one = project(
        scalars, mine, other, gains[:1], fetched_gains[:1], w_query, w_key, w_value, qkv_fetched,
        bias, cosine, sine,
    )
    cot = copy_of(cotangent, [])
    cot_row = swap_row(cot)
    cot_near = swap_bit(cot, 1)
    attended, lse, out_part = attend(scalars, q, k, v, seg_col, seg_row, w_out, out_fetched)
    gu_second = hold(gu_direct[1])
    gu_fetched += [gu_second, swap_bit(gu_second, 0)]
    cot_other = swap_col(cot)
    gu_fetched[1] = hold(gu_fetched[1])
    cot_other = hold(cot_other)
    cot_near = hold(cot_near)
    h, low_near, low_far, r_two = norm_two(
        scalars, mine, other, trade_col(out_part), gains[1:], fetched_gains[1:]
    )

    b_row = swap_row(low_near)
    b_near = swap_bit(low_near, 1)
    cot_row = hold(cot_row)
    cot_low = swap_bit(cot_row[:half], 1)
    tokens = 4 * length
    ffn = functools.partial(
        gate_up, scalars, w_gate=w_gate, w_up=w_up, fetched=gu_fetched, total=tokens, part=part,
    )
    kept = ffn([(low_near, low_far)], first=0)
    b_row = hold(b_row)
    b_row_other = swap_col(b_row)
    b_low = swap_bit(b_row[:half], 1)
    b_near = hold(b_near)
    b_near_other = swap_col(b_near)
    b_high = swap_row(b_near[half:])
    b_row_other, b_near_other = hold(b_row_other), hold(b_near_other)
    cot_high = swap_row(hold(cot_near[half:]))
    sent_down = pack_weights(scalars, [w_down], None, (part // 2, width), INNER, down=True)
    down_direct = swap_row(sent_down)
    kept = ffn([(b_row, b_row_other), (b_near, b_near_other)], first=length, kept=kept)
    b_far = jnp.concatenate([hold(b_low), hold(b_high)], axis=0)
    b_far = trade_col(jnp.stack([b_far, b_far]))
    cot_row_other, cot_near_other = swap_col(cot_row), swap_col(cot_near)
    kept = ffn([(b_far,)], first=3 * length, kept=kept, after=[sent_down], share=0)
    full_two, hidden, up_slope, gate_slope = kept
    cot_row_other, cot_near_other = hold(cot_row_other), hold(cot_near_other)
    cot_far = jnp.concatenate([hold(cot_low), hold(cot_high)], axis=0)
    cot_far = trade_col(jnp.stack([cot_far, cot_far]))
    down_direct = hold(down_direct)
    down_fetched = down_direct, swap_bit(down_direct, 0)
    full_cot = place_rows(
        scalars, [[(cot, cot_other), (cot_row, cot_row_other)],
                  [(cot_near, cot_near_other), (cot_far[0], cot_far[1])]],
    )

    piece = width // groups
    down_keep, down_send = weight_grad(scalars, full_cot, hidden, piece, part)
    down_recv = swap_bit(down_send, 0)
    low_back = hidden_back(scalars, full_cot, up_slope, gate_slope, w_down, down_fetched)
    back = functools.partial(
        norm_back, scalars, low_back, w_gate, w_up, gu_fetched
    )
    far_both = trade_col(back(3 * length, length, stacked=True)[0])
    across = (far_both[0].astype(F32) + far_both[1].astype(F32)).astype(BF)
    to_row, to_near = across[:half], across[half:]
    rest_keep, rest_send = back(0, 3 * length, after=[to_row, to_near])
    via_row, via_near = swap_row(to_row), swap_bit(to_near, 1)
    gate_keep, gate_send = weight_grad(scalars, full_two, low_back, piece, part, 0)
    gate_recv = swap_bit(gate_send, 0)
    rest_got = swap_col(rest_send)
    to_row, to_near = sum_near(rest_keep, rest_got, via_row, via_near, length)
    via_row, via_near = swap_row(to_row), swap_bit(to_near, 1)

    high_bits = range(2, groups.bit_length() - 1)

    def grad_high(keep, recv):
        for bit in high_bits:
            cut = (2, keep.size // (4 * 2 * piece * part), 2, 2 * piece, part)
            keep, send = halve(scalars, keep.reshape(cut), recv.reshape(cut), bit)
            recv = swap_bit(send, bit)
        return keep, recv

    def grad_row(keep, recv):
        cut = (2, 2, piece, part)
        near, send = sum_rows(keep.reshape(cut), recv.reshape(cut))
        return near, swap_row(send)

    def grad_near(near, far):
        own, send = deal_near(scalars, near, far)
        return own, swap_bit(send, 1)

    def square_first(left, right):
        keep, send = weight_grad(scalars, left, right, piece, right.shape[1])
        return keep, swap_bit(send, 0)

    def square_next(keep, recv, bit):
        cut = (2, groups >> (bit + 1), 2, piece, keep.shape[-1])
        keep, send = halve(scalars, keep.reshape(cut), recv.reshape(cut), bit)
        return keep, swap_bit(send, bit)

    def square_row(keep, recv):
        near, send = sum_rows(keep, recv)
        return near, swap_row(send)

    def square_last(near, far):
        return sum_plain(near, far).reshape(piece, -1)

    last_bits = range(2, groups.bit_length() - 1)

    down = grad_high(down_keep, down_recv)
    out_keep, out_send = down_project(scalars, hidden, w_down, down_fetched)
    out_got = swap_col(out_send)
    up_keep, up_send = weight_grad(scalars, full_two, low_back, piece, part, 1)
    up_recv = swap_bit(up_send, 0)
    normed_grad = sum_own(rest_keep, rest_got, via_row, via_near)
    first = 3 * length
    to_row, to_near = sum_far(out_keep, out_got, first)
    via_row, via_near = swap_row(to_row), swap_bit(to_near, 1)
    dh, low_mid, gain_two_part = middle_back(
        scalars, trade_col(normed_grad), h, r_two, gains[1:], fetched_gains[1:], full_cot,
    )
    gate = grad_high(gate_keep, gate_recv)
    to_row, to_near = sum_near(out_keep, out_got, via_row, via_near, length)
    via_row, via_near = swap_row(to_row), swap_bit(to_near, 1)
    up_recv = hold(up_recv)
    out_sum = square_first(low_mid, attended)
    down = grad_row(*down)
    back_low, bias_part, in_part = attend_back(
        scalars, low_mid, q, k, v, lse, seg_col, seg_row, w_out, out_fetched, w_query, w_key,
        w_value, qkv_fetched, cosine, sine,
    )
    down = down[0], hold(down[1])
    qkv_sum = square_first(low_one, back_low)
    via_row, via_near = hold(via_row), hold(via_near)
    up = grad_high(up_keep, up_recv)
    input_grad, gain_one_part = input_back(
        scalars, trade_col(in_part), mine, other, r_one, gains[:1], fetched_gains[:1], dh
    )
    input_grad = turn_square(input_grad)

    def canonical(value):
        first, second = value[:, :width], value[:, width:]
        return jnp.where(row == 0, value, jnp.concatenate([second, first], axis=1))[0]

    small = jnp.concatenate([bias_part[0], canonical(gain_one_part), canonical(gain_two_part)])

    def small_step(value, swap):
        return value + hold(swap(value))

    gate = grad_row(*gate)
    out_sum = square_next(*out_sum, 1)
    qkv_sum = square_next(*qkv_sum, 1)
    input_grad = hold(input_grad).astype(F32)
    output = turn_square(sum_output(scalars, out_keep, out_got, via_row, via_near, h))
    up = grad_row(*up)
    for bit in last_bits:
        out_sum = square_next(*out_sum, bit)
    gate = grad_near(*gate)
    down = grad_near(*down)
    for bit in last_bits:
        qkv_sum = square_next(*qkv_sum, bit)
    output = hold(output)
    small = small_step(small, lambda value: swap_bit(value, 0))
    gate_grad = lay_columns(scalars, *gate, overlap)
    out_sum = square_row(*out_sum)
    up = grad_near(*up)
    down_grad = lay_columns(scalars, *down, overlap).T
    for bit in range(1, groups.bit_length() - 1):
        small = small_step(small, lambda value, bit=bit: swap_bit(value, bit))
    qkv_sum = square_row(*qkv_sum)
    out_grad = square_last(*out_sum).T
    small = small_step(small, swap_row)
    up_grad = lay_columns(scalars, *up, overlap)
    qkv_grads = sum_split(*qkv_sum, (query_width, key_width, key_width))
    gain_sums = pick(small[total_width:].reshape(2, 2, width), row, 1)

    return (
        output,
        input_grad,
        *qkv_grads,
        small[:query_width],
        small[query_width : query_width + key_width],
        small[query_width + key_width : total_width],
        out_grad,
        gain_sums[0],
        gain_sums[1],
        gate_grad,
        up_grad,
        down_grad,
    )


def solution(mesh):
    return jax.shard_map(
        body,
        mesh=mesh,
        in_specs=(
            P(("dp", "col"), "row"),
            P(("dp", "row")),
            P(("dp", "row")),
            P("row", "col"),
            P("row", "col"),
            P("row", "col"),
            P("col"),
            P("col"),
            P("col"),
            P("col", "row"),
            P("row"),
            P("row"),
            P("row", "col"),
            P("row", "col"),
            P("col", "row"),
            P(("dp", "col"), "row"),
        ),
        out_specs=(
            P(("dp", "col"), "row"),
            P(("dp", "col"), "row"),
            P(("row", "dp"), "col"),
            P(("row", "dp"), "col"),
            P(("row", "dp"), "col"),
            P("col"),
            P("col"),
            P("col"),
            P("col", ("row", "dp")),
            P("row"),
            P("row"),
            P(("row", "dp"), "col"),
            P(("row", "dp"), "col"),
            P("col", ("row", "dp")),
        ),
        check_vma=False,
    )
```

```python
import functools

import jax
import jax.numpy as jnp
from jax import lax
from jax.experimental import pallas as pl
from jax.experimental.pallas import tpu as pltpu
from jax.sharding import PartitionSpec as P

D = 1536
HQ = 12
KVH = 2
HD = 128
LANES = 128
PARTS = 4
TILE = 256
WIDE_TILE = 384
MIB = 1024 * 1024
SCALE = 10.0
GLUE = 1e9

EPS = 1e-06
THETA = 1000000.0
BF = jnp.bfloat16
F32 = jnp.float32

SAME, INNER, START, START_FAR, SKIP, OWN, PAIR, NEAR, ACROSS, ROW, BITS = range(11)


def swap_row(value):
    return lax.ppermute(value, "row", [(0, 1), (1, 0)])


def swap_col(value):
    return lax.ppermute(value, "col", [(0, 1), (1, 0)])


def swap_bit(value, bit):
    size = lax.axis_size("dp")
    return lax.ppermute(value, "dp", [(i, i ^ (1 << bit)) for i in range(size)])


def trade_col(value):
    return lax.all_to_all(value, "col", 0, 0)


def turn_square(value):
    return lax.ppermute(value, ("row", "col"), [(0, 0), (1, 2), (2, 1), (3, 3)])


def pick(array, index, axis=0):
    return lax.dynamic_index_in_dim(array, index, axis, keepdims=False)


ANY = pl.BlockSpec(memory_space=pl.ANY)
SCALARS = pl.BlockSpec(memory_space=pltpu.SMEM)
WHOLE = pl.BlockSpec(memory_space=pltpu.VMEM)


def shape(dims, dtype):
    return jax.ShapeDtypeStruct(dims, dtype)


def cost(flops, moved=0, exps=0):
    return pl.CostEstimate(
        flops=int(flops * SCALE), bytes_accessed=int(moved * SCALE), transcendentals=int(exps * SCALE)
    )


LAST = []


def run(kernel, ins, outs, after=(), grid=None, out_specs=None, scratch=(), limit=56, aliases=None,
        estimate=None, name=None):
    given = len(ins)
    count = len(outs)
    after = [*after, *LAST]

    def body(*refs):
        kernel(*refs[:given], *refs[given + len(after):])

    results = pl.pallas_call(
        body,
        grid=grid if grid is not None else (),
        in_specs=[spec for _, spec in ins] + [ANY] * len(after),
        out_specs=out_specs if out_specs is not None else [WHOLE] * count,
        out_shape=outs,
        scratch_shapes=list(scratch),
        input_output_aliases=aliases or {},
        cost_estimate=estimate,
        name=name,
        compiler_params=pltpu.CompilerParams(vmem_limit_bytes=limit * MIB),
    )(*[array for array, _ in ins], *after)
    LAST[:] = [results[-1]]
    return results


def dot(left, right):
    return jnp.dot(left, right, preferred_element_type=F32)


def dot_right(left, right):
    return lax.dot_general(left, right, (((1,), (1,)), ((), ())), preferred_element_type=F32)


def dot_left(left, right):
    return lax.dot_general(left, right, (((0,), (0,)), ((), ())), preferred_element_type=F32)


def copies(pairs, sems):
    started = [pltpu.make_async_copy(src, dst, sems.at[i]) for i, (src, dst) in enumerate(pairs)]
    for one in started:
        one.start()
    for one in started:
        one.wait()


def rows_at(start, size):
    return pl.ds(pl.multiple_of(start, 16), size)


def lanes_at(start, size):
    return pl.ds(pl.multiple_of(start, LANES), size)


def pack_weights(scalars, arrays, part, dims, place, after=(), down=False, scale=1, chunk=0):
    def kernel(s, *refs):
        srcs, out, sems = refs[: len(arrays)], refs[len(arrays)], refs[len(arrays) + 1]
        start = (s[place] * scale + chunk) * dims[0]
        pairs = []
        at = 0
        for src in srcs:
            if down:
                pairs.append((src.at[rows_at(s[START_FAR] + start, dims[0]), :], out))
            elif part is not None:
                pairs.append((src.at[rows_at(start, dims[0]), lanes_at(s[START_FAR], part)],
                              out.at[:, at:at + part]))
                at += part
            else:
                wide = src.shape[1]
                pairs.append((src.at[rows_at(start, dims[0]), :], out.at[:, at:at + wide]))
                at += wide
        copies(pairs, sems)

    return run(kernel, [(scalars, SCALARS)] + [(a, ANY) for a in arrays], [shape(dims, BF)],
               after=after, scratch=[pltpu.SemaphoreType.DMA((len(arrays),))], limit=48,
               estimate=cost(0, 4 * dims[0] * dims[1]), name="pack")[0]


QUARTERS = 5
HALVES = 2
CHUNKED = 4


def placed(s, fetched, at, total):
    if len(fetched) in (HALVES, CHUNKED):
        chunks = len(fetched) // 2
        size = total // 2
        step = size // chunks
        rows = [rows_at(at + half * size + i * step, step)
                for i in range(chunks) for half in (s[INNER], 1 - s[INNER])]
    else:
        size = total // 4
        rows = [rows_at(at + s[place] * size, size) for place in (OWN, PAIR, NEAR)]
        rows += [rows_at(at + s[ACROSS] * size + i * (size // 2), size // 2) for i in range(2)]
    return list(zip(fetched, rows))


def project(scalars, mine, other, gain, gain_far, w_query, w_key, w_value, fetched, bias, cosine,
            sine, after=()):
    length, width = mine.shape
    qw, kw = w_query.shape[1], w_key.shape[1]
    total = qw + 2 * kw

    def kernel(s, mine, other, gain, gain_far, wq, wk, wv, *refs):
        fetched, (bias, cosine, sine, q, k, v, a, r, w) = refs[:QUARTERS], refs[QUARTERS:]
        x = mine[...].astype(F32)
        y = other[...].astype(F32)
        squares = jnp.sum(x * x, axis=1, keepdims=True) + jnp.sum(y * y, axis=1, keepdims=True)
        rstd = lax.rsqrt(squares / D + EPS)
        r[...] = rstd

        @pl.when(s[SAME] == 1)
        def _():
            a[:, :width] = (x * rstd * gain[...]).astype(BF)
            a[:, width:] = (y * rstd * gain_far[...]).astype(BF)

        @pl.when(s[SAME] == 0)
        def _():
            a[:, :width] = (y * rstd * gain[...]).astype(BF)
            a[:, width:] = (x * rstd * gain_far[...]).astype(BF)

        w[:width, :qw] = wq[...]
        w[:width, qw:qw + kw] = wk[...]
        w[:width, qw + kw:] = wv[...]
        for piece, rows in placed(s, fetched, width, width):
            w[rows, :] = piece[...]
        out = dot(a[...], w[...]) + bias[...]
        c, t = cosine[...], sine[...]
        for head in range(qw // HD):
            u = out[:, head * HD:(head + 1) * HD]
            q[:, head * HD:(head + 1) * HD] = (u * c + pltpu.roll(u, HD // 2, 1) * t).astype(BF)
        for head in range(kw // HD):
            u = out[:, qw + head * HD:qw + (head + 1) * HD]
            k[:, head * HD:(head + 1) * HD] = (u * c + pltpu.roll(u, HD // 2, 1) * t).astype(BF)
        v[...] = out[:, qw + kw:].astype(BF)

    arrays = [mine, other, gain, gain_far, w_query, w_key, w_value, *fetched, bias, cosine, sine]
    return run(kernel, [(scalars, SCALARS)] + [(a, WHOLE) for a in arrays],
               [shape((length, qw), BF), shape((length, kw), BF), shape((length, kw), BF),
                shape((length, 2 * width), BF), shape((length, 1), F32)], after=after,
               scratch=[pltpu.VMEM((2 * width, total), BF)],
               estimate=cost(2 * length * 2 * width * total, 12 * MIB), name="qkv")


def allowed_keys(seg_col, seg_row, start, size, keys):
    rows = lax.broadcasted_iota(jnp.int32, (size, keys), 0) + start
    cols = lax.broadcasted_iota(jnp.int32, (size, keys), 1)
    return (seg_col[start:start + size, :] == seg_row[:, :keys]) & (cols <= rows)


def attend(scalars, q, k, v, seg_col, seg_row, w_out, fetched, after=()):
    length, qw = q.shape
    heads, pairs = qw // HD, k.shape[1] // HD
    width = w_out.shape[1]

    def kernel(s, q, k, v, seg_col, seg_row, w_out, *refs):
        fetched, (o, lse, part, w) = refs[:QUARTERS], refs[QUARTERS:]
        for start in range(0, length, TILE):
            keys = start + TILE
            allowed = allowed_keys(seg_col, seg_row, start, TILE, keys)
            rows = slice(start, start + TILE)
            for head in range(heads):
                pair = head // (heads // pairs)
                place = slice(head * HD, (head + 1) * HD)
                mine = slice(pair * HD, (pair + 1) * HD)
                scores = dot_right(q[rows, place], k[:keys, mine]) * HD ** (-0.5)
                scores = jnp.where(allowed, scores, -1e30)
                top = jnp.max(scores, axis=1, keepdims=True)
                raised = jnp.exp(scores - top)
                total = jnp.sum(raised, axis=1, keepdims=True)
                weights = (raised * (1.0 / total)).astype(BF)
                o[rows, place] = dot(weights, v[:keys, mine]).astype(BF)
                lse[rows, head:head + 1] = top + jnp.log(total)
        w[:, :width] = w_out[...]
        for piece, rows in placed(s, fetched, 0, qw):
            w[rows, width:] = piece[...]
        value = dot(o[...], w[...]).astype(BF)
        part[0] = value
        part[1] = value

    arrays = [q, k, v, seg_col, seg_row, w_out, *fetched]
    return run(kernel, [(scalars, SCALARS)] + [(a, WHOLE) for a in arrays],
               [shape((length, qw), BF), shape((length, LANES), F32), shape((2, length, 2 * width), BF)],
               after=after,
               scratch=[pltpu.VMEM((qw, 2 * width), BF)],
               estimate=cost(4 * length * length * qw + 2 * length * qw * 2 * width, 12 * MIB,
                             heads * length * length), name="attention")


def tiled(array, tile):
    return array, pl.BlockSpec((tile, array.shape[1]), lambda i: (i, 0))


def both_tiled(array, tile):
    return array, pl.BlockSpec((2, tile, array.shape[2]), lambda i: (0, i, 0))


def fixed(array):
    return array, pl.BlockSpec(array.shape, lambda i: (0, 0))


def norm_two(scalars, mine, other, parts, gain, gain_far, after=()):
    length, width = mine.shape

    def kernel(s, mine, other, parts, gain, gain_far, h, near, far, r):
        added = parts[0].astype(F32) + parts[1].astype(F32)

        def fill(first, second):
            h[:, :width] = first[...].astype(F32) + added[:, :width]
            h[:, width:] = second[...].astype(F32) + added[:, width:]

        pl.when(s[SAME] == 1)(lambda: fill(mine, other))
        pl.when(s[SAME] == 0)(lambda: fill(other, mine))
        rstd = lax.rsqrt(jnp.sum(h[...] * h[...], axis=1, keepdims=True) / D + EPS)
        r[...] = rstd
        first = (h[:, :width] * rstd * gain[...]).astype(BF)
        second = (h[:, width:] * rstd * gain_far[...]).astype(BF)

        @pl.when(s[SAME] == 1)
        def _():
            near[...] = first
            far[...] = second

        @pl.when(s[SAME] == 0)
        def _():
            near[...] = second
            far[...] = first

    tile = TILE // 2
    outs = [shape((length, 2 * width), F32), shape((length, width), BF), shape((length, width), BF),
            shape((length, 1), F32)]
    return run(kernel, [(scalars, SCALARS)] + [tiled(mine, tile), tiled(other, tile), both_tiled(parts, tile)]
               + [fixed(gain), fixed(gain_far)], outs, after=after, grid=(length // tile,),
               out_specs=[tiled(o, tile)[1] for o in outs],
               estimate=cost(length * width * 20, 16 * MIB), name="norm_two")


def gate_up(scalars, pieces, w_gate, w_up, fetched, first, total, part, kept=None, after=(), share=1):
    width = pieces[0][0].shape[-1]
    counts = [piece[0].shape[-2] // WIDE_TILE for piece in pieces]
    steps = sum(counts)
    offset = first // WIDE_TILE
    starts = [sum(counts[:i]) for i in range(len(counts))]

    def kernel(s, *refs):
        halves, refs = refs[:given], refs[given:]
        wg, wu, *fetched = refs[:2 + CHUNKED]
        b, z, up_slope, gate_slope, w, sems = refs[-6:]
        step = pl.program_id(0)

        @pl.when(step == 0)
        def _():
            load_gate_up(s, wg, wu, fetched, w, sems, part, width)

        def fill(*piece):
            if len(piece) == 1:
                near, far, straight = piece[0].at[0], piece[0].at[1], s[ROW] == 0
            else:
                near, far, straight = *piece, s[SAME] == 1

            @pl.when(straight)
            def _():
                b[:, :width] = near[...]
                b[:, width:] = far[...]

            @pl.when(jnp.logical_not(straight))
            def _():
                b[:, :width] = far[...]
                b[:, width:] = near[...]

        at = 0
        for piece, start, count in zip(pieces, starts, counts):
            pl.when((step >= start) & (step < start + count))(
                functools.partial(fill, *halves[at:at + len(piece)])
            )
            at += len(piece)

        both = dot(b[...], w[...])
        gate, upward = both[:, :part], both[:, part:]
        counted = lax.broadcasted_iota(jnp.int32, gate.shape, 1) >= s[SKIP]
        sigma = 1.0 / (1.0 + jnp.exp(-gate))
        sigma = jnp.where(counted, sigma, 0.0)
        silu = gate * sigma
        z[...] = (silu * upward).astype(BF)
        up_slope[...] = silu.astype(BF)
        gate_slope[...] = (upward * sigma * (1.0 + gate * (1.0 - sigma))).astype(BF)

    def block(array, start, count):
        if len(array.shape) == 3:
            return pl.BlockSpec((2, WIDE_TILE, width), lambda i: (0, jnp.clip(i - start, 0, count - 1), 0))
        return pl.BlockSpec((WIDE_TILE, width), lambda i: (jnp.clip(i - start, 0, count - 1), 0))

    ins = [(scalars, SCALARS)]
    for piece, start, count in zip(pieces, starts, counts):
        ins += [(array, block(array, start, count)) for array in piece]
    given = len(ins) - 1
    ins += [(array, ANY) for array in (w_gate, w_up, *fetched)]
    aliases = {}
    if kept is not None:
        aliases = {len(ins) + i: i for i in range(4)}
        ins += [(array, ANY) for array in kept]
    at = lambda i: (i + offset, 0)
    length = steps * WIDE_TILE
    return run(kernel, ins,
               [shape((total, 2 * width), BF)] + [shape((total, part), BF)] * 3,
               after=after, grid=(steps,),
               out_specs=[pl.BlockSpec((WIDE_TILE, 2 * width), at)]
               + [pl.BlockSpec((WIDE_TILE, part), at)] * 3,
               scratch=[pltpu.VMEM((2 * width, 2 * part), BF), pltpu.SemaphoreType.DMA((2 + CHUNKED,))],
               aliases=aliases,
               estimate=cost(share * 8 * length * width * part, share * 12 * MIB, share * length * part),
               name="gate_up")


def load_gate_up(s, wg, wu, fetched, w, sems, part, width):
    lanes = lanes_at(s[START], part)
    copies([(wg.at[:, lanes], w.at[:width, :part]), (wu.at[:, lanes], w.at[:width, part:])]
           + [(piece, w.at[rows, :]) for piece, rows in placed(s, fetched, width, width)], sems)


def place_rows(scalars, pieces, after=()):
    length, width = pieces[0][0].shape
    flat = [array for piece in pieces for array in piece[:2]]

    def kernel(s, *refs):
        srcs, out, sems = refs[:len(flat)], refs[len(flat)], refs[len(flat) + 1]
        pairs = []
        for i, src in enumerate(srcs):
            _, _, group, side = pieces[i // 2]
            place = jnp.where(s[SAME] == 1, i % 2, 1 - i % 2) * length
            pairs.append((src, out.at[rows_at(2 * group * length + place, length),
                                      side * width:(side + 1) * width]))
        copies(pairs, sems)

    return run(kernel, [(scalars, SCALARS)] + [(a, ANY) for a in flat],
               [shape((4 * length, 2 * width), BF)], after=after,
               scratch=[pltpu.SemaphoreType.DMA((len(flat),))], limit=48,
               estimate=cost(0, 16 * len(flat) * length * width // 4), name="place_rows")[0]


def place_last(scalars, both, rows, after=()):
    _, length, width = both.shape

    def kernel(s, both, _, out, buffer, sems):
        copies([(both.at[i], buffer.at[i]) for i in range(2)], sems)
        copies([(buffer.at[i], out.at[rows_at(2 * length + jnp.where(s[ROW] == i, 0, length), length),
                                      width:]) for i in range(2)], sems)

    return run(kernel, [(scalars, SCALARS), (both, ANY), (rows, ANY)], [shape(rows.shape, BF)], after=after,
               out_specs=[ANY], aliases={2: 0},
               scratch=[pltpu.VMEM(both.shape, BF), pltpu.SemaphoreType.DMA((2,))], limit=48,
               estimate=cost(0, 8 * length * width), name="place_last")[0]


def copy_of(array, after):
    def kernel(src, out, sem):
        copies([(src, out)], sem)

    return run(kernel, [(array, ANY)], [shape(array.shape, array.dtype)], after=after,
               scratch=[pltpu.SemaphoreType.DMA((1,))], limit=48,
               estimate=cost(0, 4 * array.size), name="copy_of")[0]


def hold(array, *after):
    def kernel(src, out):
        pass

    return run(kernel, [(array, ANY)], [shape(array.shape, array.dtype)], after=after, out_specs=[ANY],
               aliases={0: 0}, limit=48, estimate=cost(0, 0), name="hold")[0]


def load_down(s, w_down, fetched, w, sems, part, width):
    copies([(w_down.at[rows_at(s[START], part), :], w.at[:, :width])]
           + [(piece, w.at[rows, width:]) for piece, rows in placed(s, fetched, 0, part)], sems)


def hidden_back(scalars, cot, up_slope, gate_slope, w_down, fetched, after=()):
    total, width = cot.shape[0], cot.shape[1] // 2
    part = up_slope.shape[1]

    def kernel(s, g, up_slope, gate_slope, w_down, *refs):
        fetched, (out, w, sems) = refs[:HALVES], refs[HALVES:]

        @pl.when(pl.program_id(0) == 0)
        def _():
            load_down(s, w_down, fetched, w, sems, part, width)

        back = dot_right(g[...], w[...])
        out[:, :part] = (back * gate_slope[...].astype(F32)).astype(BF)
        out[:, part:] = (back * up_slope[...].astype(F32)).astype(BF)

    at = lambda i: (i, 0)
    tile = 2 * TILE
    return run(kernel,
               [(scalars, SCALARS), (cot, pl.BlockSpec((tile, 2 * width), at)),
                (up_slope, pl.BlockSpec((tile, part), at)), (gate_slope, pl.BlockSpec((tile, part), at)),
                (w_down, ANY)] + [(piece, ANY) for piece in fetched],
               [shape((total, 2 * part), BF)], after=after, grid=(total // tile,),
               out_specs=[pl.BlockSpec((tile, 2 * part), at)],
               scratch=[pltpu.VMEM((part, 2 * width), BF), pltpu.SemaphoreType.DMA((1 + HALVES,))],
               estimate=cost(4 * total * width * part, total * 14000), name="hidden_back")[0]


def split_store(s, value, keep, send, width):
    first, second = value[:, :width].astype(BF), value[:, width:].astype(BF)

    @pl.when(s[SAME] == 1)
    def _():
        keep[...] = first
        send[...] = second

    @pl.when(s[SAME] == 0)
    def _():
        keep[...] = second
        send[...] = first


def norm_back(scalars, low, w_gate, w_up, fetched, first, length, after=(), stacked=False):
    width = w_gate.shape[0]
    part = low.shape[1] // 2
    offset = first // WIDE_TILE

    def kernel(s, low, wg, wu, *refs):
        fetched, (*outs, w, sems) = refs[:CHUNKED], refs[CHUNKED:]

        @pl.when(pl.program_id(0) == 0)
        def _():
            load_gate_up(s, wg, wu, fetched, w, sems, part, width)

        value = dot_right(low[...], w[...])
        if stacked:
            outs[0][s[ROW]] = value[:, :width].astype(BF)
            outs[0][1 - s[ROW]] = value[:, width:].astype(BF)
        else:
            split_store(s, value, *outs, width)

    tiles = [pl.BlockSpec((WIDE_TILE, width), lambda i: (i, 0))] * 2
    outs = [shape((length, width), BF)] * 2
    if stacked:
        outs = [shape((2, length, width), BF)]
        tiles = [pl.BlockSpec((2, WIDE_TILE, width), lambda i: (0, i, 0))]
    return run(kernel,
               [(scalars, SCALARS), (low, pl.BlockSpec((WIDE_TILE, 2 * part), lambda i: (i + offset, 0))),
                (w_gate, ANY), (w_up, ANY)] + [(piece, ANY) for piece in fetched],
               outs, after=after, grid=(length // WIDE_TILE,), out_specs=tiles,
               scratch=[pltpu.VMEM((2 * width, 2 * part), BF), pltpu.SemaphoreType.DMA((2 + CHUNKED,))],
               estimate=cost(8 * length * width * part, 8 * MIB + length * 8000), name="norm_back")


def down_project(scalars, hidden, w_down, fetched, after=()):
    total, part = hidden.shape
    width = w_down.shape[1]

    def kernel(s, z, w_down, *refs):
        fetched, (keep, send, w, sems) = refs[:HALVES], refs[HALVES:]

        @pl.when(pl.program_id(0) == 0)
        def _():
            load_down(s, w_down, fetched, w, sems, part, width)

        split_store(s, dot(z[...], w[...]), keep, send, width)

    at = lambda i: (i, 0)
    tile = 2 * TILE
    return run(kernel,
               [(scalars, SCALARS), (hidden, pl.BlockSpec((tile, part), at)), (w_down, ANY)]
               + [(piece, ANY) for piece in fetched],
               [shape((total, width), BF)] * 2, after=after, grid=(total // tile,),
               out_specs=[pl.BlockSpec((tile, width), at)] * 2,
               scratch=[pltpu.VMEM((part, 2 * width), BF), pltpu.SemaphoreType.DMA((1 + HALVES,))],
               estimate=cost(4 * total * width * part, total * 8000), name="down_project")


def weight_grad(scalars, left, right, piece, columns, place=0, after=()):
    tokens, width = left.shape[0], left.shape[1] // 2
    groups = width // (2 * piece)

    def kernel(s, left, right, keep, send):
        value = dot_left(left[...], right[...]).astype(BF).reshape(groups, 2, piece, columns)

        @pl.when(s[INNER] == 0)
        def _():
            keep[0] = value[:, 0]
            send[0] = value[:, 1]

        @pl.when(s[INNER] == 1)
        def _():
            keep[0] = value[:, 1]
            send[0] = value[:, 0]

    block = pl.BlockSpec((1, groups, piece, columns), lambda i: (i, 0, 0, 0))
    return run(kernel,
               [(scalars, SCALARS), (left, pl.BlockSpec((tokens, width), lambda i: (0, i))),
                (right, pl.BlockSpec((tokens, columns), lambda i: (0, place)))],
               [shape((2, groups, piece, columns), BF)] * 2, after=after, grid=(2,),
               out_specs=[block, block],
               estimate=cost(4 * tokens * width * columns, tokens * (4 * width + 4 * columns)),
               name="weight_grad")


def small_grad(left, right, after=()):
    tokens, width = left.shape[0], left.shape[1] // 2
    columns = right.shape[1]

    def kernel(left, right, keep, send):
        send[...] = dot_left(left[:, width:], right[...]).astype(BF)
        keep[...] = dot_left(left[:, :width], right[...]).astype(BF)

    return run(kernel, [(left, WHOLE), (right, WHOLE)], [shape((width, columns), BF)] * 2, after=after,
               estimate=cost(4 * tokens * width * columns, 8 * MIB), name="small_grad")


def middle_back(scalars, both, h, r, gain, gain_far, cot, after=()):
    _, length, width = both.shape

    def kernel(s, both, h, r, gain, gain_far, g, dh, low, gain_part, db):
        def fill(first, second):
            db[:, :width] = first.astype(F32)
            db[:, width:] = second.astype(F32)

        pl.when(s[ROW] == 0)(lambda: fill(both[0], both[1]))
        pl.when(s[ROW] == 1)(lambda: fill(both[1], both[0]))
        rstd = r[...]
        normed = h[...] * rstd
        gains = jnp.concatenate([gain[...], gain_far[...]], axis=1)

        @pl.when(pl.program_id(0) == 0)
        def _():
            gain_part[...] = jnp.zeros_like(gain_part)

        gain_part[...] += jnp.sum(db[...] * normed, axis=0, keepdims=True)
        scaled = db[...] * gains
        mean = jnp.sum(scaled * normed, axis=1, keepdims=True) / D
        value = g[...].astype(F32) + rstd * (scaled - normed * mean)
        low[...] = value.astype(BF)
        pl.when(s[SAME] == 1)(lambda: dh.__setitem__(..., value[:, :width]))
        pl.when(s[SAME] == 0)(lambda: dh.__setitem__(..., value[:, width:]))

    tile = TILE // 2
    outs = [shape((length, width), F32), shape((length, 2 * width), BF), shape((1, 2 * width), F32)]
    return run(kernel, [(scalars, SCALARS)] + [both_tiled(both, tile), tiled(h, tile), tiled(r, tile)]
               + [fixed(gain), fixed(gain_far), tiled(cot, tile)], outs, after=after,
               grid=(length // tile,),
               out_specs=[tiled(o, tile)[1] for o in outs[:2]] + [fixed(outs[2])[1]],
               scratch=[pltpu.VMEM((tile, 2 * width), F32)],
               estimate=cost(length * width * 30, 20 * MIB), name="middle_back")


def attend_back(scalars, low, q, k, v, lse, seg_col, seg_row, w_out, out_fetched, w_query, w_key, w_value,
                qkv_fetched, cosine, sine, after=()):
    length, qw = q.shape
    kw = k.shape[1]
    heads, pairs = qw // HD, kw // HD
    width = w_out.shape[1]
    total = qw + 2 * kw

    def kernel(s, low, q, k, v, lse, seg_col, seg_row, w_out, *refs):
        out_fetched, (wq, wk, wv), refs = refs[:QUARTERS], refs[QUARTERS:QUARTERS + 3], refs[QUARTERS + 3:]
        fetched, (cosine, sine, back, bias, part, wo, w, do, dk, dv) = refs[:QUARTERS], refs[QUARTERS:]
        wo[:, :width] = w_out[...]
        for piece, rows in placed(s, out_fetched, 0, qw):
            wo[rows, width:] = piece[...]
        do[...] = dot_right(low[...], wo[...]).astype(BF)
        dk[...] = jnp.zeros_like(dk)
        dv[...] = jnp.zeros_like(dv)
        for start in range(0, length, TILE):
            keys = start + TILE
            allowed = allowed_keys(seg_col, seg_row, start, TILE, keys)
            rows = slice(start, start + TILE)
            c, t = cosine[rows, :], sine[rows, :]
            for head in range(heads):
                pair = head // (heads // pairs)
                place = slice(head * HD, (head + 1) * HD)
                mine = slice(pair * HD, (pair + 1) * HD)
                scores = dot_right(q[rows, place], k[:keys, mine]) * HD ** (-0.5)
                probs = jnp.where(allowed, jnp.exp(scores - lse[rows, head:head + 1]), 0.0)
                grads = dot_right(do[rows, place], v[:keys, mine])
                delta = jnp.sum(probs * grads, axis=1, keepdims=True)
                score_grad = (probs * (grads - delta)).astype(BF)
                dv[:keys, mine] += dot_left(probs.astype(BF), do[rows, place])
                dk[:keys, mine] += dot_left(score_grad, q[rows, place])
                u = dot(score_grad, k[:keys, mine]) * HD ** (-0.5)
                back[rows, place] = (u * c - pltpu.roll(u, HD // 2, 1) * t).astype(BF)
        for pair in range(pairs):
            u = dk[:, pair * HD:(pair + 1) * HD] * HD ** (-0.5)
            u = u * cosine[...] - pltpu.roll(u, HD // 2, 1) * sine[...]
            back[:, qw + pair * HD:qw + (pair + 1) * HD] = u.astype(BF)
        back[:, qw + kw:] = dv[...].astype(BF)
        w[:width, :qw] = wq[...]
        w[:width, qw:qw + kw] = wk[...]
        w[:width, qw + kw:] = wv[...]
        for piece, rows in placed(s, fetched, width, width):
            w[rows, :] = piece[...]
        value = dot_right(back[...], w[...]).astype(BF)
        part[0] = value
        part[1] = value
        bias[...] = jnp.sum(back[...].astype(F32), axis=0, keepdims=True)

    arrays = [low, q, k, v, lse, seg_col, seg_row, w_out, *out_fetched, w_query, w_key, w_value,
              *qkv_fetched, cosine, sine]
    return run(kernel, [(scalars, SCALARS)] + [(a, WHOLE) for a in arrays],
               [shape((length, total), BF), shape((1, total), F32), shape((2, length, 2 * width), BF)],
               after=after,
               scratch=[pltpu.VMEM((qw, 2 * width), BF), pltpu.VMEM((2 * width, total), BF),
                        pltpu.VMEM((length, qw), BF), pltpu.VMEM((length, kw), F32),
                        pltpu.VMEM((length, kw), F32)],
               estimate=cost(10 * length * length * qw + 2 * length * 2 * width * (qw + total), 20 * MIB,
                             heads * length * length), name="attention_back")


def input_back(scalars, parts, mine, other, r, gain, gain_far, dh, after=()):
    length, width = mine.shape

    def kernel(s, parts, mine, other, r, dh, gain, gain_far, out, gain_part, n):
        def fill(first, second):
            n[:, :width] = first[...].astype(F32) * r[...]
            n[:, width:] = second[...].astype(F32) * r[...]

        pl.when(s[SAME] == 1)(lambda: fill(mine, other))
        pl.when(s[SAME] == 0)(lambda: fill(other, mine))
        da = parts[0].astype(F32) + parts[1].astype(F32)
        normed = n[...]

        @pl.when(pl.program_id(0) == 0)
        def _():
            gain_part[...] = jnp.zeros_like(gain_part)

        gain_part[...] += jnp.sum(da * normed, axis=0, keepdims=True)
        scaled = da * jnp.concatenate([gain[...], gain_far[...]], axis=1)
        mean = jnp.sum(scaled * normed, axis=1, keepdims=True) / D

        def put(half):
            out[...] = (dh[...] + r[...] * (scaled[:, half] - normed[:, half] * mean)).astype(BF)

        pl.when(s[SAME] == 1)(lambda: put(slice(0, width)))
        pl.when(s[SAME] == 0)(lambda: put(slice(width, 2 * width)))

    tile = TILE // 2
    outs = [shape((length, width), BF), shape((1, 2 * width), F32)]
    return run(kernel, [(scalars, SCALARS)] + [both_tiled(parts, tile)] + [tiled(a, tile) for a in (mine, other, r, dh)]
               + [fixed(gain), fixed(gain_far)], outs, after=after, grid=(length // tile,),
               out_specs=[tiled(outs[0], tile)[1], fixed(outs[1])[1]],
               scratch=[pltpu.VMEM((tile, 2 * width), F32)],
               estimate=cost(length * width * 30, 16 * MIB), name="input_back")


def halve(scalars, keep, recv, bit, after=()):
    parts, many, _, rows, columns = keep.shape

    def kernel(s, keep, recv, kept, sent):
        total = (keep[0, 0].astype(F32) + recv[0, 0].astype(F32)).astype(BF)

        @pl.when(s[BITS + bit] == 0)
        def _():
            kept[0, 0] = total[0]
            sent[0, 0] = total[1]

        @pl.when(s[BITS + bit] == 1)
        def _():
            kept[0, 0] = total[1]
            sent[0, 0] = total[0]

    wide = pl.BlockSpec((1, 1, 2, rows, columns), lambda i, j: (i, j, 0, 0, 0))
    narrow = pl.BlockSpec((1, 1, rows, columns), lambda i, j: (i, j, 0, 0))
    return run(kernel, [(scalars, SCALARS), (keep, wide), (recv, wide)],
               [shape((parts, many, rows, columns), BF)] * 2, after=after, grid=(parts, many),
               out_specs=[narrow] * 2, estimate=cost(GLUE), name="halve")


def sum_rows(keep, recv, after=()):
    _, pieces, rows, columns = keep.shape

    def kernel(keep, recv, near, sent):
        near[0] = (keep[0, 0].astype(F32) + recv[0, 0].astype(F32)).astype(BF)
        sent[0] = (keep[1, 0].astype(F32) + recv[1, 0].astype(F32)).astype(BF)

    wide = pl.BlockSpec((2, 1, rows, columns), lambda i: (0, i, 0, 0))
    narrow = pl.BlockSpec((1, rows, columns), lambda i: (i, 0, 0))
    return run(kernel, [(keep, wide), (recv, wide)], [shape((pieces, rows, columns), BF)] * 2, after=after,
               grid=(pieces,), out_specs=[narrow] * 2, estimate=cost(GLUE),
               name="sum_rows")


def deal_near(scalars, near, far, after=()):
    def kernel(s, near, far, own, sent):
        for bit, out in ((s[BITS + 1], own), (1 - s[BITS + 1], sent)):
            out[s[ROW]] = near[bit]
            out[1 - s[ROW]] = far[bit]

    return run(kernel, [(scalars, SCALARS), (near, WHOLE), (far, WHOLE)], [shape(near.shape, BF)] * 2,
               after=after, estimate=cost(GLUE), name="deal_near")


def lay_columns(scalars, own, across, overlap, after=()):
    _, rows, part = own.shape
    total = PARTS * part - overlap

    def kernel(s, own, across, out):
        def fill(first, second):
            for i, piece in enumerate((first[0], first[1], second[0])):
                out[:, i * part:(i + 1) * part] = piece.astype(F32)
            out[:, 3 * part:] = second[1][:, overlap:].astype(F32)

        pl.when(s[BITS + 1] == 0)(lambda: fill(own, across))
        pl.when(s[BITS + 1] == 1)(lambda: fill(across, own))

    return run(kernel, [(scalars, SCALARS), (own, WHOLE), (across, WHOLE)], [shape((rows, total), F32)],
               after=after, estimate=cost(GLUE), name="lay_columns")[0]


def sum_plain(keep, recv, after=()):
    def kernel(keep, recv, out):
        out[...] = keep[...].astype(F32) + recv[...].astype(F32)

    return run(kernel, [(keep, WHOLE), (recv, WHOLE)], [shape(keep.shape, F32)], after=after,
               estimate=cost(GLUE), name="sum_plain")[0]


def sum_split(keep, recv, widths, after=()):
    rows = keep.shape[1]

    def kernel(keep, recv, *outs):
        at = 0
        for out, width in zip(outs, widths):
            part = slice(at, at + width)
            out[...] = keep[0, :, part].astype(F32) + recv[0, :, part].astype(F32)
            at += width

    return run(kernel, [(keep, WHOLE), (recv, WHOLE)], [shape((rows, width), F32) for width in widths],
               after=after, estimate=cost(GLUE), name="sum_split")


def sum_far(keep, send, first, after=()):
    width = keep.shape[1]
    half = width // 2
    offset = first // half

    def kernel(keep, send, to_row, to_near):
        value = (keep[...].astype(F32) + send[...].astype(F32)).astype(BF)
        pl.when(pl.program_id(0) == 0)(lambda: to_row.__setitem__(..., value))
        pl.when(pl.program_id(0) == 1)(lambda: to_near.__setitem__(..., value))

    block = pl.BlockSpec((half, width), lambda i: (offset + i, 0))
    return run(kernel, [(keep, block), (send, block)], [shape((half, width), BF)] * 2, after=after, grid=(2,),
               out_specs=[pl.BlockSpec((half, width), lambda i: (0, 0))] * 2,
               estimate=cost(GLUE), name="sum_far")


def sum_near(keep, send, via_row, via_near, first, after=()):
    half, width = via_row.shape
    length = 2 * half
    offset = first // length

    def kernel(keep, send, via_row, via_near, to_row, to_near):
        step = pl.program_id(0)

        def put(out, plain, more, via):
            out[plain, :] = (keep[plain, :].astype(F32) + send[plain, :].astype(F32)).astype(BF)
            out[more, :] = (keep[more, :].astype(F32) + send[more, :].astype(F32)
                            + via[...].astype(F32)).astype(BF)

        low, high = slice(0, half), slice(half, length)
        pl.when(step == 0)(lambda: put(to_row, low, high, via_near))
        pl.when(step == 1)(lambda: put(to_near, high, low, via_row))

    block = pl.BlockSpec((length, width), lambda i: (offset + i, 0))
    whole = pl.BlockSpec((length, width), lambda i: (0, 0))
    return run(kernel, [(keep, block), (send, block), fixed(via_row), fixed(via_near)],
               [shape((length, width), BF)] * 2, after=after, grid=(2,), out_specs=[whole, whole],
               estimate=cost(GLUE), name="sum_near")


def sum_own(keep, send, via_row, via_near, after=()):
    length, width = via_row.shape

    def kernel(keep, send, via_row, via_near, out):
        value = (keep[...].astype(F32) + send[...].astype(F32)) + (
            via_row[...].astype(F32) + via_near[...].astype(F32))
        out[0] = value.astype(BF)
        out[1] = value.astype(BF)

    outs = [shape((2, length, width), BF)]
    return run(kernel, [tiled(a, TILE) for a in (keep, send, via_row, via_near)], outs, after=after,
               grid=(length // TILE,), out_specs=[both_tiled(outs[0], TILE)[1]],
               estimate=cost(GLUE), name="sum_own")[0]


def sum_output(scalars, keep, send, via_row, via_near, h, after=()):
    length, width = via_row.shape

    def kernel(s, keep, send, via_row, via_near, h, out):
        value = (keep[...].astype(F32) + send[...].astype(F32)) + (
            via_row[...].astype(F32) + via_near[...].astype(F32))
        pl.when(s[SAME] == 1)(lambda: out.__setitem__(..., (h[:, :width] + value).astype(BF)))
        pl.when(s[SAME] == 0)(lambda: out.__setitem__(..., (h[:, width:] + value).astype(BF)))

    outs = [shape((length, width), BF)]
    return run(kernel, [(scalars, SCALARS)] + [tiled(a, TILE) for a in (keep, send, via_row, via_near, h)],
               outs, after=after, grid=(length // TILE,), out_specs=[tiled(outs[0], TILE)[1]],
               estimate=cost(GLUE), name="sum_output")[0]


def body(
    inputs,
    segments,
    positions,
    w_query,
    w_key,
    w_value,
    b_query,
    b_key,
    b_value,
    w_out,
    gain_one,
    gain_two,
    w_gate,
    w_up,
    w_down,
    cotangent,
):
    length, width = inputs.shape
    query_width = w_query.shape[1]
    key_width = w_key.shape[1]
    total_width = query_width + 2 * key_width
    row = lax.axis_index("row")
    col = lax.axis_index("col")
    group = lax.axis_index("dp")
    groups = lax.axis_size("dp")
    inner = group % 2
    near_bit = (group // 2) % 2
    same = row == col

    hidden_here = w_gate.shape[1]
    blocks = hidden_here // LANES
    wide = -(-blocks // PARTS)
    part = wide * LANES
    overlap = PARTS * part - hidden_here

    def start_of(index):
        return jnp.minimum(index * wide, blocks - wide) * LANES

    mine_part = near_bit * 2 + row
    place_of = lambda low, high: 2 * low + high
    scalars = jnp.stack(
        [same.astype(jnp.int32), inner, start_of(mine_part), start_of(near_bit * 2 + 1 - row),
         jnp.where(mine_part == PARTS - 1, overlap, 0), place_of(inner, near_bit),
         place_of(1 - inner, near_bit), place_of(inner, 1 - near_bit), place_of(1 - inner, 1 - near_bit), row]
        + [(group >> bit) % 2 for bit in range(groups.bit_length() - 1)]
    ).astype(jnp.int32)

    def by_row(mine, other):
        return jnp.where(same, mine, other), jnp.where(same, other, mine)

    LAST.clear()
    half = width // 2
    gains = jnp.stack([gain_one, gain_two])
    fetched_gains = swap_row(gains)
    mine = turn_square(inputs)
    other = swap_col(mine)
    def pack_gate_up(chunk):
        return swap_row(pack_weights(
            scalars, [w_gate, w_up], part, (width // 4, 2 * part), INNER, scale=2, chunk=chunk
        ))

    def relay(direct):
        pair, near = swap_bit(direct, 0), swap_bit(direct, 1)
        cut = direct.shape[0] // 2
        return direct, pair, near, swap_bit(pair[:cut], 1), swap_bit(near[cut:], 0)

    qkv_fetched = relay(swap_row(
        pack_weights(scalars, [w_query, w_key, w_value], None, (width // 4, total_width), OWN)
    ))
    out_fetched = relay(swap_row(
        pack_weights(scalars, [w_out], None, (query_width // 4, width), OWN)
    ))
    fetched_gains = hold(fetched_gains).astype(F32)
    gains = gains.astype(F32)
    gu_direct = [pack_gate_up(0), pack_gate_up(1)]
    gu_first = hold(gu_direct[0])
    gu_fetched = [gu_first, swap_bit(gu_first, 0)]

    indices = jnp.arange(HD // 2, dtype=F32)
    inverse = jnp.exp(indices * (-2.0 / HD) * jnp.log(F32(THETA)))
    turned = positions.astype(F32)[:, None] * inverse[None, :]
    cosine, sine = jnp.cos(turned), jnp.sin(turned)
    cosine = jnp.concatenate([cosine, cosine], axis=1)
    sine = jnp.concatenate([-sine, sine], axis=1)
    bias = jnp.concatenate([b_query, b_key, b_value]).astype(F32)[None, :]
    seg_col, seg_row = segments[:, None], segments[None, :]

    q, k, v, low_one, r_one = project(
        scalars, mine, other, gains[:1], fetched_gains[:1], w_query, w_key, w_value, qkv_fetched,
        bias, cosine, sine,
    )
    cot = copy_of(cotangent, [])
    cot_row = swap_row(cot)
    cot_near = swap_bit(cot, 1)
    attended, lse, out_part = attend(scalars, q, k, v, seg_col, seg_row, w_out, out_fetched)
    gu_second = hold(gu_direct[1])
    gu_fetched += [gu_second, swap_bit(gu_second, 0)]
    cot_other = swap_col(cot)
    gu_fetched[1] = hold(gu_fetched[1])
    cot_other = hold(cot_other)
    h, low_near, low_far, r_two = norm_two(
        scalars, mine, other, trade_col(out_part), gains[1:], fetched_gains[1:]
    )

    b_row = swap_row(low_near)
    b_near = swap_bit(low_near, 1)
    cot_row, cot_near = hold(cot_row), hold(cot_near)
    cot_row_other, cot_near_other = swap_col(cot_row), swap_col(cot_near)
    tokens = 4 * length
    ffn = functools.partial(
        gate_up, scalars, w_gate=w_gate, w_up=w_up, fetched=gu_fetched, total=tokens, part=part,
    )
    kept = ffn([(low_near, low_far)], first=0)
    cot_row_other, cot_near_other = hold(cot_row_other), hold(cot_near_other)
    cot_low = swap_bit(hold(cot_row[:half]), 1)
    placed_cot = place_rows(scalars, [(cot, cot_other, 0, 0), (cot_row, cot_row_other, 0, 1),
                                      (cot_near, cot_near_other, 1, 0)])
    b_row = hold(b_row)
    b_row_other = swap_col(b_row)
    b_low = swap_bit(b_row[:half], 1)
    b_near = hold(b_near)
    b_near_other = swap_col(b_near)
    b_high = swap_row(b_near[half:])
    b_row_other, b_near_other = hold(b_row_other), hold(b_near_other)
    cot_high = swap_row(hold(cot_near[half:]))
    sent_down = pack_weights(scalars, [w_down], None, (part // 2, width), INNER, down=True)
    down_direct = swap_row(sent_down)
    kept = ffn([(b_row, b_row_other), (b_near, b_near_other)], first=length, kept=kept)
    b_far = jnp.concatenate([hold(b_low), hold(b_high)], axis=0)
    b_far = trade_col(jnp.stack([b_far, b_far]))
    kept = ffn([(b_far,)], first=3 * length, kept=kept, after=[sent_down], share=0)
    full_two, hidden, up_slope, gate_slope = kept
    cot_far = jnp.concatenate([hold(cot_low), hold(cot_high)], axis=0)
    cot_far = trade_col(jnp.stack([cot_far, cot_far]))
    down_direct = hold(down_direct)
    down_fetched = down_direct, swap_bit(down_direct, 0)
    full_cot = place_last(scalars, cot_far, placed_cot)

    piece = width // groups
    down_keep, down_send = weight_grad(scalars, full_cot, hidden, piece, part)
    down_recv = swap_bit(down_send, 0)
    low_back = hidden_back(scalars, full_cot, up_slope, gate_slope, w_down, down_fetched)
    back = functools.partial(
        norm_back, scalars, low_back, w_gate, w_up, gu_fetched
    )
    high_bits = range(2, groups.bit_length() - 1)

    def grad_high(keep, recv):
        for bit in high_bits:
            cut = (2, keep.size // (4 * 2 * piece * part), 2, 2 * piece, part)
            keep, send = halve(scalars, keep.reshape(cut), recv.reshape(cut), bit)
            recv = swap_bit(send, bit)
        return keep, recv

    def grad_row(keep, recv):
        cut = (2, 2, piece, part)
        near, send = sum_rows(keep.reshape(cut), recv.reshape(cut))
        return near, swap_row(send)

    def grad_near(near, far):
        own, send = deal_near(scalars, near, far)
        return own, swap_bit(send, 1)

    def square_first(left, right):
        keep, send = weight_grad(scalars, left, right, piece, right.shape[1])
        return keep, swap_bit(send, 0)

    def square_next(keep, recv, bit):
        cut = (2, groups >> (bit + 1), 2, piece, keep.shape[-1])
        keep, send = halve(scalars, keep.reshape(cut), recv.reshape(cut), bit)
        return keep, swap_bit(send, bit)

    def square_row(keep, recv):
        near, send = sum_rows(keep, recv)
        return near, swap_row(send)

    def square_last(near, far):
        return sum_plain(near, far).reshape(piece, -1)

    last_bits = range(2, groups.bit_length() - 1)

    far_both = trade_col(back(3 * length, length, stacked=True)[0])
    across = (far_both[0].astype(F32) + far_both[1].astype(F32)).astype(BF)
    to_row, to_near = across[:half], across[half:]
    down = grad_high(down_keep, down_recv)
    rest_keep, rest_send = back(0, 3 * length, after=[to_row, to_near])
    via_row, via_near = swap_row(to_row), swap_bit(to_near, 1)
    gate_keep, gate_send = weight_grad(scalars, full_two, low_back, piece, part, 0)
    gate_recv = swap_bit(gate_send, 0)
    rest_got = swap_col(rest_send)
    to_row, to_near = sum_near(rest_keep, rest_got, via_row, via_near, length)
    via_row, via_near = swap_row(to_row), swap_bit(to_near, 1)

    down = down[0], hold(down[1])
    out_keep, out_send = down_project(scalars, hidden, w_down, down_fetched)
    out_got = swap_col(out_send)
    up_keep, up_send = weight_grad(scalars, full_two, low_back, piece, part, 1)
    up_recv = swap_bit(up_send, 0)
    normed_grad = sum_own(rest_keep, rest_got, via_row, via_near)
    first = 3 * length
    to_row, to_near = sum_far(out_keep, out_got, first)
    via_row, via_near = swap_row(to_row), swap_bit(to_near, 1)
    down = grad_row(*down)
    dh, low_mid, gain_two_part = middle_back(
        scalars, trade_col(normed_grad), h, r_two, gains[1:], fetched_gains[1:], full_cot,
    )
    gate = grad_high(gate_keep, gate_recv)
    down = down[0], hold(down[1])
    out_sum = square_first(low_mid, attended)
    to_row, to_near = sum_near(out_keep, out_got, via_row, via_near, length)
    via_row, via_near = swap_row(to_row), swap_bit(to_near, 1)
    up_recv = hold(up_recv)
    back_low, bias_part, in_part = attend_back(
        scalars, low_mid, q, k, v, lse, seg_col, seg_row, w_out, out_fetched, w_query, w_key,
        w_value, qkv_fetched, cosine, sine,
    )
    qkv_sum = square_first(low_one, back_low)
    via_row = hold(via_row)
    up = grad_high(up_keep, up_recv)
    via_near = hold(via_near)
    input_grad, gain_one_part = input_back(
        scalars, trade_col(in_part), mine, other, r_one, gains[:1], fetched_gains[:1], dh
    )
    input_grad = turn_square(input_grad)

    def canonical(value):
        first, second = value[:, :width], value[:, width:]
        return jnp.where(row == 0, value, jnp.concatenate([second, first], axis=1))[0]

    small = jnp.concatenate([bias_part[0], canonical(gain_one_part), canonical(gain_two_part)])

    def small_step(value, swap):
        return value + hold(swap(value))

    gate = grad_row(*gate)
    qkv_sum = square_next(*qkv_sum, 1)
    small = small_step(small, lambda value: swap_bit(value, 0))
    out_sum = square_next(*out_sum, 1)
    input_grad = hold(input_grad).astype(F32)
    output = turn_square(sum_output(scalars, out_keep, out_got, via_row, via_near, h))
    up = grad_row(*up)
    for bit in last_bits:
        qkv_sum = square_next(*qkv_sum, bit)
    gate = grad_near(*gate)
    down = grad_near(*down)
    output = hold(output)
    small = small_step(small, lambda value: swap_bit(value, 1))
    up = grad_near(*up)
    for bit in last_bits:
        out_sum = square_next(*out_sum, bit)
    qkv_sum = square_row(*qkv_sum)
    gate_grad = lay_columns(scalars, *gate, overlap)
    for bit in last_bits:
        small = small_step(small, lambda value, bit=bit: swap_bit(value, bit))
    qkv_grads = sum_split(*qkv_sum, (query_width, key_width, key_width))
    down_grad = lay_columns(scalars, *down, overlap).T
    out_sum = square_row(*out_sum)
    up_grad = lay_columns(scalars, *up, overlap)
    small = small_step(small, swap_row)
    out_grad = square_last(*out_sum).T
    gain_sums = pick(small[total_width:].reshape(2, 2, width), row, 1)

    return (
        output,
        input_grad,
        *qkv_grads,
        small[:query_width],
        small[query_width : query_width + key_width],
        small[query_width + key_width : total_width],
        out_grad,
        gain_sums[0],
        gain_sums[1],
        gate_grad,
        up_grad,
        down_grad,
    )


def solution(mesh):
    return jax.shard_map(
        body,
        mesh=mesh,
        in_specs=(
            P(("dp", "col"), "row"),
            P(("dp", "row")),
            P(("dp", "row")),
            P("row", "col"),
            P("row", "col"),
            P("row", "col"),
            P("col"),
            P("col"),
            P("col"),
            P("col", "row"),
            P("row"),
            P("row"),
            P("row", "col"),
            P("row", "col"),
            P("col", "row"),
            P(("dp", "col"), "row"),
        ),
        out_specs=(
            P(("dp", "col"), "row"),
            P(("dp", "col"), "row"),
            P(("row", "dp"), "col"),
            P(("row", "dp"), "col"),
            P(("row", "dp"), "col"),
            P("col"),
            P("col"),
            P("col"),
            P("col", ("row", "dp")),
            P("row"),
            P("row"),
            P(("row", "dp"), "col"),
            P(("row", "dp"), "col"),
            P("col", ("row", "dp")),
        ),
        check_vma=False,
    )
```

```python
import functools

import jax
import jax.numpy as jnp
from jax import lax
from jax.experimental import pallas as pl
from jax.experimental.pallas import tpu as pltpu
from jax.sharding import PartitionSpec as P

D = 1536
HQ = 12
KVH = 2
HD = 128
LANES = 128
PARTS = 4
TILE = 256
WIDE_TILE = 384
MIB = 1024 * 1024
SCALE = 10.0
GLUE = 1e9

EPS = 1e-06
THETA = 1000000.0
BF = jnp.bfloat16
F32 = jnp.float32

SAME, INNER, START, START_FAR, SKIP, OWN, PAIR, NEAR, ACROSS, ROW, BITS = range(11)


def swap_row(value):
    return lax.ppermute(value, "row", [(0, 1), (1, 0)])


def swap_col(value):
    return lax.ppermute(value, "col", [(0, 1), (1, 0)])


def swap_bit(value, bit):
    size = lax.axis_size("dp")
    return lax.ppermute(value, "dp", [(i, i ^ (1 << bit)) for i in range(size)])


def trade_col(value):
    return lax.all_to_all(value, "col", 0, 0)


def turn_square(value):
    return lax.ppermute(value, ("row", "col"), [(0, 0), (1, 2), (2, 1), (3, 3)])


def pick(array, index, axis=0):
    return lax.dynamic_index_in_dim(array, index, axis, keepdims=False)


ANY = pl.BlockSpec(memory_space=pl.ANY)
SCALARS = pl.BlockSpec(memory_space=pltpu.SMEM)
WHOLE = pl.BlockSpec(memory_space=pltpu.VMEM)


def shape(dims, dtype):
    return jax.ShapeDtypeStruct(dims, dtype)


def cost(flops, moved=0, exps=0):
    return pl.CostEstimate(
        flops=int(flops * SCALE), bytes_accessed=int(moved * SCALE), transcendentals=int(exps * SCALE)
    )


LAST = []


def run(kernel, ins, outs, after=(), grid=None, out_specs=None, scratch=(), limit=56, aliases=None,
        estimate=None, name=None):
    given = len(ins)
    count = len(outs)
    after = [*after, *LAST]

    def body(*refs):
        kernel(*refs[:given], *refs[given + len(after):])

    results = pl.pallas_call(
        body,
        grid=grid if grid is not None else (),
        in_specs=[spec for _, spec in ins] + [ANY] * len(after),
        out_specs=out_specs if out_specs is not None else [WHOLE] * count,
        out_shape=outs,
        scratch_shapes=list(scratch),
        input_output_aliases=aliases or {},
        cost_estimate=estimate,
        name=name,
        compiler_params=pltpu.CompilerParams(vmem_limit_bytes=limit * MIB),
    )(*[array for array, _ in ins], *after)
    LAST[:] = [results[-1]]
    return results


def dot(left, right):
    return jnp.dot(left, right, preferred_element_type=F32)


def dot_right(left, right):
    return lax.dot_general(left, right, (((1,), (1,)), ((), ())), preferred_element_type=F32)


def dot_left(left, right):
    return lax.dot_general(left, right, (((0,), (0,)), ((), ())), preferred_element_type=F32)


def copies(pairs, sems):
    started = [pltpu.make_async_copy(src, dst, sems.at[i]) for i, (src, dst) in enumerate(pairs)]
    for one in started:
        one.start()
    for one in started:
        one.wait()


def rows_at(start, size):
    return pl.ds(pl.multiple_of(start, 16), size)


def lanes_at(start, size):
    return pl.ds(pl.multiple_of(start, LANES), size)


def pack_weights(scalars, arrays, part, dims, place, after=(), down=False, scale=1, chunk=0):
    def kernel(s, *refs):
        srcs, out, sems = refs[: len(arrays)], refs[len(arrays)], refs[len(arrays) + 1]
        start = (s[place] * scale + chunk) * dims[0]
        pairs = []
        at = 0
        for src in srcs:
            if down:
                pairs.append((src.at[rows_at(s[START_FAR] + start, dims[0]), :], out))
            elif part is not None:
                pairs.append((src.at[rows_at(start, dims[0]), lanes_at(s[START_FAR], part)],
                              out.at[:, at:at + part]))
                at += part
            else:
                wide = src.shape[1]
                pairs.append((src.at[rows_at(start, dims[0]), :], out.at[:, at:at + wide]))
                at += wide
        copies(pairs, sems)

    return run(kernel, [(scalars, SCALARS)] + [(a, ANY) for a in arrays], [shape(dims, BF)],
               after=after, scratch=[pltpu.SemaphoreType.DMA((len(arrays),))], limit=48,
               estimate=cost(0, 4 * dims[0] * dims[1]), name="pack")[0]


QUARTERS = 5
HALVES = 2
CHUNKED = 4


def placed(s, fetched, at, total):
    if len(fetched) in (HALVES, CHUNKED):
        chunks = len(fetched) // 2
        size = total // 2
        step = size // chunks
        rows = [rows_at(at + half * size + i * step, step)
                for i in range(chunks) for half in (s[INNER], 1 - s[INNER])]
    else:
        size = total // 4
        rows = [rows_at(at + s[place] * size, size) for place in (OWN, PAIR, NEAR)]
        rows += [rows_at(at + s[ACROSS] * size + i * (size // 2), size // 2) for i in range(2)]
    return list(zip(fetched, rows))


def project(scalars, mine, other, gain, gain_far, w_query, w_key, w_value, fetched, bias, cosine,
            sine, after=()):
    length, width = mine.shape
    qw, kw = w_query.shape[1], w_key.shape[1]
    total = qw + 2 * kw

    def kernel(s, mine, other, gain, gain_far, wq, wk, wv, *refs):
        fetched, (bias, cosine, sine, q, k, v, a, r, w) = refs[:QUARTERS], refs[QUARTERS:]
        x = mine[...].astype(F32)
        y = other[...].astype(F32)
        squares = jnp.sum(x * x, axis=1, keepdims=True) + jnp.sum(y * y, axis=1, keepdims=True)
        rstd = lax.rsqrt(squares / D + EPS)
        r[...] = rstd

        @pl.when(s[SAME] == 1)
        def _():
            a[:, :width] = (x * rstd * gain[...]).astype(BF)
            a[:, width:] = (y * rstd * gain_far[...]).astype(BF)

        @pl.when(s[SAME] == 0)
        def _():
            a[:, :width] = (y * rstd * gain[...]).astype(BF)
            a[:, width:] = (x * rstd * gain_far[...]).astype(BF)

        w[:width, :qw] = wq[...]
        w[:width, qw:qw + kw] = wk[...]
        w[:width, qw + kw:] = wv[...]
        for piece, rows in placed(s, fetched, width, width):
            w[rows, :] = piece[...]
        out = dot(a[...], w[...]) + bias[...]
        c, t = cosine[...], sine[...]
        for head in range(qw // HD):
            u = out[:, head * HD:(head + 1) * HD]
            q[:, head * HD:(head + 1) * HD] = (u * c + pltpu.roll(u, HD // 2, 1) * t).astype(BF)
        for head in range(kw // HD):
            u = out[:, qw + head * HD:qw + (head + 1) * HD]
            k[:, head * HD:(head + 1) * HD] = (u * c + pltpu.roll(u, HD // 2, 1) * t).astype(BF)
        v[...] = out[:, qw + kw:].astype(BF)

    arrays = [mine, other, gain, gain_far, w_query, w_key, w_value, *fetched, bias, cosine, sine]
    return run(kernel, [(scalars, SCALARS)] + [(a, WHOLE) for a in arrays],
               [shape((length, qw), BF), shape((length, kw), BF), shape((length, kw), BF),
                shape((length, 2 * width), BF), shape((length, 1), F32)], after=after,
               scratch=[pltpu.VMEM((2 * width, total), BF)],
               estimate=cost(2 * length * 2 * width * total, 12 * MIB), name="qkv")


def allowed_keys(seg_col, seg_row, start, size, keys):
    rows = lax.broadcasted_iota(jnp.int32, (size, keys), 0) + start
    cols = lax.broadcasted_iota(jnp.int32, (size, keys), 1)
    return (seg_col[start:start + size, :] == seg_row[:, :keys]) & (cols <= rows)


def attend(scalars, q, k, v, seg_col, seg_row, w_out, fetched, after=()):
    length, qw = q.shape
    heads, pairs = qw // HD, k.shape[1] // HD
    width = w_out.shape[1]

    def kernel(s, q, k, v, seg_col, seg_row, w_out, *refs):
        fetched, (o, lse, part, w) = refs[:QUARTERS], refs[QUARTERS:]
        for start in range(0, length, TILE):
            keys = start + TILE
            allowed = allowed_keys(seg_col, seg_row, start, TILE, keys)
            rows = slice(start, start + TILE)
            for head in range(heads):
                pair = head // (heads // pairs)
                place = slice(head * HD, (head + 1) * HD)
                mine = slice(pair * HD, (pair + 1) * HD)
                scores = dot_right(q[rows, place], k[:keys, mine]) * HD ** (-0.5)
                scores = jnp.where(allowed, scores, -1e30)
                top = jnp.max(scores, axis=1, keepdims=True)
                raised = jnp.exp(scores - top)
                total = jnp.sum(raised, axis=1, keepdims=True)
                weights = (raised * (1.0 / total)).astype(BF)
                o[rows, place] = dot(weights, v[:keys, mine]).astype(BF)
                lse[rows, head:head + 1] = top + jnp.log(total)
        w[:, :width] = w_out[...]
        for piece, rows in placed(s, fetched, 0, qw):
            w[rows, width:] = piece[...]
        value = dot(o[...], w[...]).astype(BF)
        part[0] = value
        part[1] = value

    arrays = [q, k, v, seg_col, seg_row, w_out, *fetched]
    return run(kernel, [(scalars, SCALARS)] + [(a, WHOLE) for a in arrays],
               [shape((length, qw), BF), shape((length, LANES), F32), shape((2, length, 2 * width), BF)],
               after=after,
               scratch=[pltpu.VMEM((qw, 2 * width), BF)],
               estimate=cost(4 * length * length * qw + 2 * length * qw * 2 * width, 12 * MIB,
                             heads * length * length), name="attention")


def tiled(array, tile):
    return array, pl.BlockSpec((tile, array.shape[1]), lambda i: (i, 0))


def both_tiled(array, tile):
    return array, pl.BlockSpec((2, tile, array.shape[2]), lambda i: (0, i, 0))


def fixed(array):
    return array, pl.BlockSpec(array.shape, lambda i: (0, 0))


def norm_two(scalars, mine, other, parts, gain, gain_far, after=()):
    length, width = mine.shape

    def kernel(s, mine, other, parts, gain, gain_far, h, near, far, r):
        added = parts[0].astype(F32) + parts[1].astype(F32)

        def fill(first, second):
            h[:, :width] = first[...].astype(F32) + added[:, :width]
            h[:, width:] = second[...].astype(F32) + added[:, width:]

        pl.when(s[SAME] == 1)(lambda: fill(mine, other))
        pl.when(s[SAME] == 0)(lambda: fill(other, mine))
        rstd = lax.rsqrt(jnp.sum(h[...] * h[...], axis=1, keepdims=True) / D + EPS)
        r[...] = rstd
        first = (h[:, :width] * rstd * gain[...]).astype(BF)
        second = (h[:, width:] * rstd * gain_far[...]).astype(BF)

        @pl.when(s[SAME] == 1)
        def _():
            near[...] = first
            far[...] = second

        @pl.when(s[SAME] == 0)
        def _():
            near[...] = second
            far[...] = first

    tile = TILE // 2
    outs = [shape((length, 2 * width), F32), shape((length, width), BF), shape((length, width), BF),
            shape((length, 1), F32)]
    return run(kernel, [(scalars, SCALARS)] + [tiled(mine, tile), tiled(other, tile), both_tiled(parts, tile)]
               + [fixed(gain), fixed(gain_far)], outs, after=after, grid=(length // tile,),
               out_specs=[tiled(o, tile)[1] for o in outs],
               estimate=cost(length * width * 20, 16 * MIB), name="norm_two")


def gate_up(scalars, pieces, w_gate, w_up, fetched, first, total, part, kept=None, after=(), share=1):
    width = pieces[0][0].shape[-1]
    counts = [piece[0].shape[-2] // WIDE_TILE for piece in pieces]
    steps = sum(counts)
    offset = first // WIDE_TILE
    starts = [sum(counts[:i]) for i in range(len(counts))]

    def kernel(s, *refs):
        halves, refs = refs[:given], refs[given:]
        wg, wu, *fetched = refs[:2 + CHUNKED]
        b, z, up_slope, gate_slope, w, sems = refs[-6:]
        step = pl.program_id(0)

        @pl.when(step == 0)
        def _():
            load_gate_up(s, wg, wu, fetched, w, sems, part, width)

        def fill(*piece):
            if len(piece) == 1:
                near, far, straight = piece[0].at[0], piece[0].at[1], s[ROW] == 0
            else:
                near, far, straight = *piece, s[SAME] == 1

            @pl.when(straight)
            def _():
                b[:, :width] = near[...]
                b[:, width:] = far[...]

            @pl.when(jnp.logical_not(straight))
            def _():
                b[:, :width] = far[...]
                b[:, width:] = near[...]

        at = 0
        for piece, start, count in zip(pieces, starts, counts):
            pl.when((step >= start) & (step < start + count))(
                functools.partial(fill, *halves[at:at + len(piece)])
            )
            at += len(piece)

        both = dot(b[...], w[...])
        gate, upward = both[:, :part], both[:, part:]
        counted = lax.broadcasted_iota(jnp.int32, gate.shape, 1) >= s[SKIP]
        sigma = 1.0 / (1.0 + jnp.exp(-gate))
        sigma = jnp.where(counted, sigma, 0.0)
        silu = gate * sigma
        z[...] = (silu * upward).astype(BF)
        up_slope[...] = silu.astype(BF)
        gate_slope[...] = (upward * sigma * (1.0 + gate * (1.0 - sigma))).astype(BF)

    def block(array, start, count):
        if len(array.shape) == 3:
            return pl.BlockSpec((2, WIDE_TILE, width), lambda i: (0, jnp.clip(i - start, 0, count - 1), 0))
        return pl.BlockSpec((WIDE_TILE, width), lambda i: (jnp.clip(i - start, 0, count - 1), 0))

    ins = [(scalars, SCALARS)]
    for piece, start, count in zip(pieces, starts, counts):
        ins += [(array, block(array, start, count)) for array in piece]
    given = len(ins) - 1
    ins += [(array, ANY) for array in (w_gate, w_up, *fetched)]
    aliases = {}
    if kept is not None:
        aliases = {len(ins) + i: i for i in range(4)}
        ins += [(array, ANY) for array in kept]
    at = lambda i: (i + offset, 0)
    length = steps * WIDE_TILE
    return run(kernel, ins,
               [shape((total, 2 * width), BF)] + [shape((total, part), BF)] * 3,
               after=after, grid=(steps,),
               out_specs=[pl.BlockSpec((WIDE_TILE, 2 * width), at)]
               + [pl.BlockSpec((WIDE_TILE, part), at)] * 3,
               scratch=[pltpu.VMEM((2 * width, 2 * part), BF), pltpu.SemaphoreType.DMA((2 + CHUNKED,))],
               aliases=aliases,
               estimate=cost(share * 8 * length * width * part, share * 12 * MIB, share * length * part),
               name="gate_up")


def load_gate_up(s, wg, wu, fetched, w, sems, part, width):
    lanes = lanes_at(s[START], part)
    copies([(wg.at[:, lanes], w.at[:width, :part]), (wu.at[:, lanes], w.at[:width, part:])]
           + [(piece, w.at[rows, :]) for piece, rows in placed(s, fetched, width, width)], sems)


def place_rows(scalars, pieces, after=()):
    length, width = pieces[0][0].shape
    flat = [array for piece in pieces for array in piece[:2]]

    def kernel(s, *refs):
        srcs, out, sems = refs[:len(flat)], refs[len(flat)], refs[len(flat) + 1]
        pairs = []
        for i, src in enumerate(srcs):
            _, _, group, side = pieces[i // 2]
            place = jnp.where(s[SAME] == 1, i % 2, 1 - i % 2) * length
            pairs.append((src, out.at[rows_at(2 * group * length + place, length),
                                      side * width:(side + 1) * width]))
        copies(pairs, sems)

    return run(kernel, [(scalars, SCALARS)] + [(a, ANY) for a in flat],
               [shape((4 * length, 2 * width), BF)], after=after,
               scratch=[pltpu.SemaphoreType.DMA((len(flat),))], limit=48,
               estimate=cost(0, 16 * len(flat) * length * width // 4), name="place_rows")[0]


def place_last(scalars, both, rows, after=()):
    _, length, width = both.shape

    def kernel(s, both, _, out, buffer, sems):
        copies([(both.at[i], buffer.at[i]) for i in range(2)], sems)
        copies([(buffer.at[i], out.at[rows_at(2 * length + jnp.where(s[ROW] == i, 0, length), length),
                                      width:]) for i in range(2)], sems)

    return run(kernel, [(scalars, SCALARS), (both, ANY), (rows, ANY)], [shape(rows.shape, BF)], after=after,
               out_specs=[ANY], aliases={2: 0},
               scratch=[pltpu.VMEM(both.shape, BF), pltpu.SemaphoreType.DMA((2,))], limit=48,
               estimate=cost(0, 8 * length * width), name="place_last")[0]


def copy_of(array, after):
    def kernel(src, out, sem):
        copies([(src, out)], sem)

    return run(kernel, [(array, ANY)], [shape(array.shape, array.dtype)], after=after,
               scratch=[pltpu.SemaphoreType.DMA((1,))], limit=48,
               estimate=cost(0, 4 * array.size), name="copy_of")[0]


def hold(array, *after):
    def kernel(src, out):
        pass

    return run(kernel, [(array, ANY)], [shape(array.shape, array.dtype)], after=after, out_specs=[ANY],
               aliases={0: 0}, limit=48, estimate=cost(0, 0), name="hold")[0]


def load_down(s, w_down, fetched, w, sems, part, width):
    copies([(w_down.at[rows_at(s[START], part), :], w.at[:, :width])]
           + [(piece, w.at[rows, width:]) for piece, rows in placed(s, fetched, 0, part)], sems)


def hidden_back(scalars, cot, up_slope, gate_slope, w_down, fetched, after=()):
    total, width = cot.shape[0], cot.shape[1] // 2
    part = up_slope.shape[1]

    def kernel(s, g, up_slope, gate_slope, w_down, *refs):
        fetched, (out, w, sems) = refs[:HALVES], refs[HALVES:]

        @pl.when(pl.program_id(0) == 0)
        def _():
            load_down(s, w_down, fetched, w, sems, part, width)

        back = dot_right(g[...], w[...])
        out[:, :part] = (back * gate_slope[...].astype(F32)).astype(BF)
        out[:, part:] = (back * up_slope[...].astype(F32)).astype(BF)

    at = lambda i: (i, 0)
    tile = 2 * TILE
    return run(kernel,
               [(scalars, SCALARS), (cot, pl.BlockSpec((tile, 2 * width), at)),
                (up_slope, pl.BlockSpec((tile, part), at)), (gate_slope, pl.BlockSpec((tile, part), at)),
                (w_down, ANY)] + [(piece, ANY) for piece in fetched],
               [shape((total, 2 * part), BF)], after=after, grid=(total // tile,),
               out_specs=[pl.BlockSpec((tile, 2 * part), at)],
               scratch=[pltpu.VMEM((part, 2 * width), BF), pltpu.SemaphoreType.DMA((1 + HALVES,))],
               estimate=cost(4 * total * width * part, total * 14000), name="hidden_back")[0]


def split_store(s, value, keep, send, width):
    first, second = value[:, :width].astype(BF), value[:, width:].astype(BF)

    @pl.when(s[SAME] == 1)
    def _():
        keep[...] = first
        send[...] = second

    @pl.when(s[SAME] == 0)
    def _():
        keep[...] = second
        send[...] = first


def norm_back(scalars, low, w_gate, w_up, fetched, first, length, after=(), stacked=False):
    width = w_gate.shape[0]
    part = low.shape[1] // 2
    offset = first // WIDE_TILE

    def kernel(s, low, wg, wu, *refs):
        fetched, (*outs, w, sems) = refs[:CHUNKED], refs[CHUNKED:]

        @pl.when(pl.program_id(0) == 0)
        def _():
            load_gate_up(s, wg, wu, fetched, w, sems, part, width)

        value = dot_right(low[...], w[...])
        if stacked:
            outs[0][s[ROW]] = value[:, :width].astype(BF)
            outs[0][1 - s[ROW]] = value[:, width:].astype(BF)
        else:
            split_store(s, value, *outs, width)

    tiles = [pl.BlockSpec((WIDE_TILE, width), lambda i: (i, 0))] * 2
    outs = [shape((length, width), BF)] * 2
    if stacked:
        outs = [shape((2, length, width), BF)]
        tiles = [pl.BlockSpec((2, WIDE_TILE, width), lambda i: (0, i, 0))]
    return run(kernel,
               [(scalars, SCALARS), (low, pl.BlockSpec((WIDE_TILE, 2 * part), lambda i: (i + offset, 0))),
                (w_gate, ANY), (w_up, ANY)] + [(piece, ANY) for piece in fetched],
               outs, after=after, grid=(length // WIDE_TILE,), out_specs=tiles,
               scratch=[pltpu.VMEM((2 * width, 2 * part), BF), pltpu.SemaphoreType.DMA((2 + CHUNKED,))],
               estimate=cost(8 * length * width * part, 8 * MIB + length * 8000), name="norm_back")


def down_project(scalars, hidden, w_down, fetched, after=()):
    total, part = hidden.shape
    width = w_down.shape[1]

    def kernel(s, z, w_down, *refs):
        fetched, (keep, send, w, sems) = refs[:HALVES], refs[HALVES:]

        @pl.when(pl.program_id(0) == 0)
        def _():
            load_down(s, w_down, fetched, w, sems, part, width)

        split_store(s, dot(z[...], w[...]), keep, send, width)

    at = lambda i: (i, 0)
    tile = 2 * TILE
    return run(kernel,
               [(scalars, SCALARS), (hidden, pl.BlockSpec((tile, part), at)), (w_down, ANY)]
               + [(piece, ANY) for piece in fetched],
               [shape((total, width), BF)] * 2, after=after, grid=(total // tile,),
               out_specs=[pl.BlockSpec((tile, width), at)] * 2,
               scratch=[pltpu.VMEM((part, 2 * width), BF), pltpu.SemaphoreType.DMA((1 + HALVES,))],
               estimate=cost(4 * total * width * part, total * 8000), name="down_project")


def weight_grad(scalars, left, right, piece, columns, place=0, after=()):
    tokens, width = left.shape[0], left.shape[1] // 2
    groups = width // (2 * piece)

    def kernel(s, left, right, keep, send):
        value = dot_left(left[...], right[...]).astype(BF).reshape(groups, 2, piece, columns)

        @pl.when(s[INNER] == 0)
        def _():
            keep[0] = value[:, 0]
            send[0] = value[:, 1]

        @pl.when(s[INNER] == 1)
        def _():
            keep[0] = value[:, 1]
            send[0] = value[:, 0]

    block = pl.BlockSpec((1, groups, piece, columns), lambda i: (i, 0, 0, 0))
    return run(kernel,
               [(scalars, SCALARS), (left, pl.BlockSpec((tokens, width), lambda i: (0, i))),
                (right, pl.BlockSpec((tokens, columns), lambda i: (0, place)))],
               [shape((2, groups, piece, columns), BF)] * 2, after=after, grid=(2,),
               out_specs=[block, block],
               estimate=cost(4 * tokens * width * columns, tokens * (4 * width + 4 * columns)),
               name="weight_grad")


def small_grad(left, right, after=()):
    tokens, width = left.shape[0], left.shape[1] // 2
    columns = right.shape[1]

    def kernel(left, right, keep, send):
        send[...] = dot_left(left[:, width:], right[...]).astype(BF)
        keep[...] = dot_left(left[:, :width], right[...]).astype(BF)

    return run(kernel, [(left, WHOLE), (right, WHOLE)], [shape((width, columns), BF)] * 2, after=after,
               estimate=cost(4 * tokens * width * columns, 8 * MIB), name="small_grad")


def middle_back(scalars, both, h, r, gain, gain_far, cot, after=()):
    _, length, width = both.shape

    def kernel(s, both, h, r, gain, gain_far, g, dh, low, gain_part, db):
        def fill(first, second):
            db[:, :width] = first.astype(F32)
            db[:, width:] = second.astype(F32)

        pl.when(s[ROW] == 0)(lambda: fill(both[0], both[1]))
        pl.when(s[ROW] == 1)(lambda: fill(both[1], both[0]))
        rstd = r[...]
        normed = h[...] * rstd
        gains = jnp.concatenate([gain[...], gain_far[...]], axis=1)

        @pl.when(pl.program_id(0) == 0)
        def _():
            gain_part[...] = jnp.zeros_like(gain_part)

        gain_part[...] += jnp.sum(db[...] * normed, axis=0, keepdims=True)
        scaled = db[...] * gains
        mean = jnp.sum(scaled * normed, axis=1, keepdims=True) / D
        value = g[...].astype(F32) + rstd * (scaled - normed * mean)
        low[...] = value.astype(BF)
        pl.when(s[SAME] == 1)(lambda: dh.__setitem__(..., value[:, :width]))
        pl.when(s[SAME] == 0)(lambda: dh.__setitem__(..., value[:, width:]))

    tile = TILE // 2
    outs = [shape((length, width), F32), shape((length, 2 * width), BF), shape((1, 2 * width), F32)]
    return run(kernel, [(scalars, SCALARS)] + [both_tiled(both, tile), tiled(h, tile), tiled(r, tile)]
               + [fixed(gain), fixed(gain_far), tiled(cot, tile)], outs, after=after,
               grid=(length // tile,),
               out_specs=[tiled(o, tile)[1] for o in outs[:2]] + [fixed(outs[2])[1]],
               scratch=[pltpu.VMEM((tile, 2 * width), F32)],
               estimate=cost(length * width * 30, 20 * MIB), name="middle_back")


def attend_back(scalars, low, q, k, v, lse, seg_col, seg_row, w_out, out_fetched, w_query, w_key, w_value,
                qkv_fetched, cosine, sine, after=()):
    length, qw = q.shape
    kw = k.shape[1]
    heads, pairs = qw // HD, kw // HD
    width = w_out.shape[1]
    total = qw + 2 * kw

    def kernel(s, low, q, k, v, lse, seg_col, seg_row, w_out, *refs):
        out_fetched, (wq, wk, wv), refs = refs[:QUARTERS], refs[QUARTERS:QUARTERS + 3], refs[QUARTERS + 3:]
        fetched, (cosine, sine, back, bias, part, wo, w, do, dk, dv, lse_t) = refs[:QUARTERS], refs[QUARTERS:]
        wo[:, :width] = w_out[...]
        for piece, rows in placed(s, out_fetched, 0, qw):
            wo[rows, width:] = piece[...]
        do[...] = dot_right(low[...], wo[...]).astype(BF)
        dk[...] = jnp.zeros_like(dk)
        dv[...] = jnp.zeros_like(dv)
        lse_t[...] = jnp.transpose(lse[...])
        for start in range(0, length, TILE):
            keys = start + TILE
            rows = slice(start, start + TILE)
            places = lax.broadcasted_iota(jnp.int32, (keys, TILE), 0)
            asked = lax.broadcasted_iota(jnp.int32, (keys, TILE), 1) + start
            allowed = (seg_col[:keys, :] == seg_row[:, rows]) & (places <= asked)
            c, t = cosine[rows, :], sine[rows, :]
            for head in range(heads):
                pair = head // (heads // pairs)
                place = slice(head * HD, (head + 1) * HD)
                mine = slice(pair * HD, (pair + 1) * HD)
                scores = dot_right(k[:keys, mine], q[rows, place]) * HD ** (-0.5)
                probs = jnp.where(allowed, jnp.exp(scores - lse_t[head:head + 1, rows]), 0.0)
                grads = dot_right(v[:keys, mine], do[rows, place])
                delta = jnp.sum(probs * grads, axis=0, keepdims=True)
                score_grad = (probs * (grads - delta)).astype(BF)
                dv[:keys, mine] += dot(probs.astype(BF), do[rows, place])
                dk[:keys, mine] += dot(score_grad, q[rows, place])
                u = dot_left(score_grad, k[:keys, mine]) * HD ** (-0.5)
                back[rows, place] = (u * c - pltpu.roll(u, HD // 2, 1) * t).astype(BF)
        for pair in range(pairs):
            u = dk[:, pair * HD:(pair + 1) * HD] * HD ** (-0.5)
            u = u * cosine[...] - pltpu.roll(u, HD // 2, 1) * sine[...]
            back[:, qw + pair * HD:qw + (pair + 1) * HD] = u.astype(BF)
        back[:, qw + kw:] = dv[...].astype(BF)
        w[:width, :qw] = wq[...]
        w[:width, qw:qw + kw] = wk[...]
        w[:width, qw + kw:] = wv[...]
        for piece, rows in placed(s, fetched, width, width):
            w[rows, :] = piece[...]
        value = dot_right(back[...], w[...]).astype(BF)
        part[0] = value
        part[1] = value
        bias[...] = jnp.sum(back[...].astype(F32), axis=0, keepdims=True)

    arrays = [low, q, k, v, lse, seg_col, seg_row, w_out, *out_fetched, w_query, w_key, w_value,
              *qkv_fetched, cosine, sine]
    return run(kernel, [(scalars, SCALARS)] + [(a, WHOLE) for a in arrays],
               [shape((length, total), BF), shape((1, total), F32), shape((2, length, 2 * width), BF)],
               after=after,
               scratch=[pltpu.VMEM((qw, 2 * width), BF), pltpu.VMEM((2 * width, total), BF),
                        pltpu.VMEM((length, qw), BF), pltpu.VMEM((length, kw), F32),
                        pltpu.VMEM((length, kw), F32), pltpu.VMEM((LANES, length), F32)],
               estimate=cost(10 * length * length * qw + 2 * length * 2 * width * (qw + total), 20 * MIB,
                             heads * length * length), name="attention_back")


def input_back(scalars, parts, mine, other, r, gain, gain_far, dh, after=()):
    length, width = mine.shape

    def kernel(s, parts, mine, other, r, dh, gain, gain_far, out, gain_part, n):
        def fill(first, second):
            n[:, :width] = first[...].astype(F32) * r[...]
            n[:, width:] = second[...].astype(F32) * r[...]

        pl.when(s[SAME] == 1)(lambda: fill(mine, other))
        pl.when(s[SAME] == 0)(lambda: fill(other, mine))
        da = parts[0].astype(F32) + parts[1].astype(F32)
        normed = n[...]

        @pl.when(pl.program_id(0) == 0)
        def _():
            gain_part[...] = jnp.zeros_like(gain_part)

        gain_part[...] += jnp.sum(da * normed, axis=0, keepdims=True)
        scaled = da * jnp.concatenate([gain[...], gain_far[...]], axis=1)
        mean = jnp.sum(scaled * normed, axis=1, keepdims=True) / D

        def put(half):
            out[...] = (dh[...] + r[...] * (scaled[:, half] - normed[:, half] * mean)).astype(BF)

        pl.when(s[SAME] == 1)(lambda: put(slice(0, width)))
        pl.when(s[SAME] == 0)(lambda: put(slice(width, 2 * width)))

    tile = TILE // 2
    outs = [shape((length, width), BF), shape((1, 2 * width), F32)]
    return run(kernel, [(scalars, SCALARS)] + [both_tiled(parts, tile)] + [tiled(a, tile) for a in (mine, other, r, dh)]
               + [fixed(gain), fixed(gain_far)], outs, after=after, grid=(length // tile,),
               out_specs=[tiled(outs[0], tile)[1], fixed(outs[1])[1]],
               scratch=[pltpu.VMEM((tile, 2 * width), F32)],
               estimate=cost(length * width * 30, 16 * MIB), name="input_back")


def halve(scalars, keep, recv, bit, after=()):
    parts, many, _, rows, columns = keep.shape

    def kernel(s, keep, recv, kept, sent):
        total = (keep[0, 0].astype(F32) + recv[0, 0].astype(F32)).astype(BF)

        @pl.when(s[BITS + bit] == 0)
        def _():
            kept[0, 0] = total[0]
            sent[0, 0] = total[1]

        @pl.when(s[BITS + bit] == 1)
        def _():
            kept[0, 0] = total[1]
            sent[0, 0] = total[0]

    wide = pl.BlockSpec((1, 1, 2, rows, columns), lambda i, j: (i, j, 0, 0, 0))
    narrow = pl.BlockSpec((1, 1, rows, columns), lambda i, j: (i, j, 0, 0))
    return run(kernel, [(scalars, SCALARS), (keep, wide), (recv, wide)],
               [shape((parts, many, rows, columns), BF)] * 2, after=after, grid=(parts, many),
               out_specs=[narrow] * 2, estimate=cost(GLUE), name="halve")


def sum_rows(keep, recv, after=()):
    _, pieces, rows, columns = keep.shape

    def kernel(keep, recv, near, sent):
        near[0] = (keep[0, 0].astype(F32) + recv[0, 0].astype(F32)).astype(BF)
        sent[0] = (keep[1, 0].astype(F32) + recv[1, 0].astype(F32)).astype(BF)

    wide = pl.BlockSpec((2, 1, rows, columns), lambda i: (0, i, 0, 0))
    narrow = pl.BlockSpec((1, rows, columns), lambda i: (i, 0, 0))
    return run(kernel, [(keep, wide), (recv, wide)], [shape((pieces, rows, columns), BF)] * 2, after=after,
               grid=(pieces,), out_specs=[narrow] * 2, estimate=cost(GLUE),
               name="sum_rows")


def deal_near(scalars, near, far, after=()):
    def kernel(s, near, far, own, sent):
        for bit, out in ((s[BITS + 1], own), (1 - s[BITS + 1], sent)):
            out[s[ROW]] = near[bit]
            out[1 - s[ROW]] = far[bit]

    return run(kernel, [(scalars, SCALARS), (near, WHOLE), (far, WHOLE)], [shape(near.shape, BF)] * 2,
               after=after, estimate=cost(GLUE), name="deal_near")


def lay_columns(scalars, own, across, overlap, after=()):
    _, rows, part = own.shape
    total = PARTS * part - overlap

    def kernel(s, own, across, out):
        def fill(first, second):
            for i, piece in enumerate((first[0], first[1], second[0])):
                out[:, i * part:(i + 1) * part] = piece.astype(F32)
            out[:, 3 * part:] = second[1][:, overlap:].astype(F32)

        pl.when(s[BITS + 1] == 0)(lambda: fill(own, across))
        pl.when(s[BITS + 1] == 1)(lambda: fill(across, own))

    return run(kernel, [(scalars, SCALARS), (own, WHOLE), (across, WHOLE)], [shape((rows, total), F32)],
               after=after, estimate=cost(GLUE), name="lay_columns")[0]


def sum_plain(keep, recv, after=()):
    def kernel(keep, recv, out):
        out[...] = keep[...].astype(F32) + recv[...].astype(F32)

    return run(kernel, [(keep, WHOLE), (recv, WHOLE)], [shape(keep.shape, F32)], after=after,
               estimate=cost(GLUE), name="sum_plain")[0]


def sum_split(keep, recv, widths, after=()):
    rows = keep.shape[1]

    def kernel(keep, recv, *outs):
        at = 0
        for out, width in zip(outs, widths):
            part = slice(at, at + width)
            out[...] = keep[0, :, part].astype(F32) + recv[0, :, part].astype(F32)
            at += width

    return run(kernel, [(keep, WHOLE), (recv, WHOLE)], [shape((rows, width), F32) for width in widths],
               after=after, estimate=cost(GLUE), name="sum_split")


def sum_far(keep, send, first, after=()):
    width = keep.shape[1]
    half = width // 2
    offset = first // half

    def kernel(keep, send, to_row, to_near):
        value = (keep[...].astype(F32) + send[...].astype(F32)).astype(BF)
        pl.when(pl.program_id(0) == 0)(lambda: to_row.__setitem__(..., value))
        pl.when(pl.program_id(0) == 1)(lambda: to_near.__setitem__(..., value))

    block = pl.BlockSpec((half, width), lambda i: (offset + i, 0))
    return run(kernel, [(keep, block), (send, block)], [shape((half, width), BF)] * 2, after=after, grid=(2,),
               out_specs=[pl.BlockSpec((half, width), lambda i: (0, 0))] * 2,
               estimate=cost(GLUE), name="sum_far")


def sum_near(keep, send, via_row, via_near, first, after=()):
    half, width = via_row.shape
    length = 2 * half
    offset = first // length

    def kernel(keep, send, via_row, via_near, to_row, to_near):
        step = pl.program_id(0)

        def put(out, plain, more, via):
            out[plain, :] = (keep[plain, :].astype(F32) + send[plain, :].astype(F32)).astype(BF)
            out[more, :] = (keep[more, :].astype(F32) + send[more, :].astype(F32)
                            + via[...].astype(F32)).astype(BF)

        low, high = slice(0, half), slice(half, length)
        pl.when(step == 0)(lambda: put(to_row, low, high, via_near))
        pl.when(step == 1)(lambda: put(to_near, high, low, via_row))

    block = pl.BlockSpec((length, width), lambda i: (offset + i, 0))
    whole = pl.BlockSpec((length, width), lambda i: (0, 0))
    return run(kernel, [(keep, block), (send, block), fixed(via_row), fixed(via_near)],
               [shape((length, width), BF)] * 2, after=after, grid=(2,), out_specs=[whole, whole],
               estimate=cost(GLUE), name="sum_near")


def sum_own(keep, send, via_row, via_near, after=()):
    length, width = via_row.shape

    def kernel(keep, send, via_row, via_near, out):
        value = (keep[...].astype(F32) + send[...].astype(F32)) + (
            via_row[...].astype(F32) + via_near[...].astype(F32))
        out[0] = value.astype(BF)
        out[1] = value.astype(BF)

    outs = [shape((2, length, width), BF)]
    return run(kernel, [tiled(a, TILE) for a in (keep, send, via_row, via_near)], outs, after=after,
               grid=(length // TILE,), out_specs=[both_tiled(outs[0], TILE)[1]],
               estimate=cost(GLUE), name="sum_own")[0]


def sum_output(scalars, keep, send, via_row, via_near, h, after=()):
    length, width = via_row.shape

    def kernel(s, keep, send, via_row, via_near, h, out):
        value = (keep[...].astype(F32) + send[...].astype(F32)) + (
            via_row[...].astype(F32) + via_near[...].astype(F32))
        pl.when(s[SAME] == 1)(lambda: out.__setitem__(..., (h[:, :width] + value).astype(BF)))
        pl.when(s[SAME] == 0)(lambda: out.__setitem__(..., (h[:, width:] + value).astype(BF)))

    outs = [shape((length, width), BF)]
    return run(kernel, [(scalars, SCALARS)] + [tiled(a, TILE) for a in (keep, send, via_row, via_near, h)],
               outs, after=after, grid=(length // TILE,), out_specs=[tiled(outs[0], TILE)[1]],
               estimate=cost(GLUE), name="sum_output")[0]


def body(
    inputs,
    segments,
    positions,
    w_query,
    w_key,
    w_value,
    b_query,
    b_key,
    b_value,
    w_out,
    gain_one,
    gain_two,
    w_gate,
    w_up,
    w_down,
    cotangent,
):
    length, width = inputs.shape
    query_width = w_query.shape[1]
    key_width = w_key.shape[1]
    total_width = query_width + 2 * key_width
    row = lax.axis_index("row")
    col = lax.axis_index("col")
    group = lax.axis_index("dp")
    groups = lax.axis_size("dp")
    inner = group % 2
    near_bit = (group // 2) % 2
    same = row == col

    hidden_here = w_gate.shape[1]
    blocks = hidden_here // LANES
    wide = -(-blocks // PARTS)
    part = wide * LANES
    overlap = PARTS * part - hidden_here

    def start_of(index):
        return jnp.minimum(index * wide, blocks - wide) * LANES

    mine_part = near_bit * 2 + row
    place_of = lambda low, high: 2 * low + high
    scalars = jnp.stack(
        [same.astype(jnp.int32), inner, start_of(mine_part), start_of(near_bit * 2 + 1 - row),
         jnp.where(mine_part == PARTS - 1, overlap, 0), place_of(inner, near_bit),
         place_of(1 - inner, near_bit), place_of(inner, 1 - near_bit), place_of(1 - inner, 1 - near_bit), row]
        + [(group >> bit) % 2 for bit in range(groups.bit_length() - 1)]
    ).astype(jnp.int32)

    def by_row(mine, other):
        return jnp.where(same, mine, other), jnp.where(same, other, mine)

    LAST.clear()
    half = width // 2
    gains = jnp.stack([gain_one, gain_two])
    fetched_gains = swap_row(gains)
    mine = turn_square(inputs)
    other = swap_col(mine)
    def pack_gate_up(chunk):
        return swap_row(pack_weights(
            scalars, [w_gate, w_up], part, (width // 4, 2 * part), INNER, scale=2, chunk=chunk
        ))

    def relay(direct):
        pair, near = swap_bit(direct, 0), swap_bit(direct, 1)
        cut = direct.shape[0] // 2
        return direct, pair, near, swap_bit(pair[:cut], 1), swap_bit(near[cut:], 0)

    qkv_fetched = relay(swap_row(
        pack_weights(scalars, [w_query, w_key, w_value], None, (width // 4, total_width), OWN)
    ))
    out_fetched = relay(swap_row(
        pack_weights(scalars, [w_out], None, (query_width // 4, width), OWN)
    ))
    fetched_gains = hold(fetched_gains).astype(F32)
    gains = gains.astype(F32)
    gu_direct = [pack_gate_up(0), pack_gate_up(1)]
    gu_first = hold(gu_direct[0])
    gu_fetched = [gu_first, swap_bit(gu_first, 0)]

    indices = jnp.arange(HD // 2, dtype=F32)
    inverse = jnp.exp(indices * (-2.0 / HD) * jnp.log(F32(THETA)))
    turned = positions.astype(F32)[:, None] * inverse[None, :]
    cosine, sine = jnp.cos(turned), jnp.sin(turned)
    cosine = jnp.concatenate([cosine, cosine], axis=1)
    sine = jnp.concatenate([-sine, sine], axis=1)
    bias = jnp.concatenate([b_query, b_key, b_value]).astype(F32)[None, :]
    seg_col, seg_row = segments[:, None], segments[None, :]

    q, k, v, low_one, r_one = project(
        scalars, mine, other, gains[:1], fetched_gains[:1], w_query, w_key, w_value, qkv_fetched,
        bias, cosine, sine,
    )
    cot = copy_of(cotangent, [])
    cot_row = swap_row(cot)
    cot_near = swap_bit(cot, 1)
    attended, lse, out_part = attend(scalars, q, k, v, seg_col, seg_row, w_out, out_fetched)
    gu_second = hold(gu_direct[1])
    gu_fetched += [gu_second, swap_bit(gu_second, 0)]
    cot_other = swap_col(cot)
    gu_fetched[1] = hold(gu_fetched[1])
    cot_other = hold(cot_other)
    h, low_near, low_far, r_two = norm_two(
        scalars, mine, other, trade_col(out_part), gains[1:], fetched_gains[1:]
    )

    b_row = swap_row(low_near)
    b_near = swap_bit(low_near, 1)
    cot_row, cot_near = hold(cot_row), hold(cot_near)
    cot_row_other, cot_near_other = swap_col(cot_row), swap_col(cot_near)
    tokens = 4 * length
    ffn = functools.partial(
        gate_up, scalars, w_gate=w_gate, w_up=w_up, fetched=gu_fetched, total=tokens, part=part,
    )
    kept = ffn([(low_near, low_far)], first=0)
    cot_row_other, cot_near_other = hold(cot_row_other), hold(cot_near_other)
    cot_low = swap_bit(hold(cot_row[:half]), 1)
    placed_cot = place_rows(scalars, [(cot, cot_other, 0, 0), (cot_row, cot_row_other, 0, 1),
                                      (cot_near, cot_near_other, 1, 0)])
    b_row = hold(b_row)
    b_row_other = swap_col(b_row)
    b_low = swap_bit(b_row[:half], 1)
    b_near = hold(b_near)
    b_near_other = swap_col(b_near)
    b_high = swap_row(b_near[half:])
    b_row_other, b_near_other = hold(b_row_other), hold(b_near_other)
    cot_high = swap_row(hold(cot_near[half:]))
    sent_down = pack_weights(scalars, [w_down], None, (part // 2, width), INNER, down=True)
    down_direct = swap_row(sent_down)
    kept = ffn([(b_row, b_row_other), (b_near, b_near_other)], first=length, kept=kept)
    b_far = jnp.concatenate([hold(b_low), hold(b_high)], axis=0)
    b_far = trade_col(jnp.stack([b_far, b_far]))
    kept = ffn([(b_far,)], first=3 * length, kept=kept, after=[sent_down], share=0)
    full_two, hidden, up_slope, gate_slope = kept
    cot_far = jnp.concatenate([hold(cot_low), hold(cot_high)], axis=0)
    cot_far = trade_col(jnp.stack([cot_far, cot_far]))
    down_direct = hold(down_direct)
    down_fetched = down_direct, swap_bit(down_direct, 0)
    full_cot = place_last(scalars, cot_far, placed_cot)

    piece = width // groups
    down_keep, down_send = weight_grad(scalars, full_cot, hidden, piece, part)
    down_recv = swap_bit(down_send, 0)
    low_back = hidden_back(scalars, full_cot, up_slope, gate_slope, w_down, down_fetched)
    back = functools.partial(
        norm_back, scalars, low_back, w_gate, w_up, gu_fetched
    )
    high_bits = range(2, groups.bit_length() - 1)

    def grad_high(keep, recv):
        for bit in high_bits:
            cut = (2, keep.size // (4 * 2 * piece * part), 2, 2 * piece, part)
            keep, send = halve(scalars, keep.reshape(cut), recv.reshape(cut), bit)
            recv = swap_bit(send, bit)
        return keep, recv

    def grad_row(keep, recv):
        cut = (2, 2, piece, part)
        near, send = sum_rows(keep.reshape(cut), recv.reshape(cut))
        return near, swap_row(send)

    def grad_near(near, far):
        own, send = deal_near(scalars, near, far)
        return own, swap_bit(send, 1)

    def square_first(left, right):
        keep, send = weight_grad(scalars, left, right, piece, right.shape[1])
        return keep, swap_bit(send, 0)

    def square_next(keep, recv, bit):
        cut = (2, groups >> (bit + 1), 2, piece, keep.shape[-1])
        keep, send = halve(scalars, keep.reshape(cut), recv.reshape(cut), bit)
        return keep, swap_bit(send, bit)

    def square_row(keep, recv):
        near, send = sum_rows(keep, recv)
        return near, swap_row(send)

    def square_last(near, far):
        return sum_plain(near, far).reshape(piece, -1)

    last_bits = range(2, groups.bit_length() - 1)

    far_both = trade_col(back(3 * length, length, stacked=True)[0])
    across = (far_both[0].astype(F32) + far_both[1].astype(F32)).astype(BF)
    to_row, to_near = across[:half], across[half:]
    down = grad_high(down_keep, down_recv)
    rest_keep, rest_send = back(0, 3 * length, after=[to_row, to_near])
    via_row, via_near = swap_row(to_row), swap_bit(to_near, 1)
    gate_keep, gate_send = weight_grad(scalars, full_two, low_back, piece, part, 0)
    gate_recv = swap_bit(gate_send, 0)
    rest_got = swap_col(rest_send)
    to_row, to_near = sum_near(rest_keep, rest_got, via_row, via_near, length)
    via_row, via_near = swap_row(to_row), swap_bit(to_near, 1)

    down = down[0], hold(down[1])
    out_keep, out_send = down_project(scalars, hidden, w_down, down_fetched)
    out_got = swap_col(out_send)
    up_keep, up_send = weight_grad(scalars, full_two, low_back, piece, part, 1)
    up_recv = swap_bit(up_send, 0)
    normed_grad = sum_own(rest_keep, rest_got, via_row, via_near)
    first = 3 * length
    to_row, to_near = sum_far(out_keep, out_got, first)
    via_row, via_near = swap_row(to_row), swap_bit(to_near, 1)
    down = grad_row(*down)
    dh, low_mid, gain_two_part = middle_back(
        scalars, trade_col(normed_grad), h, r_two, gains[1:], fetched_gains[1:], full_cot,
    )
    gate = grad_high(gate_keep, gate_recv)
    down = down[0], hold(down[1])
    out_sum = square_first(low_mid, attended)
    to_row, to_near = sum_near(out_keep, out_got, via_row, via_near, length)
    via_row, via_near = swap_row(to_row), swap_bit(to_near, 1)
    up_recv = hold(up_recv)
    back_low, bias_part, in_part = attend_back(
        scalars, low_mid, q, k, v, lse, seg_col, seg_row, w_out, out_fetched, w_query, w_key,
        w_value, qkv_fetched, cosine, sine,
    )
    qkv_sum = square_first(low_one, back_low)
    via_row = hold(via_row)
    up = grad_high(up_keep, up_recv)
    via_near = hold(via_near)
    input_grad, gain_one_part = input_back(
        scalars, trade_col(in_part), mine, other, r_one, gains[:1], fetched_gains[:1], dh
    )
    input_grad = turn_square(input_grad)

    def canonical(value):
        first, second = value[:, :width], value[:, width:]
        return jnp.where(row == 0, value, jnp.concatenate([second, first], axis=1))[0]

    small = jnp.concatenate([bias_part[0], canonical(gain_one_part), canonical(gain_two_part)])

    def small_step(value, swap):
        return value + hold(swap(value))

    gate = grad_row(*gate)
    qkv_sum = square_next(*qkv_sum, 1)
    small = small_step(small, lambda value: swap_bit(value, 0))
    out_sum = square_next(*out_sum, 1)
    input_grad = hold(input_grad).astype(F32)
    up = grad_row(*up)
    output = turn_square(sum_output(scalars, out_keep, out_got, via_row, via_near, h))
    for bit in last_bits:
        qkv_sum = square_next(*qkv_sum, bit)
    gate = grad_near(*gate)
    down = grad_near(*down)
    small = small_step(small, lambda value: swap_bit(value, 1))
    up = grad_near(*up)
    for bit in last_bits:
        out_sum = square_next(*out_sum, bit)
    output = hold(output)
    qkv_sum = square_row(*qkv_sum)
    for bit in last_bits:
        small = small_step(small, lambda value, bit=bit: swap_bit(value, bit))
    gate_grad = lay_columns(scalars, *gate, overlap)
    qkv_grads = sum_split(*qkv_sum, (query_width, key_width, key_width))
    down_grad = lay_columns(scalars, *down, overlap).T
    out_sum = square_row(*out_sum)
    up_grad = lay_columns(scalars, *up, overlap)
    small = small_step(small, swap_row)
    out_grad = square_last(*out_sum).T
    gain_sums = pick(small[total_width:].reshape(2, 2, width), row, 1)

    return (
        output,
        input_grad,
        *qkv_grads,
        small[:query_width],
        small[query_width : query_width + key_width],
        small[query_width + key_width : total_width],
        out_grad,
        gain_sums[0],
        gain_sums[1],
        gate_grad,
        up_grad,
        down_grad,
    )


def solution(mesh):
    return jax.shard_map(
        body,
        mesh=mesh,
        in_specs=(
            P(("dp", "col"), "row"),
            P(("dp", "row")),
            P(("dp", "row")),
            P("row", "col"),
            P("row", "col"),
            P("row", "col"),
            P("col"),
            P("col"),
            P("col"),
            P("col", "row"),
            P("row"),
            P("row"),
            P("row", "col"),
            P("row", "col"),
            P("col", "row"),
            P(("dp", "col"), "row"),
        ),
        out_specs=(
            P(("dp", "col"), "row"),
            P(("dp", "col"), "row"),
            P(("row", "dp"), "col"),
            P(("row", "dp"), "col"),
            P(("row", "dp"), "col"),
            P("col"),
            P("col"),
            P("col"),
            P("col", ("row", "dp")),
            P("row"),
            P("row"),
            P(("row", "dp"), "col"),
            P(("row", "dp"), "col"),
            P("col", ("row", "dp")),
        ),
        check_vma=False,
    )
```
